128 devices in a mesh: dp: 4 (over x_hi, core), tm: 32 (over z, y, x_lo).
Axes of the slice: x: 4 (x_hi: 2, x_lo: 2; x = x_hi * 2 + x_lo), y: 4, z: 4, core: 2. Of those that a mesh axis runs over, the one named last changes fastest.
Arguments:
- features: bfloat16 [8, 256, 81, 1152], P('dp', 'tm'), may hold values from -6 to 6
- shot_ids: int32 [8, 256], P('dp'), may hold values from 0 to 15, never falling along the last dimension, each value on 1 to 48 neighbouring positions
- band_width: int32 [8, 4], P('dp'), may hold values from 2 to 64, as said below
- proj_weight: bfloat16 [1152, 3584], replicated, may hold values from -0.1875 to 0.1875
- cotangent: bfloat16 [8, 32, 81, 3584], P('dp', 'tm'), may hold values from -1.5 to 1.5
Outputs:
- projected: bfloat16 [8, 32, 81, 3584], P('dp', 'tm')
- weight_grad: float32 [1152, 3584], P(('dp', 'tm'))
The draws below stay inside these ranges and needn't reach their ends.
Inputs may be any that keep to these rules, and one draw needn't show every extreme that they name: `shot_ids`: shot numbers never fall along a video; each shot has 1 to 48 frames. `band_width`: one block of each video has 64.
All inputs are finite; a program needn't handle non-finite values.
Results may differ from the reference program's by a relative error of at most 0.019.
Values may be sent and summed in bfloat16 or wider, within the bound.
A program may use at most 192 MiB of HBM per device.

```python
import math
import jax
import jax.numpy as jnp
import numpy as np
from jax import lax

D = 1152
H = 3584
TOKS = 81
FRAMES = 256
BLOCK = 64
POOL = 8
SHOTS = 16
VIDEOS = 8
BLOCKS = 4
PFRAMES = 32


def draw_band_width(key, part):
    key = jax.random.fold_in(key, 7)
    first_key, second_key = jax.random.split(key)
    widths = jax.random.randint(first_key, (VIDEOS, BLOCKS), 2, BLOCK + 1)
    chosen = jax.random.randint(second_key, (VIDEOS,), 0, BLOCKS)
    return jnp.where(jnp.arange(BLOCKS)[None, :] == chosen[:, None], BLOCK, widths).astype(jnp.int32)


def level_of(own_key, extent, cuts, smallest, largest):
    def one(axis_at, blocks):
        heights = jax.random.uniform(jax.random.fold_in(jax.random.fold_in(own_key, 6), axis_at), (blocks,), jnp.float32, smallest / len(cuts), largest / len(cuts))
        return jnp.repeat(jnp.exp(heights), extent[axis_at] // blocks).reshape((-1,) + (1,) * (len(extent) - axis_at - 1))

    factor_of = one(*cuts[0])
    for cut in cuts[1:]:
        factor_of = factor_of * one(*cut)
    return factor_of


def split_up(amount, total, limit, skew):
    portions = [(1 << 20) // math.isqrt(grade ** skew) + 1 for grade in range(2, amount + 1)]
    surplus, given = total - limit - (amount - 1), [1] * (amount - 1)
    while surplus > 0:
        movable = [i for i in range(amount - 1) if given[i] < limit]
        whole, budget = sum([portions[i] for i in movable]), surplus
        for i in movable:
            extra = min(limit - given[i], max(1, budget * portions[i] // whole), surplus)
            given[i] = given[i] + extra
            surplus = surplus - extra
    return np.array([limit] + given)


def ragged(own_key, number_of, total, limit, lean):
    if number_of == 2:
        one = jax.random.randint(own_key, (), max(1, total - limit), min(limit, total - 1) + 1)
        return jnp.stack([one, total - one])
    sizes = jnp.asarray(split_up(number_of, total, limit, lean), jnp.int32)
    pairs = (number_of - 1) // 2
    source_of, taker = sizes[1:1 + 2 * pairs:2], sizes[2:2 + 2 * pairs:2]
    slack = jnp.minimum(source_of - 1, limit - taker)
    passed = jax.random.randint(jax.random.fold_in(own_key, 1), (pairs,), 0, 1 << 20) % (slack + 1)
    sizes = sizes.at[1:1 + 2 * pairs:2].set(source_of - passed).at[2:2 + 2 * pairs:2].set(taker + passed)
    return sizes[jax.random.permutation(jax.random.fold_in(own_key, 2), number_of)]


def scatter_about(rng, dims, spread, reach, cuts=(), kind=jnp.bfloat16):
    result = jax.random.normal(rng, dims, jnp.float32) * spread
    if len(cuts) > 0:
        result = level_of(rng, dims, cuts, -0.22, 0.18) * result
    return jnp.clip(result, min=-reach, max=reach).astype(kind)


def setup_inputs(seed: int = 0) -> dict:
    arg_keys = jax.random.split(jax.random.key(seed), 6)
    return {
        "features": scatter_about(arg_keys[0], (VIDEOS, FRAMES, TOKS, D), 1.0, 6.0, ((0, 4), (1, 32))),
        "shot_ids": jax.vmap(lambda own: jnp.searchsorted(jnp.cumsum(ragged(own, SHOTS, FRAMES, 48, 2)), jnp.arange(FRAMES), side="right"))(jax.random.split(arg_keys[1], VIDEOS)).reshape((VIDEOS, FRAMES)).astype(jnp.int32),
        "band_width": draw_band_width(jax.random.fold_in(arg_keys[5], 71), 0),
        "proj_weight": scatter_about(arg_keys[3], (D, H), D ** -0.5, 0.1875),
        "cotangent": scatter_about(arg_keys[4], (VIDEOS, PFRAMES, TOKS, H), 0.1, 1.5, ((0, 4), (1, 32))),
    }


decay_length = 16.0

def gelu_tanh(values):
    return jax.nn.gelu(values, approximate=True)

def mixing_weights(shot_ids, band_width):
    block_shots = shot_ids.reshape(shot_ids.shape[:-1] + (-1, BLOCK))
    position = jnp.arange(BLOCK)
    distance = jnp.abs(position[:, None] - position[None, :])
    same_shot = block_shots[..., :, None] == block_shots[..., None, :]
    allowed = same_shot & (distance <= band_width[..., None, None])
    raw_weight = jnp.where(allowed, jnp.exp(-distance.astype(jnp.float32) / decay_length), jnp.float32(0.0))
    return (raw_weight / lax.optimization_barrier(jnp.sum(raw_weight, axis=-1, keepdims=True))).astype(jnp.bfloat16)

def combine_weights(mix_weight):
    lead = mix_weight.shape[:-2]
    grouped = mix_weight.astype(jnp.float32).reshape(lead + (BLOCK // POOL, POOL, BLOCK))
    return (grouped.sum(axis=-2) * 0.125).astype(jnp.bfloat16)

def reference(features, shot_ids, band_width, proj_weight, cotangent):

    def one_video(grad_total, inputs):
        frames, shots_video, band_video, cot_video = inputs
        combined = combine_weights(mixing_weights(shots_video, band_video)).astype(jnp.float32)
        blocks = frames.reshape(BLOCKS, BLOCK, TOKS * D).astype(jnp.float32)
        pooled = jnp.einsum('bps,bsf->bpf', combined, blocks).astype(jnp.bfloat16).reshape(PFRAMES * TOKS, D)
        preact = jnp.dot(pooled, proj_weight, preferred_element_type=jnp.float32)
        activation, pullback = jax.vjp(gelu_tanh, preact)
        grad_preact = pullback(cot_video.reshape(PFRAMES * TOKS, H).astype(jnp.float32))[0].astype(jnp.bfloat16)
        grad_term = jnp.dot(pooled.T, grad_preact, preferred_element_type=jnp.float32)
        projected = activation.astype(jnp.bfloat16).reshape(PFRAMES, TOKS, H)
        return (grad_total + grad_term, projected)
    grad_total, projected = lax.scan(one_video, jnp.zeros((D, H), jnp.float32), (features, shot_ids, band_width, cotangent))
    return (projected, grad_total)
```

```python
import jax
import jax.numpy as jnp
from jax import lax
from jax.experimental import pallas as pl
from jax.experimental.pallas import tpu as pltpu
from jax.sharding import PartitionSpec as P

BLOCK = 64
POOL = 8
DECAY = 16.0
F32, BF16 = jnp.float32, jnp.bfloat16
MESH = pl.DeviceIdType.MESH

D, H, TOKS = 1152, 3584, 81
ROWS = 2 * TOKS
PADDED = 176
XL = 512
YL = D - XL
CHUNK = H // 4
HALF = 512
STEP = CHUNK - HALF
SUB = 24
DY = (2, 1, 3, 0)
J2, J1, J3, J0 = 0, 1, 2, 3
C0 = 0.7978845608028654
C1 = 0.044715


def add16(a, b):
    return (a.astype(F32) + b.astype(F32)).astype(BF16)


def kernel(
    feat, wgt, cot, shots, band,
    out_proj, out_grad,
    fv, wv, cn, cv, pa, pre, kron, part, sel, pb, pt, gr,
    xa, xfu, xfd, xnu, xnd, yfu, yfd, ynu, ynd, sb, yx,
    g,
    a_fu, a_fd, a_nu, a_nd, a_1, a_gu, a_gd, a_mu, a_md, a_2, a_r,
    b_fu, b_fd, b_nu, b_nd, b_1, b_gu, b_gd, b_mu, b_md, b_2, b_r,
    c_fu, c_fd, c_nu, c_nd, c_1, c_gu, c_gd, c_mu, c_md, c_2, c_r,
    fin, fs, fr,
    local_sem, send_sem, recv_sem,
):
    dp, tm = lax.axis_index("dp"), lax.axis_index("tm")
    x_hi, core = lax.div(dp, 2), lax.rem(dp, 2)
    z, y, lo = lax.div(tm, 8), lax.rem(lax.div(tm, 2), 4), lax.rem(tm, 2)
    x = x_hi * 2 + lo

    def dev(xx=x, yy=y, zz=z, cc=core):
        return (lax.div(xx, 2) * 2 + cc, zz * 8 + yy * 2 + lax.rem(xx, 2))

    def ring(value, step):
        return lax.rem(value + step, 4)

    mate = x_hi * 2 + 1 - lo
    x_of = [ring(x, d) for d in range(4)]
    y_of = [ring(y, d) for d in range(4)]
    z_of = [ring(z, d) for d in range(4)]
    hi_of = [lax.div(v, 2) for v in x_of]
    off_of = [pl.multiple_of(lax.rem(v, 2) * STEP, 128) for v in x_of]
    cut = [pl.ds(o, HALF) for o in off_of]

    count = [0, 0]
    sends = []

    def settle():
        for copy in sends:
            copy.wait_send()
        sends.clear()

    def local(src, dst):
        i = count[0]
        count[0] += 1
        copy = pltpu.make_async_copy(src, dst, local_sem.at[i])
        copy.start()
        return copy

    def send(src, dst, to):
        i = count[1]
        count[1] += 1
        copy = pltpu.make_async_remote_copy(
            src_ref=src, dst_ref=dst, send_sem=send_sem.at[i], recv_sem=recv_sem.at[i],
            device_id=to, device_id_type=MESH,
        )
        copy.start()
        sends.append(copy)
        return copy

    la, lb = pl.ds(0, XL), pl.ds(XL, YL)
    feat_a = local(feat.at[:, :, la], fv.at[:, :, la])
    feat_b = local(feat.at[:, :, lb], fv.at[:, :, lb])

    barrier = pltpu.get_barrier_semaphore()
    group = [(lx, dy) for dy in range(4) for lx in (0, 1) if (lx, dy) != (0, 0)]
    friends = [dev(xx=mate if lx else x, yy=y_of[dy]) for lx, dy in group]
    far_x = [ring(x, 2), ring(mate, 2)]
    friends += [dev(xx=v) for v in far_x]
    friends += [dev(zz=z_of[d]) for d in (1, 2, 3)]
    friends += [dev(cc=1 - core)]
    for friend in friends:
        pl.semaphore_signal(barrier, inc=1, device_id=friend, device_id_type=MESH)

    def iota(shape, axis):
        return lax.broadcasted_iota(jnp.int32, shape, axis)

    frame, other = iota((BLOCK, 128), 0), iota((BLOCK, 128), 1)
    distance = jnp.abs(frame - other)
    decay = jnp.exp(-distance.astype(F32) / DECAY)
    ids = shots[...].astype(F32)
    ids = jnp.where(z < 2, ids[:, 0:128], ids[:, 128:256])
    ids = jnp.where(lax.rem(z, 2) == 0, ids, pltpu.roll(ids, 64, 1))
    target_of = iota((256, 128), 0)
    rel = lax.div(target_of, 32)
    target_of = lax.rem(y + lax.div(rel, 2), 4) * 2 + jnp.where(lax.rem(rel, 2) == 0, lo, 1 - lo)
    own_frame = jnp.where(iota((128, 256), 0) == (y * 2 + lo) * POOL + lax.rem(iota((128, 256), 1), 8), 1.0, 0.0)
    own_frame = own_frame.astype(BF16)
    out_row, in_row = iota((256, 256), 0), iota((256, 256), 1)
    same_token = lax.div(lax.rem(out_row, 32), 2) == lax.div(lax.rem(in_row, 128), 8)
    spread = jnp.zeros((256, 256), F32)
    for v in range(2):
        along = jnp.broadcast_to(ids[v : v + 1], (BLOCK, 128))
        down_ids = jnp.sum(jnp.where(frame == other, along, 0.0), axis=1, keepdims=True)
        allowed = (along == down_ids) & (distance <= band[v, z]) & (other < BLOCK)
        raw = jnp.where(allowed, decay, 0.0)
        mix = (raw / jnp.sum(raw, axis=1, keepdims=True)).astype(BF16).astype(F32)
        combined = (mix.reshape(8, POOL, 128).sum(axis=1) * 0.125).astype(BF16).astype(F32)
        rows = jnp.zeros((256, 128), F32)
        for p in range(8):
            rows = jnp.where(target_of == p, combined[p : p + 1], rows)
        full = jnp.dot(rows.astype(BF16), own_frame, preferred_element_type=F32)
        mine_too = same_token & (lax.rem(out_row, 2) == v) & (lax.div(in_row, 128) == v)
        spread = jnp.where(mine_too, full, spread)
    kron[...] = spread.astype(BF16)

    def partial_sums(lanes):
        for c in range(6):
            if c < 5:
                blocks = [fv[v, 128 * c : 128 * c + 128, lanes] for v in range(2)]
            else:
                empty = jnp.zeros((120, lanes.stop - lanes.start), BF16)
                blocks = [b for v in range(2) for b in (fv[v, 640:648, lanes], empty)]
            got = jnp.dot(kron[...], jnp.concatenate(blocks, axis=0), preferred_element_type=F32)
            size = 32 if c < 5 else 2
            for r in range(8):
                part[r // 2, r % 2, 32 * c : 32 * c + size, lanes] = got[32 * r : 32 * r + size].astype(BF16)

    l1, l2 = pl.ds(0, XL // 2), pl.ds(XL // 2, XL // 2)
    up, down, side, twin = dev(yy=y_of[1]), dev(yy=y_of[3]), dev(xx=mate), dev(cc=1 - core)

    feat_a.wait()
    partial_sums(slice(0, XL))
    pl.semaphore_wait(barrier, len(friends))
    x_first = {dy: send(part.at[dy, 1, :, la], xa.at[dy], side) for dy in (2, 1, 3, 0)}
    feat_b.wait()
    partial_sums(slice(XL, D))
    far_up = send(part.at[2, 0, :, lb], yfu, up)
    far_down = send(part.at[2, 1, :, lb], yfd, down)
    near_up = {1: send(part.at[1, 1, :, lb], ynu.at[1], up)}
    near_down = {0: send(part.at[3, 0, :, lb], ynd.at[0], down)}

    columns = [pl.ds(pl.multiple_of(y_of[d] * CHUNK, 128), CHUNK) for d in DY]
    cot_in = [local(cot.at[:, :, columns[j]], cn.at[j]) for j in range(4)]
    wgt_in = [local(wgt.at[:, columns[j]], wv.at[j]) for j in range(4)]

    row, col = iota((576, D), 0), iota((576, D), 1)
    wanted = row + core * 288 + jnp.where(row >= 288, 288, 0)
    sel[...] = jnp.where(col == wanted, 1.0, 0.0).astype(BF16)

    def take(dy):
        x_first[dy].wait_recv()
        xa[dy] = add16(xa[dy], part[dy, 0, :, 0:XL])

    take(2)
    far_up2 = send(xa.at[2, :, l1], xfu, up)
    far_up.wait_recv()
    yfu[...] = add16(yfu[...], part[1, 0, :, XL:D])
    near_up[0] = send(yfu, ynu.at[0], up)
    far_down.wait_recv()
    yfd[...] = add16(yfd[...], part[3, 1, :, XL:D])
    near_down[1] = send(yfd, ynd.at[1], down)
    far_down2 = send(xa.at[2, :, l2], xfd, down)
    take(1)
    near_up2 = [send(xa.at[1, :, l2], xnu.at[:, l2], up)]
    take(3)
    near_down2 = [send(xa.at[3, :, l1], xnd.at[:, l1], down)]

    for j in range(4):
        cot_in[j].wait()

        @pl.loop(0, 10)
        def _(i):
            cv[j, pl.ds(pl.multiple_of(i * 16, 16), 16), :] = cn[j, pl.ds(i * 8, 8)].reshape(16, CHUNK)

        tail = jnp.concatenate([cn[j, 80].astype(F32), jnp.zeros((14, CHUNK), F32)], axis=0)
        cv[j, 160:176, :] = tail.astype(BF16)

    far_up2.wait_recv()
    xfu[...] = add16(xfu[...], xa[1, :, 0 : XL // 2])
    near_up2.append(send(xfu, xnu.at[:, l1], up))
    near_up[1].wait_recv()
    near_down[1].wait_recv()
    sb[...] = (
        part[0, 1, :, XL:D].astype(F32) + ynu[1].astype(F32) + ynd[1].astype(F32)
    ).astype(BF16)
    last_x = send(sb, yx, side)
    far_down2.wait_recv()
    xfd[...] = add16(xfd[...], xa[3, :, XL // 2 : XL])
    near_down2.append(send(xfd, xnd.at[:, l2], down))

    def keep(value, lanes):
        value = value.astype(BF16)
        pb[0:160, lanes] = value[0:160]
        tail = jnp.concatenate(
            [value[160:162].astype(F32), jnp.zeros((14, value.shape[1]), F32)], axis=0
        )
        pb[160:176, lanes] = tail.astype(BF16)

    take(0)
    for copy in near_up2 + near_down2:
        copy.wait_recv()
    keep(xa[0].astype(F32) + xnu[...].astype(F32) + xnd[...].astype(F32), slice(0, XL))
    near_up[0].wait_recv()
    near_down[0].wait_recv()
    last_x.wait_recv()
    keep(
        part[0, 0, :, XL:D].astype(F32) + ynu[0].astype(F32) + ynd[0].astype(F32) + yx[...].astype(F32),
        slice(XL, D),
    )
    pooled_twin = send(pb.at[pl.ds(0, PADDED)], pb.at[pl.ds(PADDED, PADDED)], twin)

    grad_twin = []

    def gelu_rows(values, cotangent):
        square = values * values
        t = jnp.tanh(values * (C0 + (C0 * C1) * square))
        plus = 0.5 * (1.0 + t)
        slope = plus + (0.5 * values) * (1.0 - t * t) * (C0 + (3.0 * C0 * C1) * square)
        return (values * plus).astype(BF16), (cotangent * slope).astype(BF16)

    def forward(j):
        wgt_in[j].wait()
        pre[...] = jnp.dot(pb[0:PADDED, :], wv[j], preferred_element_type=F32)

        @pl.loop(0, 11)
        def _(i):
            rows = pl.ds(pl.multiple_of(i * 16, 16), 16)
            act, grad = gelu_rows(pre[rows, :], cv[j, rows, :].astype(F32))
            pa[j, rows, :] = act
            gr[j, rows, :] = grad

        grad_twin.append(send(gr.at[j, pl.ds(0, PADDED)], gr.at[j, pl.ds(PADDED, PADDED)], twin))

    def give(j):
        @pl.loop(0, 10)
        def _(i):
            rows = pl.ds(pl.multiple_of(i * 16, 16), 16)
            out_proj[pl.ds(i * 8, 8), :, columns[j]] = pa[j, rows, :].reshape(8, 2, CHUNK)

        out_proj[80, :, columns[j]] = pa[j, 160:162, :]

    z_up, z_down = dev(zz=z_of[1]), dev(zz=z_of[3])
    x_up, x_down = dev(xx=x_of[1]), dev(xx=x_of[3])
    zlo, zhi = pl.ds(0, 2), pl.ds(2, 2)
    msg = {}

    def backward(j):
        grad_twin[j].wait_recv()
        for h in range(2):
            got = jnp.dot(pt[288 * h : 288 * h + 288, :], gr[j], preferred_element_type=F32)
            for zz in range(4):
                for s in range(3):
                    at = zz * 72 + s * SUB
                    g[s, h, zz, j] = got[at : at + SUB].astype(BF16)
        msg["afu", j] = send(g.at[0, 0, z_of[2], j], a_fu.at[j], z_up)
        msg["afd", j] = send(g.at[0, 1, z_of[2], j], a_fd.at[j], z_down)
        msg["cfu", j] = send(g.at[2, hi_of[2], zlo, j, :, cut[2]], c_fu.at[j], x_up)
        msg["cfd", j] = send(g.at[2, hi_of[2], zhi, j, :, cut[2]], c_fd.at[j], x_down)
        if j == J2:
            msg["bfu"] = send(g.at[1, 0, :, j], b_fu, up)
            msg["bfd"] = send(g.at[1, 1, :, j], b_fd, down)
        if j == J1:
            msg["bnu1"] = send(g.at[1, 1, :, j], b_nu.at[1], up)
        if j == J3:
            msg["bnd0"] = send(g.at[1, 0, :, j], b_nd.at[0], down)
        msg["anu1", j] = send(g.at[0, 1, z_of[1], j], a_nu.at[j, 1], z_up)
        msg["and0", j] = send(g.at[0, 0, z_of[3], j], a_nd.at[j, 0], z_down)
        msg["cnu1", j] = send(g.at[2, hi_of[1], zhi, j, :, cut[1]], c_nu.at[j, zhi], x_up)
        msg["cnd0", j] = send(g.at[2, hi_of[3], zlo, j, :, cut[3]], c_nd.at[j, zlo], x_down)

    def relay(j):
        msg["afu", j].wait_recv()
        a_fu[j] = add16(a_fu[j], g[0, 0, z_of[1], j])
        msg["anu0", j] = send(a_fu.at[j], a_nu.at[j, 0], z_up)
        msg["afd", j].wait_recv()
        a_fd[j] = add16(a_fd[j], g[0, 1, z_of[3], j])
        msg["and1", j] = send(a_fd.at[j], a_nd.at[j, 1], z_down)
        msg["cfu", j].wait_recv()
        c_fu[j] = add16(c_fu[j], g[2, hi_of[1], 0:2, j, :, cut[1]])
        msg["cnu0", j] = send(c_fu.at[j], c_nu.at[j, zlo], x_up)
        msg["cfd", j].wait_recv()
        c_fd[j] = add16(c_fd[j], g[2, hi_of[3], 2:4, j, :, cut[3]])
        msg["cnd1", j] = send(c_fd.at[j], c_nd.at[j, zhi], x_down)
        if j == J1:
            msg["bfu"].wait_recv()
            b_fu[...] = add16(b_fu[...], g[1, 0, :, J1])
            msg["bnu0"] = send(b_fu, b_nu.at[0], up)
        if j == J3:
            msg["bfd"].wait_recv()
            b_fd[...] = add16(b_fd[...], g[1, 1, :, J3])
            msg["bnd1"] = send(b_fd, b_nd.at[1], down)

    forward(0)
    pooled_twin.wait_recv()
    pt[...] = lax.dot_general(
        sel[...], pb[...], (((1,), (1,)), ((), ())), preferred_element_type=F32
    ).astype(BF16)
    backward(0)
    forward(1)
    forward(2)
    backward(1)
    relay(0)
    forward(3)
    backward(2)
    relay(1)
    backward(3)
    relay(2)
    relay(3)

    def three(a, b, c):
        return (a.astype(F32) + b.astype(F32) + c.astype(F32)).astype(BF16)

    def wait(*names):
        for name in names:
            msg[name].wait_recv()

    for j in range(4):
        wait(("anu0", j), ("anu1", j), ("and0", j), ("and1", j))
        a_1[:, j] = three(g[0, :, z, j], a_nu[j], a_nd[j])
        if j == J2:
            msg["agu"] = send(a_1.at[0, j], a_gu, up)
            msg["agd"] = send(a_1.at[1, j], a_gd, down)
        if j == J1:
            msg["amu1"] = send(a_1.at[1, j], a_mu.at[1], up)
        if j == J3:
            msg["amd0"] = send(a_1.at[0, j], a_md.at[0], down)
        wait(("cnu0", j), ("cnu1", j), ("cnd0", j), ("cnd1", j))
        c_1[:, j] = three(g[2, x_hi, :, j, :, cut[0]], c_nu[j], c_nd[j])
        if j == 1:
            msg["cgu"] = send(c_1.at[z_of[2], pl.ds(0, 2)], c_gu, z_up)
            msg["cmd0"] = send(c_1.at[z_of[3], pl.ds(0, 2)], c_md.at[pl.ds(0, 2)], z_down)
        if j == 3:
            msg["cgd"] = send(c_1.at[z_of[2], pl.ds(2, 2)], c_gd, z_down)
            msg["cmu1"] = send(c_1.at[z_of[1], pl.ds(2, 2)], c_mu.at[pl.ds(2, 2)], z_up)
        if j == 2:
            give(0)
            give(1)
    wait("bnu0", "bnu1", "bnd0", "bnd1")
    b_1[...] = three(g[1, :, :, J0], b_nu[...], b_nd[...])
    msg["bgu"] = send(b_1.at[hi_of[2], zlo, :, cut[2]], b_gu, x_up)
    msg["bgd"] = send(b_1.at[hi_of[2], zhi, :, cut[2]], b_gd, x_down)
    msg["bmu1"] = send(b_1.at[hi_of[1], zhi, :, cut[1]], b_mu.at[zhi], x_up)
    msg["bmd0"] = send(b_1.at[hi_of[3], zlo, :, cut[3]], b_md.at[zlo], x_down)

    wait("agu")
    a_gu[...] = add16(a_gu[...], a_1[0, J1])
    msg["amu0"] = send(a_gu, a_mu.at[0], up)
    wait("agd")
    a_gd[...] = add16(a_gd[...], a_1[1, J3])
    msg["amd1"] = send(a_gd, a_md.at[1], down)
    wait("cgu")
    c_gu[...] = add16(c_gu[...], c_1[z_of[1], 0:2])
    msg["cmu0"] = send(c_gu, c_mu.at[pl.ds(0, 2)], z_up)
    wait("cgd")
    c_gd[...] = add16(c_gd[...], c_1[z_of[3], 2:4])
    msg["cmd1"] = send(c_gd, c_md.at[pl.ds(2, 2)], z_down)
    give(2)
    wait("bgu")
    b_gu[...] = add16(b_gu[...], b_1[hi_of[1], 0:2, :, cut[1]])
    msg["bmu0"] = send(b_gu, b_mu.at[zlo], x_up)
    wait("bgd")
    b_gd[...] = add16(b_gd[...], b_1[hi_of[3], 2:4, :, cut[3]])
    msg["bmd1"] = send(b_gd, b_md.at[zhi], x_down)

    give(3)

    wait("amu0", "amu1", "amd0", "amd1")
    a_2[...] = three(a_1[:, J0], a_mu[...], a_md[...])
    for d in (2, 1, 3):
        msg["ar", d] = send(a_2.at[hi_of[d], :, cut[d]], a_r.at[d], dev(xx=x_of[d]))
    wait("cmu0", "cmu1", "cmd0", "cmd1")
    c_2[...] = three(c_1[z], c_mu[...], c_md[...])
    for j in (J2, J1, J3):
        msg["cr", j] = send(c_2.at[j], c_r.at[j], dev(yy=y_of[DY[j]]))
    wait("bmu0", "bmu1", "bmd0", "bmd1")
    b_2[...] = three(b_1[x_hi, :, :, cut[0]], b_mu[...], b_md[...])
    for d in (2, 1, 3):
        msg["br", d] = send(b_2.at[z_of[d]], b_r.at[d], dev(zz=z_of[d]))

    def total(own, parts):
        value = own.astype(F32)
        for p in parts:
            value = value + p.astype(F32)
        return value

    settle()
    wait(("ar", 1), ("ar", 2), ("ar", 3))
    fin[0:SUB] = total(a_2[x_hi, :, cut[0]], [a_r[d] for d in (1, 2, 3)])
    wait(("cr", J1), ("cr", J2), ("cr", J3))
    fin[2 * SUB : 3 * SUB] = total(c_2[J0], [c_r[j] for j in (J1, J2, J3)])
    wait(("br", 1), ("br", 2), ("br", 3))
    fin[SUB : 2 * SUB] = total(b_2[z], [b_r[d] for d in (1, 2, 3)])

    for e in range(8):
        fs[e] = fin[9 * e : 9 * e + 9].astype(BF16)
    mine = y * 2 + lo
    for lx, dy in group:
        to_lo = 1 - lo if lx else lo
        owner = y_of[dy] * 2 + to_lo
        msg["out", lx, dy] = send(
            fs.at[owner], fr.at[lx, dy], dev(xx=mate if lx else x, yy=y_of[dy])
        )
    fr[0, 0] = fs[mine]
    for lx, dy in group:
        wait(("out", lx, dy))
    for first in (0, 1):
        for dy in range(4):
            base = y_of[(4 - dy) % 4] * CHUNK + first * STEP
            value = jnp.where(lo == first, fr[0, dy].astype(F32), fr[1, dy].astype(F32))
            out_grad[:, pl.ds(pl.multiple_of(base, 128), HALF)] = value

    settle()


def hand_over(projected, weight_grad, out_projected, out_grad, sem):
    copies = [pltpu.make_async_copy(weight_grad, out_grad, sem.at[9])]
    for i in range(9):
        rows = pl.ds(9 * i, 9)
        copies.append(pltpu.make_async_copy(projected.at[rows], out_projected.at[rows], sem.at[i]))
    for copy in copies:
        copy.start()
    for copy in copies:
        copy.wait()


N_LOCAL = 2 + 4 + 4
N_SEND = 160


def per_device(features, shot_ids, band_width, proj_weight, cotangent):
    frames = jnp.swapaxes(features, 1, 2).reshape(2, TOKS * POOL, D)
    cot = cotangent.transpose(1, 2, 0, 3).reshape(TOKS, 2, H)
    vm = lambda *shape: pltpu.VMEM(shape, BF16)
    scratch = [
        vm(2, TOKS * POOL, D), vm(4, D, CHUNK), vm(4, TOKS, 2, CHUNK), vm(4, PADDED, CHUNK),
        vm(4, PADDED, CHUNK),
        pltpu.VMEM((PADDED, CHUNK), F32), vm(256, 256), vm(4, 2, ROWS, D), vm(576, D),
        vm(2 * PADDED, D), vm(576, 2 * PADDED), vm(4, 2 * PADDED, CHUNK),
        vm(4, ROWS, XL), vm(ROWS, XL // 2), vm(ROWS, XL // 2), vm(ROWS, XL), vm(ROWS, XL),
        vm(ROWS, YL), vm(ROWS, YL), vm(2, ROWS, YL), vm(2, ROWS, YL), vm(ROWS, YL), vm(ROWS, YL),
        vm(3, 2, 4, 4, SUB, CHUNK),
        vm(4, SUB, CHUNK), vm(4, SUB, CHUNK), vm(4, 2, SUB, CHUNK), vm(4, 2, SUB, CHUNK),
        vm(2, 4, SUB, CHUNK), vm(SUB, CHUNK), vm(SUB, CHUNK), vm(2, SUB, CHUNK), vm(2, SUB, CHUNK),
        vm(2, SUB, CHUNK), vm(4, SUB, HALF),
        vm(4, SUB, CHUNK), vm(4, SUB, CHUNK), vm(2, 4, SUB, CHUNK), vm(2, 4, SUB, CHUNK),
        vm(2, 4, SUB, CHUNK), vm(2, SUB, HALF), vm(2, SUB, HALF), vm(4, SUB, HALF), vm(4, SUB, HALF),
        vm(4, SUB, HALF), vm(4, SUB, HALF),
        vm(4, 2, SUB, HALF), vm(4, 2, SUB, HALF), vm(4, 4, SUB, HALF), vm(4, 4, SUB, HALF),
        vm(4, 4, SUB, HALF), vm(2, SUB, HALF), vm(2, SUB, HALF), vm(4, SUB, HALF), vm(4, SUB, HALF),
        vm(4, SUB, HALF), vm(4, SUB, HALF),
        pltpu.VMEM((72, HALF), F32), vm(8, 9, HALF), vm(2, 4, 9, HALF),
        pltpu.SemaphoreType.DMA((N_LOCAL,)),
        pltpu.SemaphoreType.DMA((N_SEND,)),
        pltpu.SemaphoreType.DMA((N_SEND,)),
    ]
    any_spec = pl.BlockSpec(memory_space=pl.ANY)
    vmem_spec = pl.BlockSpec(memory_space=pltpu.VMEM)
    smem_spec = pl.BlockSpec(memory_space=pltpu.SMEM)
    projected, weight_grad = pl.pallas_call(
        kernel,
        out_shape=(
            pltpu.VMEM(cot.shape, BF16),
            pltpu.VMEM((9, H), F32),
        ),
        in_specs=[any_spec, any_spec, any_spec, vmem_spec, smem_spec],
        out_specs=(vmem_spec, vmem_spec),
        scratch_shapes=scratch,
        compiler_params=pltpu.CompilerParams(
            collective_id=0, has_side_effects=True, vmem_limit_bytes=50 * 1024 * 1024
        ),
        cost_estimate=pl.CostEstimate(flops=4 * 10**9, bytes_accessed=14 * 10**6, transcendentals=600000),
    )(frames, proj_weight, cot, shot_ids, band_width)
    projected, weight_grad = pl.pallas_call(
        hand_over,
        out_shape=(
            jax.ShapeDtypeStruct(projected.shape, BF16),
            jax.ShapeDtypeStruct(weight_grad.shape, F32),
        ),
        in_specs=[vmem_spec, vmem_spec],
        out_specs=(any_spec, any_spec),
        scratch_shapes=[pltpu.SemaphoreType.DMA((10,))],
    )(projected, weight_grad)
    return projected.reshape(1, TOKS, 2, H).transpose(2, 0, 1, 3), weight_grad


def solution(mesh):
    return jax.shard_map(
        per_device,
        mesh=mesh,
        in_specs=(
            P("dp", "tm", None, None),
            P("dp", None),
            P("dp", None),
            P(),
            P("dp", "tm", None, None),
        ),
        out_specs=(P("dp", "tm", None, None), P(("dp", "tm"), None)),
        check_vma=False,
    )
```

```python
import jax
import jax.numpy as jnp
from jax import lax
from jax.experimental import pallas as pl
from jax.experimental.pallas import tpu as pltpu
from jax.sharding import PartitionSpec as P

BLOCK = 64
POOL = 8
DECAY = 16.0
F32, BF16 = jnp.float32, jnp.bfloat16
MESH = pl.DeviceIdType.MESH

D, H, TOKS = 1152, 3584, 81
ROWS = 2 * TOKS
PADDED = 176
XL = 512
YL = D - XL
CHUNK = H // 4
ORDER = (("z", "y", "x"), ("y", "x", "z"), ("x", "z", "y"))
S1, S2, S3 = 24, 12, 3
C0 = 0.7978845608028654
C1 = 0.044715


def add16(a, b):
    return (a.astype(F32) + b.astype(F32)).astype(BF16)


def kernel(
    feat, wgt, cot, shots_in, band_in,
    out_proj, out_grad,
    fv, wv, cn, cv, pa, pre, kron, part, sel, pb, pt, gr,
    xa, xfu, xfd, xnu, xnd, yfu, yfd, ynu, ynd, sb, yx,
    g,
    fu, fd, nu, nd, r1, fu2, fd2, nu2, nd2, r2, r3,
    ids_v, band_s,
    local_sem, send_sem, recv_sem,
):
    dp, tm = lax.axis_index("dp"), lax.axis_index("tm")
    x_hi, core = lax.div(dp, 2), lax.rem(dp, 2)
    z, y, lo = lax.div(tm, 8), lax.rem(lax.div(tm, 2), 4), lax.rem(tm, 2)
    x = x_hi * 2 + lo

    def dev(xx=x, yy=y, zz=z, cc=core):
        return (lax.div(xx, 2) * 2 + cc, zz * 8 + yy * 2 + lax.rem(xx, 2))

    def ring(value, step):
        return lax.rem(value + step, 4)

    mate = x_hi * 2 + 1 - lo
    here = {"x": x, "y": y, "z": z}
    index = {axis: [ring(here[axis], d) for d in range(4)] for axis in "xyz"}
    hop = {axis: [dev(**{axis * 2: index[axis][d]}) for d in range(4)] for axis in "xyz"}

    count = [0, 0]
    sends = []

    def settle():
        for copy in sends:
            copy.wait_send()
        sends.clear()

    def local(src, dst):
        i = count[0]
        count[0] += 1
        copy = pltpu.make_async_copy(src, dst, local_sem.at[i])
        copy.start()
        return copy

    def send(src, dst, to):
        i = count[1]
        count[1] += 1
        copy = pltpu.make_async_remote_copy(
            src_ref=src, dst_ref=dst, send_sem=send_sem.at[i], recv_sem=recv_sem.at[i],
            device_id=to, device_id_type=MESH,
        )
        copy.start()
        sends.append(copy)
        return copy

    la, lb = pl.ds(0, XL), pl.ds(XL, YL)
    ids_in = local(shots_in, ids_v)
    width_in = local(band_in, band_s)
    feat_a = local(feat.at[:, :, la], fv.at[:, :, la])
    feat_b = local(feat.at[:, :, lb], fv.at[:, :, lb])

    barrier = pltpu.get_barrier_semaphore()
    friends = [hop[axis][d] for axis in "xyz" for d in (1, 2, 3)] + [dev(cc=1 - core)]
    for friend in friends:
        pl.semaphore_signal(barrier, inc=1, device_id=friend, device_id_type=MESH)

    def iota(shape, axis):
        return lax.broadcasted_iota(jnp.int32, shape, axis)

    frame, other = iota((BLOCK, 128), 0), iota((BLOCK, 128), 1)
    distance = jnp.abs(frame - other)
    decay = jnp.exp(-distance.astype(F32) / DECAY)
    ids_in.wait()
    width_in.wait()
    ids = ids_v[...].astype(F32)
    ids = jnp.where(z < 2, ids[:, 0:128], ids[:, 128:256])
    ids = jnp.where(lax.rem(z, 2) == 0, ids, pltpu.roll(ids, 64, 1))
    target_of = iota((256, 128), 0)
    rel = lax.div(target_of, 32)
    target_of = lax.rem(y + lax.div(rel, 2), 4) * 2 + jnp.where(lax.rem(rel, 2) == 0, lo, 1 - lo)
    own_frame = jnp.where(iota((128, 256), 0) == (y * 2 + lo) * POOL + lax.rem(iota((128, 256), 1), 8), 1.0, 0.0)
    own_frame = own_frame.astype(BF16)
    out_row, in_row = iota((256, 256), 0), iota((256, 256), 1)
    same_token = lax.div(lax.rem(out_row, 32), 2) == lax.div(lax.rem(in_row, 128), 8)
    spread = jnp.zeros((256, 256), F32)
    for v in range(2):
        along = jnp.broadcast_to(ids[v : v + 1], (BLOCK, 128))
        down_ids = jnp.sum(jnp.where(frame == other, along, 0.0), axis=1, keepdims=True)
        allowed = (along == down_ids) & (distance <= band_s[v, z]) & (other < BLOCK)
        raw = jnp.where(allowed, decay, 0.0)
        mix = (raw / jnp.sum(raw, axis=1, keepdims=True)).astype(BF16).astype(F32)
        combined = (mix.reshape(8, POOL, 128).sum(axis=1) * 0.125).astype(BF16).astype(F32)
        rows = jnp.zeros((256, 128), F32)
        for p in range(8):
            rows = jnp.where(target_of == p, combined[p : p + 1], rows)
        full = jnp.dot(rows.astype(BF16), own_frame, preferred_element_type=F32)
        mine_too = same_token & (lax.rem(out_row, 2) == v) & (lax.div(in_row, 128) == v)
        spread = jnp.where(mine_too, full, spread)
    kron[...] = spread.astype(BF16)

    def partial_sums(lanes):
        for c in range(6):
            if c < 5:
                blocks = [fv[v, 128 * c : 128 * c + 128, lanes] for v in range(2)]
            else:
                empty = jnp.zeros((120, lanes.stop - lanes.start), BF16)
                blocks = [b for v in range(2) for b in (fv[v, 640:648, lanes], empty)]
            got = jnp.dot(kron[...], jnp.concatenate(blocks, axis=0), preferred_element_type=F32)
            size = 32 if c < 5 else 2
            for r in range(8):
                part[r // 2, r % 2, 32 * c : 32 * c + size, lanes] = got[32 * r : 32 * r + size].astype(BF16)

    l1, l2 = pl.ds(0, XL // 2), pl.ds(XL // 2, XL // 2)
    up, down, side, twin = hop["y"][1], hop["y"][3], dev(xx=mate), dev(cc=1 - core)

    feat_a.wait()
    partial_sums(slice(0, XL))
    pl.semaphore_wait(barrier, len(friends))
    x_first = {dy: send(part.at[dy, 1, :, la], xa.at[dy], side) for dy in (2, 1, 3, 0)}
    feat_b.wait()
    partial_sums(slice(XL, D))
    far_up = send(part.at[2, 0, :, lb], yfu, up)
    far_down = send(part.at[2, 1, :, lb], yfd, down)
    near_up = {1: send(part.at[1, 1, :, lb], ynu.at[1], up)}
    near_down = {0: send(part.at[3, 0, :, lb], ynd.at[0], down)}

    columns = [pl.ds(j * CHUNK, CHUNK) for j in range(4)]
    cot_in = [local(cot.at[:, :, columns[j]], cn.at[j]) for j in range(4)]
    wgt_in = [local(wgt.at[:, columns[j]], wv.at[j]) for j in range(4)]

    row, lane = iota((576, 128), 0), iota((576, 128), 1)
    which = lax.div(row, 192)
    first, second, third = lax.div(lax.rem(row, 192), 48), lax.div(lax.rem(row, 48), 12), lax.div(lax.rem(row, 12), 3)
    at = {}
    for axis in "xyz":
        at[axis] = jnp.zeros((576, 128), jnp.int32)
        for s in range(3):
            place = (first, second, third)[ORDER[s].index(axis)]
            at[axis] = jnp.where(which == s, place, at[axis])
    owner = (lax.div(at["x"], 2) * 2 + core) * 32 + at["z"] * 8 + at["y"] * 2 + lax.rem(at["x"], 2)
    wanted = owner * 9 + which * S3 + lax.rem(row, S3)
    for k in range(D // 128):
        sel[:, 128 * k : 128 * k + 128] = jnp.where(wanted == lane + 128 * k, 1.0, 0.0).astype(BF16)

    def take(dy):
        x_first[dy].wait_recv()
        xa[dy] = add16(xa[dy], part[dy, 0, :, 0:XL])

    take(2)
    far_up2 = send(xa.at[2, :, l1], xfu, up)
    far_up.wait_recv()
    yfu[...] = add16(yfu[...], part[1, 0, :, XL:D])
    near_up[0] = send(yfu, ynu.at[0], up)
    far_down.wait_recv()
    yfd[...] = add16(yfd[...], part[3, 1, :, XL:D])
    near_down[1] = send(yfd, ynd.at[1], down)
    far_down2 = send(xa.at[2, :, l2], xfd, down)
    take(1)
    near_up2 = [send(xa.at[1, :, l2], xnu.at[:, l2], up)]
    take(3)
    near_down2 = [send(xa.at[3, :, l1], xnd.at[:, l1], down)]

    for j in range(4):
        cot_in[j].wait()

        @pl.loop(0, 10)
        def _(i):
            cv[j, pl.ds(pl.multiple_of(i * 16, 16), 16), :] = cn[j, pl.ds(i * 8, 8)].reshape(16, CHUNK)

        tail = jnp.concatenate([cn[j, 80].astype(F32), jnp.zeros((14, CHUNK), F32)], axis=0)
        cv[j, 160:176, :] = tail.astype(BF16)

    far_up2.wait_recv()
    xfu[...] = add16(xfu[...], xa[1, :, 0 : XL // 2])
    near_up2.append(send(xfu, xnu.at[:, l1], up))
    near_up[1].wait_recv()
    near_down[1].wait_recv()
    sb[...] = (
        part[0, 1, :, XL:D].astype(F32) + ynu[1].astype(F32) + ynd[1].astype(F32)
    ).astype(BF16)
    last_x = send(sb, yx, side)
    far_down2.wait_recv()
    xfd[...] = add16(xfd[...], xa[3, :, XL // 2 : XL])
    near_down2.append(send(xfd, xnd.at[:, l2], down))

    def keep(value, lanes):
        value = value.astype(BF16)
        pb[0:160, lanes] = value[0:160]
        tail = jnp.concatenate(
            [value[160:162].astype(F32), jnp.zeros((14, value.shape[1]), F32)], axis=0
        )
        pb[160:176, lanes] = tail.astype(BF16)

    take(0)
    for copy in near_up2 + near_down2:
        copy.wait_recv()
    keep(xa[0].astype(F32) + xnu[...].astype(F32) + xnd[...].astype(F32), slice(0, XL))
    near_up[0].wait_recv()
    near_down[0].wait_recv()
    last_x.wait_recv()
    keep(
        part[0, 0, :, XL:D].astype(F32) + ynu[0].astype(F32) + ynd[0].astype(F32) + yx[...].astype(F32),
        slice(XL, D),
    )
    pooled_twin = send(pb.at[pl.ds(0, PADDED)], pb.at[pl.ds(PADDED, PADDED)], twin)

    grad_twin = []

    def gelu_rows(values, cotangent):
        square = values * values
        t = jnp.tanh(values * (C0 + (C0 * C1) * square))
        plus = 0.5 * (1.0 + t)
        slope = plus + (0.5 * values) * (1.0 - t * t) * (C0 + (3.0 * C0 * C1) * square)
        return (values * plus).astype(BF16), (cotangent * slope).astype(BF16)

    def forward(j):
        wgt_in[j].wait()
        pre[...] = jnp.dot(pb[0:PADDED, :], wv[j], preferred_element_type=F32)

        @pl.loop(0, 11)
        def _(i):
            rows = pl.ds(pl.multiple_of(i * 16, 16), 16)
            act, grad = gelu_rows(pre[rows, :], cv[j, rows, :].astype(F32))
            pa[j, rows, :] = act
            gr[j, rows, :] = grad

        grad_twin.append(send(gr.at[j, pl.ds(0, PADDED)], gr.at[j, pl.ds(PADDED, PADDED)], twin))

    def give(j):
        @pl.loop(0, 10)
        def _(i):
            rows = pl.ds(pl.multiple_of(i * 16, 16), 16)
            out_proj[pl.ds(i * 8, 8), :, columns[j]] = pa[j, rows, :].reshape(8, 2, CHUNK)

        out_proj[80, :, columns[j]] = pa[j, 160:162, :]

    msg = {}

    def wait(*names):
        for name in names:
            msg[name].wait_recv()

    def add3(a, b, c):
        return a.astype(F32) + b.astype(F32) + c.astype(F32)

    def backward(j):
        grad_twin[j].wait_recv()
        got = jnp.dot(pt[...], gr[j], preferred_element_type=F32)
        for s in range(3):
            for a in range(4):
                for h in range(2):
                    base = s * 192 + a * 48 + h * S1
                    g[s, a, h, j] = got[base : base + S1].astype(BF16)
        for s in range(3):
            i, to = index[ORDER[s][0]], hop[ORDER[s][0]]
            msg["fu", s, j] = send(g.at[s, i[2], 0, j], fu.at[s, j], to[1])
            msg["fd", s, j] = send(g.at[s, i[2], 1, j], fd.at[s, j], to[3])
        for s in range(3):
            i, to = index[ORDER[s][0]], hop[ORDER[s][0]]
            msg["nu1", s, j] = send(g.at[s, i[1], 1, j], nu.at[s, j, 1], to[1])
            msg["nd0", s, j] = send(g.at[s, i[3], 0, j], nd.at[s, j, 0], to[3])

    def relay(j):
        for s in range(3):
            i, to = index[ORDER[s][0]], hop[ORDER[s][0]]
            wait(("fu", s, j))
            fu[s, j] = add16(fu[s, j], g[s, i[1], 0, j])
            msg["nu0", s, j] = send(fu.at[s, j], nu.at[s, j, 0], to[1])
            wait(("fd", s, j))
            fd[s, j] = add16(fd[s, j], g[s, i[3], 1, j])
            msg["nd1", s, j] = send(fd.at[s, j], nd.at[s, j, 1], to[3])

    def finish(j):
        for s in range(3):
            i = index[ORDER[s][0]]
            wait(("nu1", s, j), ("nd0", s, j), ("nu0", s, j), ("nd1", s, j))
            value = add3(g[s, i[0], :, j], nu[s, j], nd[s, j]).reshape(2 * S1, CHUNK)
            for b in range(4):
                r1[s, b, j] = value[S2 * b : S2 * b + S2].astype(BF16)

    def second_stage(q):
        for s in range(3):
            i, to = index[ORDER[s][1]], hop[ORDER[s][1]]
            msg["fu2", s, q] = send(r1.at[s, i[2], 2 * q], fu2.at[s, q], to[1])
            msg["fd2", s, q] = send(r1.at[s, i[2], 2 * q + 1], fd2.at[s, q], to[3])
        for s in range(3):
            i, to = index[ORDER[s][1]], hop[ORDER[s][1]]
            msg["mu1", s, q] = send(r1.at[s, i[1], 2 * q + 1], nu2.at[s, q, 1], to[1])
            msg["md0", s, q] = send(r1.at[s, i[3], 2 * q], nd2.at[s, q, 0], to[3])

    def second_relay(q):
        for s in range(3):
            i, to = index[ORDER[s][1]], hop[ORDER[s][1]]
            wait(("fu2", s, q))
            fu2[s, q] = add16(fu2[s, q], r1[s, i[1], 2 * q])
            msg["mu0", s, q] = send(fu2.at[s, q], nu2.at[s, q, 0], to[1])
            wait(("fd2", s, q))
            fd2[s, q] = add16(fd2[s, q], r1[s, i[3], 2 * q + 1])
            msg["md1", s, q] = send(fd2.at[s, q], nd2.at[s, q, 1], to[3])

    def third_stage(q):
        for s in range(3):
            i = index[ORDER[s][1]]
            wait(("mu1", s, q), ("md0", s, q), ("mu0", s, q), ("md1", s, q))
            for k in range(2):
                value = add3(r1[s, i[0], 2 * q + k], nu2[s, q, k], nd2[s, q, k])
                for c in range(4):
                    r2[s, c, q, k] = value[S3 * c : S3 * c + S3].astype(BF16)
            i, to = index[ORDER[s][2]], hop[ORDER[s][2]]
            for d in (2, 1, 3):
                msg["last", s, q, d] = send(r2.at[s, i[d], q], r3.at[s, d, q], to[d])

    def owned(q):
        for s in range(3):
            i = index[ORDER[s][2]]
            wait(*(("last", s, q, d) for d in (1, 2, 3)))
            for k in range(2):
                total = r2[s, i[0], q, k].astype(F32)
                for d in (1, 2, 3):
                    total = total + r3[s, d, q, k].astype(F32)
                base = (2 * q + k) * CHUNK
                out_grad[S3 * s : S3 * s + S3, base : base + CHUNK] = total

    forward(0)
    pooled_twin.wait_recv()
    pt[...] = lax.dot_general(
        sel[...], pb[...], (((1,), (1,)), ((), ())), preferred_element_type=F32
    ).astype(BF16)
    backward(0)
    forward(1)
    forward(2)
    backward(1)
    relay(0)
    forward(3)
    backward(2)
    relay(1)
    backward(3)
    relay(2)
    finish(0)
    relay(3)
    finish(1)
    second_stage(0)
    give(0)
    finish(2)
    second_relay(0)
    finish(3)
    second_stage(1)
    give(1)
    third_stage(0)
    give(2)
    second_relay(1)
    give(3)
    settle()
    third_stage(1)
    owned(0)
    owned(1)
    settle()


def hand_over(projected, weight_grad, out_projected, out_grad, sem):
    copies = [pltpu.make_async_copy(weight_grad, out_grad, sem.at[9])]
    for i in range(9):
        rows = pl.ds(9 * i, 9)
        copies.append(pltpu.make_async_copy(projected.at[rows], out_projected.at[rows], sem.at[i]))
    for copy in copies:
        copy.start()
    for copy in copies:
        copy.wait()


N_LOCAL = 4 + 4 + 4
N_SEND = 160


def per_device(features, shot_ids, band_width, proj_weight, cotangent):
    frames = jnp.swapaxes(features, 1, 2).reshape(2, TOKS * POOL, D)
    cot = cotangent.transpose(1, 2, 0, 3).reshape(TOKS, 2, H)
    vm = lambda *shape: pltpu.VMEM(shape, BF16)
    scratch = [
        vm(2, TOKS * POOL, D), vm(4, D, CHUNK), vm(4, TOKS, 2, CHUNK), vm(4, PADDED, CHUNK),
        vm(4, PADDED, CHUNK),
        pltpu.VMEM((PADDED, CHUNK), F32), vm(256, 256), vm(4, 2, ROWS, D), vm(576, D),
        vm(2 * PADDED, D), vm(576, 2 * PADDED), vm(4, 2 * PADDED, CHUNK),
        vm(4, ROWS, XL), vm(ROWS, XL // 2), vm(ROWS, XL // 2), vm(ROWS, XL), vm(ROWS, XL),
        vm(ROWS, YL), vm(ROWS, YL), vm(2, ROWS, YL), vm(2, ROWS, YL), vm(ROWS, YL), vm(ROWS, YL),
        vm(3, 4, 2, 4, S1, CHUNK),
        vm(3, 4, S1, CHUNK), vm(3, 4, S1, CHUNK), vm(3, 4, 2, S1, CHUNK), vm(3, 4, 2, S1, CHUNK),
        vm(3, 4, 4, S2, CHUNK), vm(3, 2, S2, CHUNK), vm(3, 2, S2, CHUNK),
        vm(3, 2, 2, S2, CHUNK), vm(3, 2, 2, S2, CHUNK),
        vm(3, 4, 2, 2, S3, CHUNK), vm(3, 4, 2, 2, S3, CHUNK),
        pltpu.VMEM(shot_ids.shape, jnp.int32), pltpu.SMEM(band_width.shape, jnp.int32),
        pltpu.SemaphoreType.DMA((N_LOCAL,)),
        pltpu.SemaphoreType.DMA((N_SEND,)),
        pltpu.SemaphoreType.DMA((N_SEND,)),
    ]
    any_spec = pl.BlockSpec(memory_space=pl.ANY)
    vmem_spec = pl.BlockSpec(memory_space=pltpu.VMEM)
    inputs = [
        pltpu.with_memory_space_constraint(a, pltpu.HBM)
        for a in (frames, proj_weight, cot, shot_ids, band_width)
    ]
    projected, weight_grad = pl.pallas_call(
        kernel,
        out_shape=(
            pltpu.VMEM(cot.shape, BF16),
            pltpu.VMEM((9, H), F32),
        ),
        in_specs=[any_spec] * 5,
        out_specs=(vmem_spec, vmem_spec),
        scratch_shapes=scratch,
        compiler_params=pltpu.CompilerParams(
            collective_id=0, has_side_effects=True, vmem_limit_bytes=50 * 1024 * 1024
        ),
        cost_estimate=pl.CostEstimate(flops=4 * 10**9, bytes_accessed=14 * 10**6, transcendentals=600000),
    )(*inputs)
    projected, weight_grad = pl.pallas_call(
        hand_over,
        out_shape=(
            jax.ShapeDtypeStruct(projected.shape, BF16),
            jax.ShapeDtypeStruct(weight_grad.shape, F32),
        ),
        in_specs=[vmem_spec, vmem_spec],
        out_specs=(any_spec, any_spec),
        scratch_shapes=[pltpu.SemaphoreType.DMA((10,))],
    )(*(pltpu.with_memory_space_constraint(a, pltpu.VMEM) for a in (projected, weight_grad)))
    return projected.reshape(1, TOKS, 2, H).transpose(2, 0, 1, 3), weight_grad


def solution(mesh):
    return jax.shard_map(
        per_device,
        mesh=mesh,
        in_specs=(
            P("dp", "tm", None, None),
            P("dp", None),
            P("dp", None),
            P(),
            P("dp", "tm", None, None),
        ),
        out_specs=(P("dp", "tm", None, None), P(("dp", "tm"), None)),
        check_vma=False,
    )
```

```python
import jax
import jax.numpy as jnp
from jax import lax
from jax.experimental import pallas as pl
from jax.experimental.pallas import tpu as pltpu
from jax.sharding import PartitionSpec as P

BLOCK = 64
POOL = 8
DECAY = 16.0
F32, BF16 = jnp.float32, jnp.bfloat16
MESH = pl.DeviceIdType.MESH

D, H, TOKS = 1152, 3584, 81
ROWS = 2 * TOKS
PADDED = 176
XL = 512
YL = D - XL
CHUNK = H // 4
ORDER = (("z", "y", "x"), ("y", "x", "z"), ("x", "z", "y"))
S1, S2, S3 = 24, 12, 3
C0 = 0.7978845608028654
C1 = 0.044715


def add16(a, b):
    return (a.astype(F32) + b.astype(F32)).astype(BF16)


class Place:
    def __init__(self, local_sem, send_sem, recv_sem):
        dp, tm = lax.axis_index("dp"), lax.axis_index("tm")
        self.core = lax.rem(dp, 2)
        self.lo = lax.rem(tm, 2)
        self.z, self.y = lax.div(tm, 8), lax.rem(lax.div(tm, 2), 4)
        self.x = lax.div(dp, 2) * 2 + self.lo
        here = {"x": self.x, "y": self.y, "z": self.z}
        self.index = {a: [lax.rem(here[a] + d, 4) for d in range(4)] for a in "xyz"}
        self.hop = {a: [self.dev(**{a: self.index[a][d]}) for d in range(4)] for a in "xyz"}
        self.mate = self.dev(x=self.x + 1 - 2 * self.lo)
        self.twin = self.dev(core=1 - self.core)
        self.sems = local_sem, send_sem, recv_sem
        self.count = [0, 0]
        self.sends = []

    def dev(self, x=None, y=None, z=None, core=None):
        x, y, z, core = (
            mine if other is None else other
            for other, mine in ((x, self.x), (y, self.y), (z, self.z), (core, self.core))
        )
        return (lax.div(x, 2) * 2 + core, z * 8 + y * 2 + lax.rem(x, 2))

    def greet(self, friends):
        barrier = pltpu.get_barrier_semaphore()
        for friend in friends:
            pl.semaphore_signal(barrier, inc=1, device_id=friend, device_id_type=MESH)
        return lambda: pl.semaphore_wait(barrier, len(friends))

    def local(self, src, dst):
        i = self.count[0]
        self.count[0] += 1
        copy = pltpu.make_async_copy(src, dst, self.sems[0].at[i])
        copy.start()
        return copy

    def send(self, src, dst, to):
        i = self.count[1]
        self.count[1] += 1
        copy = pltpu.make_async_remote_copy(
            src_ref=src, dst_ref=dst, send_sem=self.sems[1].at[i], recv_sem=self.sems[2].at[i],
            device_id=to, device_id_type=MESH,
        )
        copy.start()
        self.sends.append(copy)
        return copy

    def settle(self):
        for copy in self.sends:
            copy.wait_send()
        self.sends.clear()


def iota(shape, axis):
    return lax.broadcasted_iota(jnp.int32, shape, axis)


def pool_kernel(
    feat, wgt, cot, shots_in, band_in,
    pb, wv, cv, sel,
    fv, cn, kron, part,
    xa, xfu, xfd, xnu, xnd, yfu, yfd, ynu, ynd, sb, yx,
    ids_v, band_s,
    local_sem, send_sem, recv_sem,
):
    here = Place(local_sem, send_sem, recv_sem)
    core, x, y, z, lo = here.core, here.x, here.y, here.z, here.lo
    hop, local, send = here.hop, here.local, here.send
    la, lb = pl.ds(0, XL), pl.ds(XL, YL)
    ids_in = local(shots_in, ids_v)
    width_in = local(band_in, band_s)
    feat_a = local(feat.at[:, :, la], fv.at[:, :, la])
    feat_b = local(feat.at[:, :, lb], fv.at[:, :, lb])

    everybody = here.greet([hop["y"][1], hop["y"][3], here.mate])

    frame, other = iota((BLOCK, 128), 0), iota((BLOCK, 128), 1)
    distance = jnp.abs(frame - other)
    decay = jnp.exp(-distance.astype(F32) / DECAY)
    ids_in.wait()
    width_in.wait()
    ids = ids_v[...].astype(F32)
    ids = jnp.where(z < 2, ids[:, 0:128], ids[:, 128:256])
    ids = jnp.where(lax.rem(z, 2) == 0, ids, pltpu.roll(ids, 64, 1))
    target_of = iota((256, 128), 0)
    rel = lax.div(target_of, 32)
    target_of = lax.rem(y + lax.div(rel, 2), 4) * 2 + jnp.where(lax.rem(rel, 2) == 0, lo, 1 - lo)
    own_frame = jnp.where(iota((128, 256), 0) == (y * 2 + lo) * POOL + lax.rem(iota((128, 256), 1), 8), 1.0, 0.0)
    own_frame = own_frame.astype(BF16)
    out_row, in_row = iota((256, 256), 0), iota((256, 256), 1)
    same_token = lax.div(lax.rem(out_row, 32), 2) == lax.div(lax.rem(in_row, 128), 8)
    spread = jnp.zeros((256, 256), F32)
    for v in range(2):
        along = jnp.broadcast_to(ids[v : v + 1], (BLOCK, 128))
        down_ids = jnp.sum(jnp.where(frame == other, along, 0.0), axis=1, keepdims=True)
        allowed = (along == down_ids) & (distance <= band_s[v, z]) & (other < BLOCK)
        raw = jnp.where(allowed, decay, 0.0)
        mix = (raw / jnp.sum(raw, axis=1, keepdims=True)).astype(BF16).astype(F32)
        combined = (mix.reshape(8, POOL, 128).sum(axis=1) * 0.125).astype(BF16).astype(F32)
        rows = jnp.zeros((256, 128), F32)
        for p in range(8):
            rows = jnp.where(target_of == p, combined[p : p + 1], rows)
        full = jnp.dot(rows.astype(BF16), own_frame, preferred_element_type=F32)
        mine_too = same_token & (lax.rem(out_row, 2) == v) & (lax.div(in_row, 128) == v)
        spread = jnp.where(mine_too, full, spread)
    kron[...] = spread.astype(BF16)

    def partial_sums(lanes):
        for c in range(6):
            if c < 5:
                blocks = [fv[v, 128 * c : 128 * c + 128, lanes] for v in range(2)]
            else:
                empty = jnp.zeros((120, lanes.stop - lanes.start), BF16)
                blocks = [b for v in range(2) for b in (fv[v, 640:648, lanes], empty)]
            got = jnp.dot(kron[...], jnp.concatenate(blocks, axis=0), preferred_element_type=F32)
            size = 32 if c < 5 else 2
            for r in range(8):
                part[r // 2, r % 2, 32 * c : 32 * c + size, lanes] = got[32 * r : 32 * r + size].astype(BF16)

    l1, l2 = pl.ds(0, XL // 2), pl.ds(XL // 2, XL // 2)
    up, down, side = hop["y"][1], hop["y"][3], here.mate

    feat_a.wait()
    partial_sums(slice(0, XL))
    everybody()
    x_first = {dy: send(part.at[dy, 1, :, la], xa.at[dy], side) for dy in (2, 1, 3, 0)}
    feat_b.wait()
    partial_sums(slice(XL, D))
    far_up = send(part.at[2, 0, :, lb], yfu, up)
    far_down = send(part.at[2, 1, :, lb], yfd, down)
    near_up = {1: send(part.at[1, 1, :, lb], ynu.at[1], up)}
    near_down = {0: send(part.at[3, 0, :, lb], ynd.at[0], down)}

    columns = [pl.ds(j * CHUNK, CHUNK) for j in range(4)]
    cot_in = [local(cot.at[:, :, columns[j]], cn.at[j]) for j in range(4)]
    wgt_in = [local(wgt.at[:, columns[j]], wv.at[j]) for j in range(4)]

    row, lane = iota((576, 128), 0), iota((576, 128), 1)
    which = lax.div(row, 192)
    first, second, third = lax.div(lax.rem(row, 192), 48), lax.div(lax.rem(row, 48), 12), lax.div(lax.rem(row, 12), 3)
    at = {}
    for axis in "xyz":
        at[axis] = jnp.zeros((576, 128), jnp.int32)
        for s in range(3):
            place = (first, second, third)[ORDER[s].index(axis)]
            at[axis] = jnp.where(which == s, place, at[axis])
    owner = (lax.div(at["x"], 2) * 2 + core) * 32 + at["z"] * 8 + at["y"] * 2 + lax.rem(at["x"], 2)
    wanted = owner * 9 + which * S3 + lax.rem(row, S3)
    for k in range(D // 128):
        sel[:, 128 * k : 128 * k + 128] = jnp.where(wanted == lane + 128 * k, 1.0, 0.0).astype(BF16)

    def take(dy):
        x_first[dy].wait_recv()
        xa[dy] = add16(xa[dy], part[dy, 0, :, 0:XL])

    take(2)
    far_up2 = send(xa.at[2, :, l1], xfu, up)
    far_up.wait_recv()
    yfu[...] = add16(yfu[...], part[1, 0, :, XL:D])
    near_up[0] = send(yfu, ynu.at[0], up)
    far_down.wait_recv()
    yfd[...] = add16(yfd[...], part[3, 1, :, XL:D])
    near_down[1] = send(yfd, ynd.at[1], down)
    far_down2 = send(xa.at[2, :, l2], xfd, down)
    take(1)
    near_up2 = [send(xa.at[1, :, l2], xnu.at[:, l2], up)]
    take(3)
    near_down2 = [send(xa.at[3, :, l1], xnd.at[:, l1], down)]

    for j in range(4):
        cot_in[j].wait()

        @pl.loop(0, 10)
        def _(i):
            cv[j, pl.ds(pl.multiple_of(i * 16, 16), 16), :] = cn[j, pl.ds(i * 8, 8)].reshape(16, CHUNK)

        tail = jnp.concatenate([cn[j, 80].astype(F32), jnp.zeros((14, CHUNK), F32)], axis=0)
        cv[j, 160:176, :] = tail.astype(BF16)

    far_up2.wait_recv()
    xfu[...] = add16(xfu[...], xa[1, :, 0 : XL // 2])
    near_up2.append(send(xfu, xnu.at[:, l1], up))
    near_up[1].wait_recv()
    near_down[1].wait_recv()
    sb[...] = (
        part[0, 1, :, XL:D].astype(F32) + ynu[1].astype(F32) + ynd[1].astype(F32)
    ).astype(BF16)
    last_x = send(sb, yx, side)
    far_down2.wait_recv()
    xfd[...] = add16(xfd[...], xa[3, :, XL // 2 : XL])
    near_down2.append(send(xfd, xnd.at[:, l2], down))

    def keep(value, lanes):
        value = value.astype(BF16)
        pb[0:160, lanes] = value[0:160]
        tail = jnp.concatenate(
            [value[160:162].astype(F32), jnp.zeros((14, value.shape[1]), F32)], axis=0
        )
        pb[160:176, lanes] = tail.astype(BF16)

    take(0)
    for copy in near_up2 + near_down2:
        copy.wait_recv()
    keep(xa[0].astype(F32) + xnu[...].astype(F32) + xnd[...].astype(F32), slice(0, XL))
    near_up[0].wait_recv()
    near_down[0].wait_recv()
    last_x.wait_recv()
    keep(
        part[0, 0, :, XL:D].astype(F32) + ynu[0].astype(F32) + ynd[0].astype(F32) + yx[...].astype(F32),
        slice(XL, D),
    )
    for copy in wgt_in:
        copy.wait()
    here.settle()


def main_kernel(
    pooled, wv, cv, sel,
    out_proj, out_grad,
    pa, pre, pb, pt, gr, g,
    fu, fd, nu, nd, r1, fu2, fd2, nu2, nd2, r2, r3,
    send_sem, recv_sem,
):
    here = Place(None, send_sem, recv_sem)
    index, hop, send, settle, twin = here.index, here.hop, here.send, here.settle, here.twin
    everybody = here.greet([hop[a][d] for a in "xyz" for d in (1, 2, 3)] + [twin])
    pb[0:PADDED, :] = pooled[...]

    grad_twin, pooled_twin = [], []

    def gelu_rows(values, cotangent):
        square = values * values
        t = jnp.tanh(values * (C0 + (C0 * C1) * square))
        plus = 0.5 * (1.0 + t)
        slope = plus + (0.5 * values) * (1.0 - t * t) * (C0 + (3.0 * C0 * C1) * square)
        return (values * plus).astype(BF16), (cotangent * slope).astype(BF16)

    def forward(j):
        pre[...] = jnp.dot(pooled[...], wv[j], preferred_element_type=F32)

        @pl.loop(0, 11)
        def _(i):
            rows = pl.ds(pl.multiple_of(i * 16, 16), 16)
            act, grad = gelu_rows(pre[rows, :], cv[j, rows, :].astype(F32))
            pa[j, rows, :] = act
            gr[j, rows, :] = grad

        if j == 0:
            everybody()
            pooled_twin.append(send(pb.at[pl.ds(0, PADDED)], pb.at[pl.ds(PADDED, PADDED)], twin))
        grad_twin.append(send(gr.at[j, pl.ds(0, PADDED)], gr.at[j, pl.ds(PADDED, PADDED)], twin))

    def give(j):
        @pl.loop(0, 10)
        def _(i):
            rows = pl.ds(pl.multiple_of(i * 16, 16), 16)
            out_proj[pl.ds(i * 8, 8), :, pl.ds(j * CHUNK, CHUNK)] = pa[j, rows, :].reshape(8, 2, CHUNK)

        out_proj[80, :, pl.ds(j * CHUNK, CHUNK)] = pa[j, 160:162, :]

    msg = {}

    def wait(*names):
        for name in names:
            msg[name].wait_recv()

    def add3(a, b, c):
        return a.astype(F32) + b.astype(F32) + c.astype(F32)

    def backward(j):
        grad_twin[j].wait_recv()
        got = jnp.dot(pt[...], gr[j], preferred_element_type=F32)
        for s in range(3):
            for a in range(4):
                for h in range(2):
                    base = s * 192 + a * 48 + h * S1
                    g[s, a, h, j] = got[base : base + S1].astype(BF16)
        for s in range(3):
            i, to = index[ORDER[s][0]], hop[ORDER[s][0]]
            msg["fu", s, j] = send(g.at[s, i[2], 0, j], fu.at[s, j], to[1])
            msg["fd", s, j] = send(g.at[s, i[2], 1, j], fd.at[s, j], to[3])
        for s in range(3):
            i, to = index[ORDER[s][0]], hop[ORDER[s][0]]
            msg["nu1", s, j] = send(g.at[s, i[1], 1, j], nu.at[s, j, 1], to[1])
            msg["nd0", s, j] = send(g.at[s, i[3], 0, j], nd.at[s, j, 0], to[3])

    def relay(j):
        for s in range(3):
            i, to = index[ORDER[s][0]], hop[ORDER[s][0]]
            wait(("fu", s, j))
            fu[s, j] = add16(fu[s, j], g[s, i[1], 0, j])
            msg["nu0", s, j] = send(fu.at[s, j], nu.at[s, j, 0], to[1])
            wait(("fd", s, j))
            fd[s, j] = add16(fd[s, j], g[s, i[3], 1, j])
            msg["nd1", s, j] = send(fd.at[s, j], nd.at[s, j, 1], to[3])

    def finish(j):
        for s in range(3):
            i = index[ORDER[s][0]]
            wait(("nu1", s, j), ("nd0", s, j), ("nu0", s, j), ("nd1", s, j))
            value = add3(g[s, i[0], :, j], nu[s, j], nd[s, j]).reshape(2 * S1, CHUNK)
            for b in range(4):
                r1[s, b, j] = value[S2 * b : S2 * b + S2].astype(BF16)

    def second_stage(q):
        for s in range(3):
            i, to = index[ORDER[s][1]], hop[ORDER[s][1]]
            msg["fu2", s, q] = send(r1.at[s, i[2], 2 * q], fu2.at[s, q], to[1])
            msg["fd2", s, q] = send(r1.at[s, i[2], 2 * q + 1], fd2.at[s, q], to[3])
        for s in range(3):
            i, to = index[ORDER[s][1]], hop[ORDER[s][1]]
            msg["mu1", s, q] = send(r1.at[s, i[1], 2 * q + 1], nu2.at[s, q, 1], to[1])
            msg["md0", s, q] = send(r1.at[s, i[3], 2 * q], nd2.at[s, q, 0], to[3])

    def second_relay(q):
        for s in range(3):
            i, to = index[ORDER[s][1]], hop[ORDER[s][1]]
            wait(("fu2", s, q))
            fu2[s, q] = add16(fu2[s, q], r1[s, i[1], 2 * q])
            msg["mu0", s, q] = send(fu2.at[s, q], nu2.at[s, q, 0], to[1])
            wait(("fd2", s, q))
            fd2[s, q] = add16(fd2[s, q], r1[s, i[3], 2 * q + 1])
            msg["md1", s, q] = send(fd2.at[s, q], nd2.at[s, q, 1], to[3])

    def third_stage(q):
        for s in range(3):
            i = index[ORDER[s][1]]
            wait(("mu1", s, q), ("md0", s, q), ("mu0", s, q), ("md1", s, q))
            for k in range(2):
                value = add3(r1[s, i[0], 2 * q + k], nu2[s, q, k], nd2[s, q, k])
                for c in range(4):
                    r2[s, c, q, k] = value[S3 * c : S3 * c + S3].astype(BF16)
            i, to = index[ORDER[s][2]], hop[ORDER[s][2]]
            for d in (2, 1, 3):
                msg["last", s, q, d] = send(r2.at[s, i[d], q], r3.at[s, d, q], to[d])

    def owned(q):
        for s in range(3):
            i = index[ORDER[s][2]]
            wait(*(("last", s, q, d) for d in (1, 2, 3)))
            for k in range(2):
                total = r2[s, i[0], q, k].astype(F32)
                for d in (1, 2, 3):
                    total = total + r3[s, d, q, k].astype(F32)
                base = (2 * q + k) * CHUNK
                out_grad[S3 * s : S3 * s + S3, base : base + CHUNK] = total

    forward(0)
    pooled_twin[0].wait_recv()
    pt[...] = lax.dot_general(
        sel[...], pb[...], (((1,), (1,)), ((), ())), preferred_element_type=F32
    ).astype(BF16)
    backward(0)
    forward(1)
    forward(2)
    backward(1)
    relay(0)
    forward(3)
    backward(2)
    relay(1)
    backward(3)
    relay(2)
    finish(0)
    relay(3)
    finish(1)
    second_stage(0)
    give(0)
    finish(2)
    second_relay(0)
    finish(3)
    second_stage(1)
    give(1)
    third_stage(0)
    give(2)
    second_relay(1)
    give(3)
    settle()
    third_stage(1)
    owned(0)
    owned(1)
    settle()


def hand_over(projected, weight_grad, out_projected, out_grad, sem):
    copies = [pltpu.make_async_copy(weight_grad, out_grad, sem.at[9])]
    for i in range(9):
        rows = pl.ds(9 * i, 9)
        copies.append(pltpu.make_async_copy(projected.at[rows], out_projected.at[rows], sem.at[i]))
    for copy in copies:
        copy.start()
    for copy in copies:
        copy.wait()


def per_device(features, shot_ids, band_width, proj_weight, cotangent):
    frames = jnp.swapaxes(features, 1, 2).reshape(2, TOKS * POOL, D)
    cot = cotangent.transpose(1, 2, 0, 3).reshape(TOKS, 2, H)
    vm = lambda *shape: pltpu.VMEM(shape, BF16)
    sems = lambda n: pltpu.SemaphoreType.DMA((n,))
    any_spec = pl.BlockSpec(memory_space=pl.ANY)
    vmem_spec = pl.BlockSpec(memory_space=pltpu.VMEM)
    pin = lambda space, *arrays: [pltpu.with_memory_space_constraint(a, space) for a in arrays]
    shared = pl.pallas_call(
        pool_kernel,
        out_shape=(vm(PADDED, D), vm(4, D, CHUNK), vm(4, PADDED, CHUNK), vm(576, D)),
        in_specs=[any_spec] * 5,
        out_specs=(vmem_spec,) * 4,
        scratch_shapes=[
            vm(2, TOKS * POOL, D), vm(4, TOKS, 2, CHUNK), vm(256, 256), vm(4, 2, ROWS, D),
            vm(4, ROWS, XL), vm(ROWS, XL // 2), vm(ROWS, XL // 2), vm(ROWS, XL), vm(ROWS, XL),
            vm(ROWS, YL), vm(ROWS, YL), vm(2, ROWS, YL), vm(2, ROWS, YL), vm(ROWS, YL), vm(ROWS, YL),
            pltpu.VMEM(shot_ids.shape, jnp.int32), pltpu.SMEM(band_width.shape, jnp.int32),
            sems(12), sems(24), sems(24),
        ],
        compiler_params=pltpu.CompilerParams(
            collective_id=0, has_side_effects=True, vmem_limit_bytes=24 * 1024 * 1024
        ),
        cost_estimate=pl.CostEstimate(flops=10**9, bytes_accessed=14 * 10**6, transcendentals=0),
    )(*pin(pltpu.HBM, frames, proj_weight, cot, shot_ids, band_width))
    projected, weight_grad = pl.pallas_call(
        main_kernel,
        out_shape=(pltpu.VMEM(cot.shape, BF16), pltpu.VMEM((9, H), F32)),
        in_specs=[vmem_spec] * 4,
        out_specs=(vmem_spec, vmem_spec),
        scratch_shapes=[
            vm(4, PADDED, CHUNK), pltpu.VMEM((PADDED, CHUNK), F32),
            vm(2 * PADDED, D), vm(576, 2 * PADDED), vm(4, 2 * PADDED, CHUNK),
            vm(3, 4, 2, 4, S1, CHUNK),
            vm(3, 4, S1, CHUNK), vm(3, 4, S1, CHUNK), vm(3, 4, 2, S1, CHUNK), vm(3, 4, 2, S1, CHUNK),
            vm(3, 4, 4, S2, CHUNK), vm(3, 2, S2, CHUNK), vm(3, 2, S2, CHUNK),
            vm(3, 2, 2, S2, CHUNK), vm(3, 2, 2, S2, CHUNK),
            vm(3, 4, 2, 2, S3, CHUNK), vm(3, 4, 2, 2, S3, CHUNK),
            sems(144), sems(144),
        ],
        compiler_params=pltpu.CompilerParams(
            collective_id=1, has_side_effects=True, vmem_limit_bytes=36 * 1024 * 1024
        ),
        cost_estimate=pl.CostEstimate(flops=3 * 10**9, bytes_accessed=10**6, transcendentals=600000),
    )(*pin(pltpu.VMEM, *shared))
    projected, weight_grad = pl.pallas_call(
        hand_over,
        out_shape=(
            jax.ShapeDtypeStruct(projected.shape, BF16),
            jax.ShapeDtypeStruct(weight_grad.shape, F32),
        ),
        in_specs=[vmem_spec, vmem_spec],
        out_specs=(any_spec, any_spec),
        scratch_shapes=[pltpu.SemaphoreType.DMA((10,))],
    )(*pin(pltpu.VMEM, projected, weight_grad))
    return projected.reshape(1, TOKS, 2, H).transpose(2, 0, 1, 3), weight_grad


def solution(mesh):
    return jax.shard_map(
        per_device,
        mesh=mesh,
        in_specs=(
            P("dp", "tm", None, None),
            P("dp", None),
            P("dp", None),
            P(),
            P("dp", "tm", None, None),
        ),
        out_specs=(P("dp", "tm", None, None), P(("dp", "tm"), None)),
        check_vma=False,
    )
```

```python
import jax
import jax.numpy as jnp
from jax import lax
from jax.experimental import pallas as pl
from jax.experimental.pallas import tpu as pltpu
from jax.sharding import PartitionSpec as P

BLOCK = 64
POOL = 8
DECAY = 16.0
F32, BF16 = jnp.float32, jnp.bfloat16
MESH = pl.DeviceIdType.MESH

D, H, TOKS = 1152, 3584, 81
ROWS = 2 * TOKS
PADDED = 176
XL = 512
YL = D - XL
CHUNK = H // 4
ORDER = (("z", "y", "x"), ("y", "x", "z"), ("x", "z", "y"))
SLOTS = ((2, 0), (1, 1), (2, 1), (3, 0), (1, 0), (3, 1), (0, 0), (0, 1))
S1, S2, S3 = 24, 12, 3
C0 = 0.7978845608028654
C1 = 0.044715


def add16(a, b):
    return (a.astype(F32) + b.astype(F32)).astype(BF16)


class Place:
    def __init__(self, local_sem, send_sem, recv_sem):
        dp, tm = lax.axis_index("dp"), lax.axis_index("tm")
        self.core = lax.rem(dp, 2)
        self.lo = lax.rem(tm, 2)
        self.z, self.y = lax.div(tm, 8), lax.rem(lax.div(tm, 2), 4)
        self.x = lax.div(dp, 2) * 2 + self.lo
        here = {"x": self.x, "y": self.y, "z": self.z}
        self.index = {a: [lax.rem(here[a] + d, 4) for d in range(4)] for a in "xyz"}
        self.hop = {a: [self.dev(**{a: self.index[a][d]}) for d in range(4)] for a in "xyz"}
        self.mate = self.dev(x=self.x + 1 - 2 * self.lo)
        self.twin = self.dev(core=1 - self.core)
        self.sems = local_sem, send_sem, recv_sem
        self.count = [0, 0]
        self.sends = []

    def dev(self, x=None, y=None, z=None, core=None):
        x, y, z, core = (
            mine if other is None else other
            for other, mine in ((x, self.x), (y, self.y), (z, self.z), (core, self.core))
        )
        return (lax.div(x, 2) * 2 + core, z * 8 + y * 2 + lax.rem(x, 2))

    def greet(self, friends):
        barrier = pltpu.get_barrier_semaphore()
        for friend in friends:
            pl.semaphore_signal(barrier, inc=1, device_id=friend, device_id_type=MESH)
        return lambda: pl.semaphore_wait(barrier, len(friends))

    def local(self, src, dst):
        i = self.count[0]
        self.count[0] += 1
        copy = pltpu.make_async_copy(src, dst, self.sems[0].at[i])
        copy.start()
        return copy

    def send(self, src, dst, to):
        i = self.count[1]
        self.count[1] += 1
        copy = pltpu.make_async_remote_copy(
            src_ref=src, dst_ref=dst, send_sem=self.sems[1].at[i], recv_sem=self.sems[2].at[i],
            device_id=to, device_id_type=MESH,
        )
        copy.start()
        self.sends.append(copy)
        return copy

    def settle(self):
        for copy in self.sends:
            copy.wait_send()
        self.sends.clear()


def iota(shape, axis):
    return lax.broadcasted_iota(jnp.int32, shape, axis)


def pool_kernel(
    feat, wgt, cot, shots_in, band_in,
    pb, wv, cv, sel,
    fv, cn, kron, part,
    xa, xfu, xfd, xnu, xnd, yfu, yfd, ynu, ynd, sb, yx,
    ids_v, band_s,
    local_sem, send_sem, recv_sem,
):
    here = Place(local_sem, send_sem, recv_sem)
    core, x, y, z, lo = here.core, here.x, here.y, here.z, here.lo
    hop, local, send = here.hop, here.local, here.send
    la, lb = pl.ds(0, XL), pl.ds(XL, YL)
    ids_in = local(shots_in, ids_v)
    width_in = local(band_in, band_s)
    feat_a = local(feat.at[:, :, la], fv.at[:, :, la])
    feat_b = local(feat.at[:, :, lb], fv.at[:, :, lb])

    everybody = here.greet([hop["y"][1], hop["y"][3], here.mate])

    frame, other = iota((BLOCK, 128), 0), iota((BLOCK, 128), 1)
    distance = jnp.abs(frame - other)
    decay = jnp.exp(-distance.astype(F32) / DECAY)
    ids_in.wait()
    width_in.wait()
    ids = ids_v[...].astype(F32)
    ids = jnp.where(z < 2, ids[:, 0:128], ids[:, 128:256])
    ids = jnp.where(lax.rem(z, 2) == 0, ids, pltpu.roll(ids, 64, 1))
    target_of = iota((256, 128), 0)
    rel = lax.div(target_of, 32)
    target_of = lax.rem(y + lax.div(rel, 2), 4) * 2 + jnp.where(lax.rem(rel, 2) == 0, lo, 1 - lo)
    own_frame = jnp.where(iota((128, 256), 0) == (y * 2 + lo) * POOL + lax.rem(iota((128, 256), 1), 8), 1.0, 0.0)
    own_frame = own_frame.astype(BF16)
    out_row, in_row = iota((256, 256), 0), iota((256, 256), 1)
    same_token = lax.div(lax.rem(out_row, 32), 2) == lax.div(lax.rem(in_row, 128), 8)
    spread = jnp.zeros((256, 256), F32)
    for v in range(2):
        along = jnp.broadcast_to(ids[v : v + 1], (BLOCK, 128))
        down_ids = jnp.sum(jnp.where(frame == other, along, 0.0), axis=1, keepdims=True)
        allowed = (along == down_ids) & (distance <= band_s[v, z]) & (other < BLOCK)
        raw = jnp.where(allowed, decay, 0.0)
        mix = (raw / jnp.sum(raw, axis=1, keepdims=True)).astype(BF16).astype(F32)
        combined = (mix.reshape(8, POOL, 128).sum(axis=1) * 0.125).astype(BF16).astype(F32)
        rows = jnp.zeros((256, 128), F32)
        for p in range(8):
            rows = jnp.where(target_of == p, combined[p : p + 1], rows)
        full = jnp.dot(rows.astype(BF16), own_frame, preferred_element_type=F32)
        mine_too = same_token & (lax.rem(out_row, 2) == v) & (lax.div(in_row, 128) == v)
        spread = jnp.where(mine_too, full, spread)
    kron[...] = spread.astype(BF16)

    def partial_sums(lanes):
        for c in range(6):
            if c < 5:
                blocks = [fv[v, 128 * c : 128 * c + 128, lanes] for v in range(2)]
            else:
                empty = jnp.zeros((120, lanes.stop - lanes.start), BF16)
                blocks = [b for v in range(2) for b in (fv[v, 640:648, lanes], empty)]
            got = jnp.dot(kron[...], jnp.concatenate(blocks, axis=0), preferred_element_type=F32)
            size = 32 if c < 5 else 2
            for r in range(8):
                part[r // 2, r % 2, 32 * c : 32 * c + size, lanes] = got[32 * r : 32 * r + size].astype(BF16)

    l1, l2 = pl.ds(0, XL // 2), pl.ds(XL // 2, XL // 2)
    up, down, side = hop["y"][1], hop["y"][3], here.mate

    feat_a.wait()
    partial_sums(slice(0, XL))
    everybody()
    x_first = {dy: send(part.at[dy, 1, :, la], xa.at[dy], side) for dy in (2, 1, 3, 0)}
    feat_b.wait()
    partial_sums(slice(XL, D))
    far_up = send(part.at[2, 0, :, lb], yfu, up)
    far_down = send(part.at[2, 1, :, lb], yfd, down)
    near_up = {1: send(part.at[1, 1, :, lb], ynu.at[1], up)}
    near_down = {0: send(part.at[3, 0, :, lb], ynd.at[0], down)}

    columns = [pl.ds(j * CHUNK, CHUNK) for j in range(4)]
    cot_in = [local(cot.at[:, :, columns[j]], cn.at[j]) for j in range(4)]
    wgt_in = [local(wgt.at[:, columns[j]], wv.at[j]) for j in range(4)]

    row, lane = iota((576, 128), 0), iota((576, 128), 1)
    which, slot = lax.div(row, 192), lax.div(lax.rem(row, 192), S1)
    half, first = jnp.zeros_like(row), jnp.zeros_like(row)
    for p, (d, h) in enumerate(SLOTS):
        first = jnp.where(slot == p, d, first)
        half = jnp.where(slot == p, h, half)
    second = half * 2 + lax.div(lax.rem(row, S1), S2)
    third = lax.div(lax.rem(row, S2), S3)
    at = {}
    for axis, mine in (("x", x), ("y", y), ("z", z)):
        far = jnp.zeros_like(row)
        for s in range(3):
            far = jnp.where(which == s, (first, second, third)[ORDER[s].index(axis)], far)
        at[axis] = lax.rem(far + mine, 4)
    owner = (lax.div(at["x"], 2) * 2 + core) * 32 + at["z"] * 8 + at["y"] * 2 + lax.rem(at["x"], 2)
    wanted = owner * 9 + which * S3 + lax.rem(row, S3)
    for k in range(D // 128):
        sel[:, 128 * k : 128 * k + 128] = jnp.where(wanted == lane + 128 * k, 1.0, 0.0).astype(BF16)

    def take(dy):
        x_first[dy].wait_recv()
        xa[dy] = add16(xa[dy], part[dy, 0, :, 0:XL])

    take(2)
    far_up2 = send(xa.at[2, :, l1], xfu, up)
    far_up.wait_recv()
    yfu[...] = add16(yfu[...], part[1, 0, :, XL:D])
    near_up[0] = send(yfu, ynu.at[0], up)
    far_down.wait_recv()
    yfd[...] = add16(yfd[...], part[3, 1, :, XL:D])
    near_down[1] = send(yfd, ynd.at[1], down)
    far_down2 = send(xa.at[2, :, l2], xfd, down)
    take(1)
    near_up2 = [send(xa.at[1, :, l2], xnu.at[:, l2], up)]
    take(3)
    near_down2 = [send(xa.at[3, :, l1], xnd.at[:, l1], down)]

    for j in range(4):
        cot_in[j].wait()

        @pl.loop(0, 10)
        def _(i):
            cv[j, pl.ds(pl.multiple_of(i * 16, 16), 16), :] = cn[j, pl.ds(i * 8, 8)].reshape(16, CHUNK)

        tail = jnp.concatenate([cn[j, 80].astype(F32), jnp.zeros((14, CHUNK), F32)], axis=0)
        cv[j, 160:176, :] = tail.astype(BF16)

    far_up2.wait_recv()
    xfu[...] = add16(xfu[...], xa[1, :, 0 : XL // 2])
    near_up2.append(send(xfu, xnu.at[:, l1], up))
    near_up[1].wait_recv()
    near_down[1].wait_recv()
    sb[...] = (
        part[0, 1, :, XL:D].astype(F32) + ynu[1].astype(F32) + ynd[1].astype(F32)
    ).astype(BF16)
    last_x = send(sb, yx, side)
    far_down2.wait_recv()
    xfd[...] = add16(xfd[...], xa[3, :, XL // 2 : XL])
    near_down2.append(send(xfd, xnd.at[:, l2], down))

    def keep(value, lanes):
        value = value.astype(BF16)
        pb[0:160, lanes] = value[0:160]
        tail = jnp.concatenate(
            [value[160:162].astype(F32), jnp.zeros((14, value.shape[1]), F32)], axis=0
        )
        pb[160:176, lanes] = tail.astype(BF16)

    take(0)
    for copy in near_up2 + near_down2:
        copy.wait_recv()
    keep(xa[0].astype(F32) + xnu[...].astype(F32) + xnd[...].astype(F32), slice(0, XL))
    near_up[0].wait_recv()
    near_down[0].wait_recv()
    last_x.wait_recv()
    keep(
        part[0, 0, :, XL:D].astype(F32) + ynu[0].astype(F32) + ynd[0].astype(F32) + yx[...].astype(F32),
        slice(XL, D),
    )
    for copy in wgt_in:
        copy.wait()
    here.settle()


def main_kernel(
    pooled, wv, cv, sel,
    out_proj, out_grad,
    pa, pre, pb, pt, gr, g,
    ru, rd, nu, nd, r1, ru2, rd2, nu2, nd2, r2, r3,
    send_sem, recv_sem,
):
    here = Place(None, send_sem, recv_sem)
    hop, send, settle, twin = here.hop, here.send, here.settle, here.twin
    everybody = here.greet([hop[a][d] for a in "xyz" for d in (1, 2, 3)] + [twin])
    pb[0:PADDED, :] = pooled[...]

    grad_twin, pooled_twin = [], []

    def gelu_rows(values, cotangent):
        square = values * values
        t = jnp.tanh(values * (C0 + (C0 * C1) * square))
        plus = 0.5 * (1.0 + t)
        slope = plus + (0.5 * values) * (1.0 - t * t) * (C0 + (3.0 * C0 * C1) * square)
        return (values * plus).astype(BF16), (cotangent * slope).astype(BF16)

    def forward(j):
        pre[...] = jnp.dot(pooled[...], wv[j], preferred_element_type=F32)

        @pl.loop(0, 11)
        def _(i):
            rows = pl.ds(pl.multiple_of(i * 16, 16), 16)
            act, grad = gelu_rows(pre[rows, :], cv[j, rows, :].astype(F32))
            pa[j, rows, :] = act
            gr[j, rows, :] = grad

        if j == 0:
            everybody()
            pooled_twin.append(send(pb.at[pl.ds(0, PADDED)], pb.at[pl.ds(PADDED, PADDED)], twin))
        grad_twin.append(send(gr.at[j, pl.ds(0, PADDED)], gr.at[j, pl.ds(PADDED, PADDED)], twin))

    def give(j):
        @pl.loop(0, 10)
        def _(i):
            rows = pl.ds(pl.multiple_of(i * 16, 16), 16)
            out_proj[pl.ds(i * 8, 8), :, pl.ds(j * CHUNK, CHUNK)] = pa[j, rows, :].reshape(8, 2, CHUNK)

        out_proj[80, :, pl.ds(j * CHUNK, CHUNK)] = pa[j, 160:162, :]

    msg = {}

    def wait(*names):
        for name in names:
            msg[name].wait_recv()

    def add3(a, b, c):
        return a.astype(F32) + b.astype(F32) + c.astype(F32)

    def backward(j):
        grad_twin[j].wait_recv()
        got = jnp.dot(pt[...], gr[j], preferred_element_type=F32)
        for s in range(3):
            for p in range(8):
                base = s * 192 + p * S1
                g[s, j, p] = got[base : base + S1].astype(BF16)
        for s in range(3):
            to = hop[ORDER[s][0]]
            msg["ru", s, j] = send(g.at[s, j, pl.ds(0, 2)], ru.at[s, j], to[1])
            msg["rd", s, j] = send(g.at[s, j, pl.ds(2, 2)], rd.at[s, j], to[3])

    def relay(j):
        for s in range(3):
            to = hop[ORDER[s][0]]
            wait(("ru", s, j))
            ru[s, j, 0] = add16(ru[s, j, 0], g[s, j, 4])
            msg["nu", s, j] = send(ru.at[s, j, 0], nu.at[s, j], to[1])
            wait(("rd", s, j))
            rd[s, j, 0] = add16(rd[s, j, 0], g[s, j, 5])
            msg["nd", s, j] = send(rd.at[s, j, 0], nd.at[s, j], to[3])

    def finish(j):
        q, k = j // 2, j % 2
        for s in range(3):
            wait(("nu", s, j), ("nd", s, j))
            for h, value in enumerate(
                (add3(g[s, j, 6], nu[s, j], rd[s, j, 1]), add3(g[s, j, 7], ru[s, j, 1], nd[s, j]))
            ):
                for b in range(2):
                    slot = SLOTS.index((2 * h + b, k))
                    r1[s, q, slot] = value[S2 * b : S2 * b + S2].astype(BF16)

    def second_stage(q):
        for s in range(3):
            to = hop[ORDER[s][1]]
            msg["ru2", s, q] = send(r1.at[s, q, pl.ds(0, 2)], ru2.at[s, q], to[1])
            msg["rd2", s, q] = send(r1.at[s, q, pl.ds(2, 2)], rd2.at[s, q], to[3])

    def second_relay(q):
        for s in range(3):
            to = hop[ORDER[s][1]]
            wait(("ru2", s, q))
            ru2[s, q, 0] = add16(ru2[s, q, 0], r1[s, q, 4])
            msg["nu2", s, q] = send(ru2.at[s, q, 0], nu2.at[s, q], to[1])
            wait(("rd2", s, q))
            rd2[s, q, 0] = add16(rd2[s, q, 0], r1[s, q, 5])
            msg["nd2", s, q] = send(rd2.at[s, q, 0], nd2.at[s, q], to[3])

    def second_finish(q):
        for s in range(3):
            wait(("nu2", s, q), ("nd2", s, q))
            for k, value in enumerate(
                (add3(r1[s, q, 6], nu2[s, q], rd2[s, q, 1]), add3(r1[s, q, 7], ru2[s, q, 1], nd2[s, q]))
            ):
                for c in range(4):
                    r2[s, c, 2 * q + k] = value[S3 * c : S3 * c + S3].astype(BF16)

    def third_stage():
        for s in range(3):
            to = hop[ORDER[s][2]]
            for d in (2, 1, 3):
                msg["last", s, d] = send(r2.at[s, d], r3.at[s, d], to[d])

    def owned():
        for s in range(3):
            wait(*(("last", s, d) for d in (1, 2, 3)))
            for j in range(4):
                total = r2[s, 0, j].astype(F32)
                for d in (1, 2, 3):
                    total = total + r3[s, d, j].astype(F32)
                out_grad[S3 * s : S3 * s + S3, j * CHUNK : j * CHUNK + CHUNK] = total

    forward(0)
    pooled_twin[0].wait_recv()
    pt[...] = lax.dot_general(
        sel[...], pb[...], (((1,), (1,)), ((), ())), preferred_element_type=F32
    ).astype(BF16)
    backward(0)
    forward(1)
    forward(2)
    backward(1)
    relay(0)
    forward(3)
    backward(2)
    relay(1)
    backward(3)
    relay(2)
    finish(0)
    finish(1)
    second_stage(0)
    relay(3)
    give(0)
    finish(2)
    second_relay(0)
    finish(3)
    second_stage(1)
    give(1)
    second_finish(0)
    give(2)
    second_relay(1)
    give(3)
    settle()
    second_finish(1)
    third_stage()
    owned()
    settle()


def hand_over(projected, weight_grad, out_projected, out_grad, sem):
    copies = [pltpu.make_async_copy(weight_grad, out_grad, sem.at[9])]
    for i in range(9):
        rows = pl.ds(9 * i, 9)
        copies.append(pltpu.make_async_copy(projected.at[rows], out_projected.at[rows], sem.at[i]))
    for copy in copies:
        copy.start()
    for copy in copies:
        copy.wait()


def per_device(features, shot_ids, band_width, proj_weight, cotangent):
    frames = jnp.swapaxes(features, 1, 2).reshape(2, TOKS * POOL, D)
    cot = cotangent.transpose(1, 2, 0, 3).reshape(TOKS, 2, H)
    vm = lambda *shape: pltpu.VMEM(shape, BF16)
    sems = lambda n: pltpu.SemaphoreType.DMA((n,))
    any_spec = pl.BlockSpec(memory_space=pl.ANY)
    vmem_spec = pl.BlockSpec(memory_space=pltpu.VMEM)
    pin = lambda space, *arrays: [pltpu.with_memory_space_constraint(a, space) for a in arrays]
    shared = pl.pallas_call(
        pool_kernel,
        out_shape=(vm(PADDED, D), vm(4, D, CHUNK), vm(4, PADDED, CHUNK), vm(576, D)),
        in_specs=[any_spec] * 5,
        out_specs=(vmem_spec,) * 4,
        scratch_shapes=[
            vm(2, TOKS * POOL, D), vm(4, TOKS, 2, CHUNK), vm(256, 256), vm(4, 2, ROWS, D),
            vm(4, ROWS, XL), vm(ROWS, XL // 2), vm(ROWS, XL // 2), vm(ROWS, XL), vm(ROWS, XL),
            vm(ROWS, YL), vm(ROWS, YL), vm(2, ROWS, YL), vm(2, ROWS, YL), vm(ROWS, YL), vm(ROWS, YL),
            pltpu.VMEM(shot_ids.shape, jnp.int32), pltpu.SMEM(band_width.shape, jnp.int32),
            sems(12), sems(24), sems(24),
        ],
        compiler_params=pltpu.CompilerParams(
            collective_id=0, has_side_effects=True, vmem_limit_bytes=24 * 1024 * 1024
        ),
        cost_estimate=pl.CostEstimate(flops=10**9, bytes_accessed=14 * 10**6, transcendentals=0),
    )(*pin(pltpu.HBM, frames, proj_weight, cot, shot_ids, band_width))
    projected, weight_grad = pl.pallas_call(
        main_kernel,
        out_shape=(pltpu.VMEM(cot.shape, BF16), pltpu.VMEM((9, H), F32)),
        in_specs=[vmem_spec] * 4,
        out_specs=(vmem_spec, vmem_spec),
        scratch_shapes=[
            vm(4, PADDED, CHUNK), pltpu.VMEM((PADDED, CHUNK), F32),
            vm(2 * PADDED, D), vm(576, 2 * PADDED), vm(4, 2 * PADDED, CHUNK),
            vm(3, 4, 8, S1, CHUNK),
            vm(3, 4, 2, S1, CHUNK), vm(3, 4, 2, S1, CHUNK), vm(3, 4, S1, CHUNK), vm(3, 4, S1, CHUNK),
            vm(3, 2, 8, S2, CHUNK), vm(3, 2, 2, S2, CHUNK), vm(3, 2, 2, S2, CHUNK),
            vm(3, 2, S2, CHUNK), vm(3, 2, S2, CHUNK),
            vm(3, 4, 4, S3, CHUNK), vm(3, 4, 4, S3, CHUNK),
            sems(88), sems(88),
        ],
        compiler_params=pltpu.CompilerParams(
            collective_id=1, has_side_effects=True, vmem_limit_bytes=36 * 1024 * 1024
        ),
        cost_estimate=pl.CostEstimate(flops=3 * 10**9, bytes_accessed=10**6, transcendentals=600000),
    )(*pin(pltpu.VMEM, *shared))
    projected, weight_grad = pl.pallas_call(
        hand_over,
        out_shape=(
            jax.ShapeDtypeStruct(projected.shape, BF16),
            jax.ShapeDtypeStruct(weight_grad.shape, F32),
        ),
        in_specs=[vmem_spec, vmem_spec],
        out_specs=(any_spec, any_spec),
        scratch_shapes=[pltpu.SemaphoreType.DMA((10,))],
    )(*pin(pltpu.VMEM, projected, weight_grad))
    return projected.reshape(1, TOKS, 2, H).transpose(2, 0, 1, 3), weight_grad


def solution(mesh):
    return jax.shard_map(
        per_device,
        mesh=mesh,
        in_specs=(
            P("dp", "tm", None, None),
            P("dp", None),
            P("dp", None),
            P(),
            P("dp", "tm", None, None),
        ),
        out_specs=(P("dp", "tm", None, None), P(("dp", "tm"), None)),
        check_vma=False,
    )
```

```python
import jax
import jax.numpy as jnp
from jax import lax
from jax.experimental import pallas as pl
from jax.experimental.pallas import tpu as pltpu
from jax.sharding import PartitionSpec as P

BLOCK = 64
POOL = 8
DECAY = 16.0
F32, BF16 = jnp.float32, jnp.bfloat16
MESH = pl.DeviceIdType.MESH

D, H, TOKS = 1152, 3584, 81
ROWS = 2 * TOKS
PADDED = 176
XL = 512
YL = D - XL
CHUNK = 512
STEPS = H // CHUNK
HALF = CHUNK // 2
GROUPS = ((0, 3), (3, 6), (6, 7))
ORDER = (("z", "y", "x"), ("y", "x", "z"), ("x", "z", "y"))
SLOTS = ((2, 0), (1, 1), (2, 1), (3, 0), (1, 0), (3, 1), (0, 0), (0, 1))
S1, S2, S3 = 24, 12, 3
C0 = 0.7978845608028654
C1 = 0.044715


def add16(a, b):
    return (a.astype(F32) + b.astype(F32)).astype(BF16)


class Place:
    def __init__(self, local_sem, send_sem, recv_sem):
        dp, tm = lax.axis_index("dp"), lax.axis_index("tm")
        self.core = lax.rem(dp, 2)
        self.lo = lax.rem(tm, 2)
        self.z, self.y = lax.div(tm, 8), lax.rem(lax.div(tm, 2), 4)
        self.x = lax.div(dp, 2) * 2 + self.lo
        here = {"x": self.x, "y": self.y, "z": self.z}
        self.index = {a: [lax.rem(here[a] + d, 4) for d in range(4)] for a in "xyz"}
        self.hop = {a: [self.dev(**{a: self.index[a][d]}) for d in range(4)] for a in "xyz"}
        self.mate = self.dev(x=self.x + 1 - 2 * self.lo)
        self.twin = self.dev(core=1 - self.core)
        self.sems = local_sem, send_sem, recv_sem
        self.count = [0, 0]
        self.sends = []

    def dev(self, x=None, y=None, z=None, core=None):
        x, y, z, core = (
            mine if other is None else other
            for other, mine in ((x, self.x), (y, self.y), (z, self.z), (core, self.core))
        )
        return (lax.div(x, 2) * 2 + core, z * 8 + y * 2 + lax.rem(x, 2))

    def greet(self, friends):
        barrier = pltpu.get_barrier_semaphore()
        for friend in friends:
            pl.semaphore_signal(barrier, inc=1, device_id=friend, device_id_type=MESH)
        return lambda: pl.semaphore_wait(barrier, len(friends))

    def local(self, src, dst):
        i = self.count[0]
        self.count[0] += 1
        copy = pltpu.make_async_copy(src, dst, self.sems[0].at[i])
        copy.start()
        return copy

    def send(self, src, dst, to):
        i = self.count[1]
        self.count[1] += 1
        copy = pltpu.make_async_remote_copy(
            src_ref=src, dst_ref=dst, send_sem=self.sems[1].at[i], recv_sem=self.sems[2].at[i],
            device_id=to, device_id_type=MESH,
        )
        copy.start()
        self.sends.append(copy)
        return copy

    def settle(self):
        for copy in self.sends:
            copy.wait_send()
        self.sends.clear()


def iota(shape, axis):
    return lax.broadcasted_iota(jnp.int32, shape, axis)


def pool_kernel(
    feat, wgt, cot, shots_in, band_in,
    pb, wv, cv, sel,
    fv, cn, kron, part,
    xa, xfu, xfd, xnu, xnd, yfu, yfd, ynu, ynd, sb, yx,
    ids_v, band_s,
    local_sem, send_sem, recv_sem,
):
    here = Place(local_sem, send_sem, recv_sem)
    core, x, y, z, lo = here.core, here.x, here.y, here.z, here.lo
    hop, local, send = here.hop, here.local, here.send
    la, lb = pl.ds(0, XL), pl.ds(XL, YL)
    ids_in = local(shots_in, ids_v)
    width_in = local(band_in, band_s)
    feat_a = local(feat.at[:, :, la], fv.at[:, :, la])
    feat_b = local(feat.at[:, :, lb], fv.at[:, :, lb])

    everybody = here.greet([hop["y"][1], hop["y"][3], here.mate])

    frame, other = iota((BLOCK, 128), 0), iota((BLOCK, 128), 1)
    distance = jnp.abs(frame - other)
    decay = jnp.exp(-distance.astype(F32) / DECAY)
    ids_in.wait()
    width_in.wait()
    ids = ids_v[...].astype(F32)
    ids = jnp.where(z < 2, ids[:, 0:128], ids[:, 128:256])
    ids = jnp.where(lax.rem(z, 2) == 0, ids, pltpu.roll(ids, 64, 1))
    target_of = iota((256, 128), 0)
    rel = lax.div(target_of, 32)
    target_of = lax.rem(y + lax.div(rel, 2), 4) * 2 + jnp.where(lax.rem(rel, 2) == 0, lo, 1 - lo)
    own_frame = jnp.where(iota((128, 256), 0) == (y * 2 + lo) * POOL + lax.rem(iota((128, 256), 1), 8), 1.0, 0.0)
    own_frame = own_frame.astype(BF16)
    out_row, in_row = iota((256, 256), 0), iota((256, 256), 1)
    same_token = lax.div(lax.rem(out_row, 32), 2) == lax.div(lax.rem(in_row, 128), 8)
    spread = jnp.zeros((256, 256), F32)
    for v in range(2):
        along = jnp.broadcast_to(ids[v : v + 1], (BLOCK, 128))
        down_ids = jnp.sum(jnp.where(frame == other, along, 0.0), axis=1, keepdims=True)
        allowed = (along == down_ids) & (distance <= band_s[v, z]) & (other < BLOCK)
        raw = jnp.where(allowed, decay, 0.0)
        mix = (raw / jnp.sum(raw, axis=1, keepdims=True)).astype(BF16).astype(F32)
        combined = (mix.reshape(8, POOL, 128).sum(axis=1) * 0.125).astype(BF16).astype(F32)
        rows = jnp.zeros((256, 128), F32)
        for p in range(8):
            rows = jnp.where(target_of == p, combined[p : p + 1], rows)
        full = jnp.dot(rows.astype(BF16), own_frame, preferred_element_type=F32)
        mine_too = same_token & (lax.rem(out_row, 2) == v) & (lax.div(in_row, 128) == v)
        spread = jnp.where(mine_too, full, spread)
    kron[...] = spread.astype(BF16)

    def partial_sums(lanes):
        for c in range(6):
            if c < 5:
                blocks = [fv[v, 128 * c : 128 * c + 128, lanes] for v in range(2)]
            else:
                empty = jnp.zeros((120, lanes.stop - lanes.start), BF16)
                blocks = [b for v in range(2) for b in (fv[v, 640:648, lanes], empty)]
            got = jnp.dot(kron[...], jnp.concatenate(blocks, axis=0), preferred_element_type=F32)
            size = 32 if c < 5 else 2
            for r in range(8):
                part[r // 2, r % 2, 32 * c : 32 * c + size, lanes] = got[32 * r : 32 * r + size].astype(BF16)

    l1, l2 = pl.ds(0, XL // 2), pl.ds(XL // 2, XL // 2)
    up, down, side = hop["y"][1], hop["y"][3], here.mate

    feat_a.wait()
    partial_sums(slice(0, XL))
    everybody()
    x_first = {dy: send(part.at[dy, 1, :, la], xa.at[dy], side) for dy in (2, 1, 3, 0)}
    feat_b.wait()
    partial_sums(slice(XL, D))
    far_up = send(part.at[2, 0, :, lb], yfu, up)
    far_down = send(part.at[2, 1, :, lb], yfd, down)
    near_up = {1: send(part.at[1, 1, :, lb], ynu.at[1], up)}
    near_down = {0: send(part.at[3, 0, :, lb], ynd.at[0], down)}

    columns = [pl.ds(j * CHUNK, CHUNK) for j in range(STEPS)]
    cot_in = [local(cot.at[:, :, columns[j]], cn.at[j]) for j in range(STEPS)]
    wgt_in = [local(wgt.at[:, columns[j]], wv.at[j]) for j in range(STEPS)]

    row, lane = iota((576, 128), 0), iota((576, 128), 1)
    which, slot = lax.div(row, 192), lax.div(lax.rem(row, 192), S1)
    half, first = jnp.zeros_like(row), jnp.zeros_like(row)
    for p, (d, h) in enumerate(SLOTS):
        first = jnp.where(slot == p, d, first)
        half = jnp.where(slot == p, h, half)
    second = half * 2 + lax.div(lax.rem(row, S1), S2)
    third = lax.div(lax.rem(row, S2), S3)
    at = {}
    for axis, mine in (("x", x), ("y", y), ("z", z)):
        far = jnp.zeros_like(row)
        for s in range(3):
            far = jnp.where(which == s, (first, second, third)[ORDER[s].index(axis)], far)
        at[axis] = lax.rem(far + mine, 4)
    owner = (lax.div(at["x"], 2) * 2 + core) * 32 + at["z"] * 8 + at["y"] * 2 + lax.rem(at["x"], 2)
    wanted = owner * 9 + which * S3 + lax.rem(row, S3)
    for k in range(D // 128):
        sel[:, 128 * k : 128 * k + 128] = jnp.where(wanted == lane + 128 * k, 1.0, 0.0).astype(BF16)

    def take(dy):
        x_first[dy].wait_recv()
        xa[dy] = add16(xa[dy], part[dy, 0, :, 0:XL])

    take(2)
    far_up2 = send(xa.at[2, :, l1], xfu, up)
    far_up.wait_recv()
    yfu[...] = add16(yfu[...], part[1, 0, :, XL:D])
    near_up[0] = send(yfu, ynu.at[0], up)
    far_down.wait_recv()
    yfd[...] = add16(yfd[...], part[3, 1, :, XL:D])
    near_down[1] = send(yfd, ynd.at[1], down)
    far_down2 = send(xa.at[2, :, l2], xfd, down)
    take(1)
    near_up2 = [send(xa.at[1, :, l2], xnu.at[:, l2], up)]
    take(3)
    near_down2 = [send(xa.at[3, :, l1], xnd.at[:, l1], down)]

    for j in range(STEPS):
        cot_in[j].wait()

        @pl.loop(0, 10)
        def _(i):
            cv[j, pl.ds(pl.multiple_of(i * 16, 16), 16), :] = cn[j, pl.ds(i * 8, 8)].reshape(16, CHUNK)

        tail = jnp.concatenate([cn[j, 80].astype(F32), jnp.zeros((14, CHUNK), F32)], axis=0)
        cv[j, 160:176, :] = tail.astype(BF16)

    far_up2.wait_recv()
    xfu[...] = add16(xfu[...], xa[1, :, 0 : XL // 2])
    near_up2.append(send(xfu, xnu.at[:, l1], up))
    near_up[1].wait_recv()
    near_down[1].wait_recv()
    sb[...] = (
        part[0, 1, :, XL:D].astype(F32) + ynu[1].astype(F32) + ynd[1].astype(F32)
    ).astype(BF16)
    last_x = send(sb, yx, side)
    far_down2.wait_recv()
    xfd[...] = add16(xfd[...], xa[3, :, XL // 2 : XL])
    near_down2.append(send(xfd, xnd.at[:, l2], down))

    def keep(value, lanes):
        value = value.astype(BF16)
        pb[0:160, lanes] = value[0:160]
        tail = jnp.concatenate(
            [value[160:162].astype(F32), jnp.zeros((14, value.shape[1]), F32)], axis=0
        )
        pb[160:176, lanes] = tail.astype(BF16)

    take(0)
    for copy in near_up2 + near_down2:
        copy.wait_recv()
    keep(xa[0].astype(F32) + xnu[...].astype(F32) + xnd[...].astype(F32), slice(0, XL))
    near_up[0].wait_recv()
    near_down[0].wait_recv()
    last_x.wait_recv()
    keep(
        part[0, 0, :, XL:D].astype(F32) + ynu[0].astype(F32) + ynd[0].astype(F32) + yx[...].astype(F32),
        slice(XL, D),
    )
    for copy in wgt_in:
        copy.wait()
    here.settle()


def main_kernel(
    pooled, wv, cv, sel,
    out_proj, out_grad,
    pa, pre, pb, pt, gr, g,
    ru, rd, nu, nd, r1, ru2, rd2, nu2, nd2, r2, r3,
    send_sem, recv_sem,
):
    here = Place(None, send_sem, recv_sem)
    hop, send, settle, twin = here.hop, here.send, here.settle, here.twin
    everybody = here.greet([hop[a][d] for a in "xyz" for d in (1, 2, 3)] + [twin])
    pb[0:PADDED, :] = pooled[...]

    grad_twin, pooled_twin = [], []

    def gelu_rows(values, cotangent):
        square = values * values
        t = jnp.tanh(values * (C0 + (C0 * C1) * square))
        plus = 0.5 * (1.0 + t)
        slope = plus + (0.5 * values) * (1.0 - t * t) * (C0 + (3.0 * C0 * C1) * square)
        return (values * plus).astype(BF16), (cotangent * slope).astype(BF16)

    def forward(j):
        pre[...] = jnp.dot(pooled[...], wv[j], preferred_element_type=F32)

        @pl.loop(0, 11)
        def _(i):
            rows = pl.ds(pl.multiple_of(i * 16, 16), 16)
            act, grad = gelu_rows(pre[rows, :], cv[j, rows, :].astype(F32))
            pa[j, rows, :] = act
            gr[j, rows, :] = grad

        if j == 0:
            everybody()
            pooled_twin.append(send(pb.at[pl.ds(0, PADDED)], pb.at[pl.ds(PADDED, PADDED)], twin))
        grad_twin.append(send(gr.at[j, pl.ds(0, PADDED)], gr.at[j, pl.ds(PADDED, PADDED)], twin))

    def give(j):
        @pl.loop(0, 10)
        def _(i):
            rows = pl.ds(pl.multiple_of(i * 16, 16), 16)
            out_proj[pl.ds(i * 8, 8), :, pl.ds(j * CHUNK, CHUNK)] = pa[j, rows, :].reshape(8, 2, CHUNK)

        out_proj[80, :, pl.ds(j * CHUNK, CHUNK)] = pa[j, 160:162, :]

    msg = {}

    def wait(*names):
        for name in names:
            msg[name].wait_recv()

    def add3(a, b, c):
        return a.astype(F32) + b.astype(F32) + c.astype(F32)

    def backward(j):
        grad_twin[j].wait_recv()
        got = jnp.dot(pt[...], gr[j], preferred_element_type=F32)
        for s in range(3):
            for p in range(8):
                base = s * 192 + p * S1
                g[s, j, p] = got[base : base + S1].astype(BF16)
        for s in range(3):
            to = hop[ORDER[s][0]]
            msg["ru", s, j] = send(g.at[s, j, pl.ds(0, 2)], ru.at[s, j], to[1])
            msg["rd", s, j] = send(g.at[s, j, pl.ds(2, 2)], rd.at[s, j], to[3])

    def relay(j):
        for s in range(3):
            to = hop[ORDER[s][0]]
            wait(("ru", s, j))
            ru[s, j, 0] = add16(ru[s, j, 0], g[s, j, 4])
            msg["nu", s, j] = send(ru.at[s, j, 0], nu.at[s, j], to[1])
            wait(("rd", s, j))
            rd[s, j, 0] = add16(rd[s, j, 0], g[s, j, 5])
            msg["nd", s, j] = send(rd.at[s, j, 0], nd.at[s, j], to[3])

    def finish(j):
        for s in range(3):
            wait(("nu", s, j), ("nd", s, j))
            for h, value in enumerate(
                (add3(g[s, j, 6], nu[s, j], rd[s, j, 1]), add3(g[s, j, 7], ru[s, j, 1], nd[s, j]))
            ):
                for b in range(2):
                    rows = value[S2 * b : S2 * b + S2].astype(BF16)
                    for k in range(2):
                        r1[s, SLOTS.index((2 * h + b, k)), j] = rows[:, HALF * k : HALF * k + HALF]

    def second_stage(q):
        steps = pl.ds(GROUPS[q][0], GROUPS[q][1] - GROUPS[q][0])
        for s in range(3):
            to = hop[ORDER[s][1]]
            msg["ru2", s, q] = send(r1.at[s, pl.ds(0, 2), steps], ru2.at[s, :, steps], to[1])
            msg["rd2", s, q] = send(r1.at[s, pl.ds(2, 2), steps], rd2.at[s, :, steps], to[3])

    def second_relay(q):
        steps = pl.ds(GROUPS[q][0], GROUPS[q][1] - GROUPS[q][0])
        for s in range(3):
            to = hop[ORDER[s][1]]
            wait(("ru2", s, q))
            ru2[s, 0, steps] = add16(ru2[s, 0, steps], r1[s, 4, steps])
            msg["nu2", s, q] = send(ru2.at[s, 0, steps], nu2.at[s, steps], to[1])
            wait(("rd2", s, q))
            rd2[s, 0, steps] = add16(rd2[s, 0, steps], r1[s, 5, steps])
            msg["nd2", s, q] = send(rd2.at[s, 0, steps], nd2.at[s, steps], to[3])

    def second_finish(q):
        for s in range(3):
            wait(("nu2", s, q), ("nd2", s, q))
            for j in range(*GROUPS[q]):
                for k, value in enumerate(
                    (add3(r1[s, 6, j], nu2[s, j], rd2[s, 1, j]), add3(r1[s, 7, j], ru2[s, 1, j], nd2[s, j]))
                ):
                    for c in range(4):
                        r2[s, c, j, :, HALF * k : HALF * k + HALF] = value[S3 * c : S3 * c + S3].astype(BF16)

    def third_stage():
        for s in range(3):
            to = hop[ORDER[s][2]]
            for d in (2, 1, 3):
                msg["last", s, d] = send(r2.at[s, d], r3.at[s, d], to[d])

    def owned():
        for s in range(3):
            wait(*(("last", s, d) for d in (1, 2, 3)))
            for j in range(STEPS):
                total = r2[s, 0, j].astype(F32)
                for d in (1, 2, 3):
                    total = total + r3[s, d, j].astype(F32)
                out_grad[S3 * s : S3 * s + S3, j * CHUNK : j * CHUNK + CHUNK] = total

    forward(0)
    pooled_twin[0].wait_recv()
    pt[...] = lax.dot_general(
        sel[...], pb[...], (((1,), (1,)), ((), ())), preferred_element_type=F32
    ).astype(BF16)
    backward(0)
    forward(1)
    forward(2)
    backward(1)
    relay(0)
    forward(3)
    backward(2)
    relay(1)
    forward(4)
    backward(3)
    relay(2)
    finish(0)
    forward(5)
    backward(4)
    relay(3)
    finish(1)
    forward(6)
    backward(5)
    relay(4)
    finish(2)
    second_stage(0)
    backward(6)
    relay(5)
    finish(3)
    second_relay(0)
    finish(4)
    relay(6)
    give(0)
    give(1)
    finish(5)
    second_stage(1)
    second_finish(0)
    finish(6)
    second_stage(2)
    give(2)
    second_relay(1)
    give(3)
    second_relay(2)
    second_finish(1)
    give(4)
    settle()
    second_finish(2)
    third_stage()
    give(5)
    give(6)
    owned()
    settle()


def hand_over(projected, weight_grad, out_projected, out_grad, sem):
    copies = [pltpu.make_async_copy(weight_grad, out_grad, sem.at[9])]
    for i in range(9):
        rows = pl.ds(9 * i, 9)
        copies.append(pltpu.make_async_copy(projected.at[rows], out_projected.at[rows], sem.at[i]))
    for copy in copies:
        copy.start()
    for copy in copies:
        copy.wait()


def per_device(features, shot_ids, band_width, proj_weight, cotangent):
    frames = jnp.swapaxes(features, 1, 2).reshape(2, TOKS * POOL, D)
    cot = cotangent.transpose(1, 2, 0, 3).reshape(TOKS, 2, H)
    vm = lambda *shape: pltpu.VMEM(shape, BF16)
    sems = lambda n: pltpu.SemaphoreType.DMA((n,))
    any_spec = pl.BlockSpec(memory_space=pl.ANY)
    vmem_spec = pl.BlockSpec(memory_space=pltpu.VMEM)
    pin = lambda space, *arrays: [pltpu.with_memory_space_constraint(a, space) for a in arrays]
    shared = pl.pallas_call(
        pool_kernel,
        out_shape=(vm(PADDED, D), vm(STEPS, D, CHUNK), vm(STEPS, PADDED, CHUNK), vm(576, D)),
        in_specs=[any_spec] * 5,
        out_specs=(vmem_spec,) * 4,
        scratch_shapes=[
            vm(2, TOKS * POOL, D), vm(STEPS, TOKS, 2, CHUNK), vm(256, 256), vm(4, 2, ROWS, D),
            vm(4, ROWS, XL), vm(ROWS, XL // 2), vm(ROWS, XL // 2), vm(ROWS, XL), vm(ROWS, XL),
            vm(ROWS, YL), vm(ROWS, YL), vm(2, ROWS, YL), vm(2, ROWS, YL), vm(ROWS, YL), vm(ROWS, YL),
            pltpu.VMEM(shot_ids.shape, jnp.int32), pltpu.SMEM(band_width.shape, jnp.int32),
            sems(4 + 2 * STEPS), sems(24), sems(24),
        ],
        compiler_params=pltpu.CompilerParams(
            collective_id=0, has_side_effects=True, vmem_limit_bytes=24 * 1024 * 1024
        ),
        cost_estimate=pl.CostEstimate(flops=10**9, bytes_accessed=14 * 10**6, transcendentals=0),
    )(*pin(pltpu.HBM, frames, proj_weight, cot, shot_ids, band_width))
    projected, weight_grad = pl.pallas_call(
        main_kernel,
        out_shape=(pltpu.VMEM(cot.shape, BF16), pltpu.VMEM((9, H), F32)),
        in_specs=[vmem_spec] * 4,
        out_specs=(vmem_spec, vmem_spec),
        scratch_shapes=[
            vm(STEPS, PADDED, CHUNK), pltpu.VMEM((PADDED, CHUNK), F32),
            vm(2 * PADDED, D), vm(576, 2 * PADDED), vm(STEPS, 2 * PADDED, CHUNK),
            vm(3, STEPS, 8, S1, CHUNK),
            vm(3, STEPS, 2, S1, CHUNK), vm(3, STEPS, 2, S1, CHUNK),
            vm(3, STEPS, S1, CHUNK), vm(3, STEPS, S1, CHUNK),
            vm(3, 8, STEPS, S2, HALF), vm(3, 2, STEPS, S2, HALF), vm(3, 2, STEPS, S2, HALF),
            vm(3, STEPS, S2, HALF), vm(3, STEPS, S2, HALF),
            vm(3, 4, STEPS, S3, CHUNK), vm(3, 4, STEPS, S3, CHUNK),
            sems(144), sems(144),
        ],
        compiler_params=pltpu.CompilerParams(
            collective_id=1, has_side_effects=True, vmem_limit_bytes=36 * 1024 * 1024
        ),
        cost_estimate=pl.CostEstimate(flops=3 * 10**9, bytes_accessed=10**6, transcendentals=600000),
    )(*pin(pltpu.VMEM, *shared))
    projected, weight_grad = pl.pallas_call(
        hand_over,
        out_shape=(
            jax.ShapeDtypeStruct(projected.shape, BF16),
            jax.ShapeDtypeStruct(weight_grad.shape, F32),
        ),
        in_specs=[vmem_spec, vmem_spec],
        out_specs=(any_spec, any_spec),
        scratch_shapes=[pltpu.SemaphoreType.DMA((10,))],
    )(*pin(pltpu.VMEM, projected, weight_grad))
    return projected.reshape(1, TOKS, 2, H).transpose(2, 0, 1, 3), weight_grad


def solution(mesh):
    return jax.shard_map(
        per_device,
        mesh=mesh,
        in_specs=(
            P("dp", "tm", None, None),
            P("dp", None),
            P("dp", None),
            P(),
            P("dp", "tm", None, None),
        ),
        out_specs=(P("dp", "tm", None, None), P(("dp", "tm"), None)),
        check_vma=False,
    )
```

```python
import jax
import jax.numpy as jnp
from jax import lax
from jax.experimental import pallas as pl
from jax.experimental.pallas import tpu as pltpu
from jax.sharding import PartitionSpec as P

BLOCK = 64
POOL = 8
DECAY = 16.0
F32, BF16 = jnp.float32, jnp.bfloat16
MESH = pl.DeviceIdType.MESH

D, H, TOKS = 1152, 3584, 81
ROWS = 2 * TOKS
PADDED = 176
XL = 512
YL = D - XL
CHUNK = H // 4
ORDER = (("z", "y", "x"), ("y", "x", "z"), ("x", "z", "y"))
SLOTS = ((2, 0), (1, 1), (2, 1), (3, 0), (1, 0), (3, 1), (0, 0), (0, 1))
S1, S2, S3 = 24, 12, 3
C0 = 0.7978845608028654
C1 = 0.044715


def add16(a, b):
    return (a.astype(F32) + b.astype(F32)).astype(BF16)


class Place:
    def __init__(self, local_sem, send_sem, recv_sem):
        dp, tm = lax.axis_index("dp"), lax.axis_index("tm")
        self.core = lax.rem(dp, 2)
        self.lo = lax.rem(tm, 2)
        self.z, self.y = lax.div(tm, 8), lax.rem(lax.div(tm, 2), 4)
        self.x = lax.div(dp, 2) * 2 + self.lo
        here = {"x": self.x, "y": self.y, "z": self.z}
        self.index = {a: [lax.rem(here[a] + d, 4) for d in range(4)] for a in "xyz"}
        self.hop = {a: [self.dev(**{a: self.index[a][d]}) for d in range(4)] for a in "xyz"}
        self.mate = self.dev(x=self.x + 1 - 2 * self.lo)
        self.twin = self.dev(core=1 - self.core)
        self.sems = local_sem, send_sem, recv_sem
        self.count = [0, 0]
        self.sends = []

    def dev(self, x=None, y=None, z=None, core=None):
        x, y, z, core = (
            mine if other is None else other
            for other, mine in ((x, self.x), (y, self.y), (z, self.z), (core, self.core))
        )
        return (lax.div(x, 2) * 2 + core, z * 8 + y * 2 + lax.rem(x, 2))

    def greet(self, friends):
        barrier = pltpu.get_barrier_semaphore()
        for friend in friends:
            pl.semaphore_signal(barrier, inc=1, device_id=friend, device_id_type=MESH)
        return lambda: pl.semaphore_wait(barrier, len(friends))

    def local(self, src, dst):
        i = self.count[0]
        self.count[0] += 1
        copy = pltpu.make_async_copy(src, dst, self.sems[0].at[i])
        copy.start()
        return copy

    def send(self, src, dst, to):
        i = self.count[1]
        self.count[1] += 1
        copy = pltpu.make_async_remote_copy(
            src_ref=src, dst_ref=dst, send_sem=self.sems[1].at[i], recv_sem=self.sems[2].at[i],
            device_id=to, device_id_type=MESH,
        )
        copy.start()
        self.sends.append(copy)
        return copy

    def settle(self):
        for copy in self.sends:
            copy.wait_send()
        self.sends.clear()


def iota(shape, axis):
    return lax.broadcasted_iota(jnp.int32, shape, axis)


def pool_kernel(
    feat, wgt, cot, shots_in, band_in,
    pb, wv, cv, sel,
    fv, cn, kron, part,
    xa, xfu, xfd, xnu, xnd, yfu, yfd, ynu, ynd, sb, yx,
    ids_v, band_s,
    local_sem, send_sem, recv_sem,
):
    here = Place(local_sem, send_sem, recv_sem)
    core, x, y, z, lo = here.core, here.x, here.y, here.z, here.lo
    hop, local, send = here.hop, here.local, here.send
    la, lb = pl.ds(0, XL), pl.ds(XL, YL)
    ids_in = local(shots_in, ids_v)
    width_in = local(band_in, band_s)
    feat_a = local(feat.at[:, :, la], fv.at[:, :, la])
    feat_b = local(feat.at[:, :, lb], fv.at[:, :, lb])

    everybody = here.greet([hop["y"][1], hop["y"][3], here.mate])

    frame, other = iota((BLOCK, 128), 0), iota((BLOCK, 128), 1)
    distance = jnp.abs(frame - other)
    decay = jnp.exp(-distance.astype(F32) / DECAY)
    ids_in.wait()
    width_in.wait()
    ids = ids_v[...].astype(F32)
    ids = jnp.where(z < 2, ids[:, 0:128], ids[:, 128:256])
    ids = jnp.where(lax.rem(z, 2) == 0, ids, pltpu.roll(ids, 64, 1))
    target_of = iota((256, 128), 0)
    rel = lax.div(target_of, 32)
    target_of = lax.rem(y + lax.div(rel, 2), 4) * 2 + jnp.where(lax.rem(rel, 2) == 0, lo, 1 - lo)
    own_frame = jnp.where(iota((128, 256), 0) == (y * 2 + lo) * POOL + lax.rem(iota((128, 256), 1), 8), 1.0, 0.0)
    own_frame = own_frame.astype(BF16)
    out_row, in_row = iota((256, 256), 0), iota((256, 256), 1)
    same_token = lax.div(lax.rem(out_row, 32), 2) == lax.div(lax.rem(in_row, 128), 8)
    spread = jnp.zeros((256, 256), F32)
    for v in range(2):
        along = jnp.broadcast_to(ids[v : v + 1], (BLOCK, 128))
        down_ids = jnp.sum(jnp.where(frame == other, along, 0.0), axis=1, keepdims=True)
        allowed = (along == down_ids) & (distance <= band_s[v, z]) & (other < BLOCK)
        raw = jnp.where(allowed, decay, 0.0)
        mix = (raw / jnp.sum(raw, axis=1, keepdims=True)).astype(BF16).astype(F32)
        combined = (mix.reshape(8, POOL, 128).sum(axis=1) * 0.125).astype(BF16).astype(F32)
        rows = jnp.zeros((256, 128), F32)
        for p in range(8):
            rows = jnp.where(target_of == p, combined[p : p + 1], rows)
        full = jnp.dot(rows.astype(BF16), own_frame, preferred_element_type=F32)
        mine_too = same_token & (lax.rem(out_row, 2) == v) & (lax.div(in_row, 128) == v)
        spread = jnp.where(mine_too, full, spread)
    kron[...] = spread.astype(BF16)

    def partial_sums(lanes):
        for c in range(6):
            if c < 5:
                blocks = [fv[v, 128 * c : 128 * c + 128, lanes] for v in range(2)]
            else:
                empty = jnp.zeros((120, lanes.stop - lanes.start), BF16)
                blocks = [b for v in range(2) for b in (fv[v, 640:648, lanes], empty)]
            got = jnp.dot(kron[...], jnp.concatenate(blocks, axis=0), preferred_element_type=F32)
            size = 32 if c < 5 else 2
            for r in range(8):
                part[r // 2, r % 2, 32 * c : 32 * c + size, lanes] = got[32 * r : 32 * r + size].astype(BF16)

    l1, l2 = pl.ds(0, XL // 2), pl.ds(XL // 2, XL // 2)
    up, down, side = hop["y"][1], hop["y"][3], here.mate

    feat_a.wait()
    partial_sums(slice(0, XL))
    everybody()
    x_first = {dy: send(part.at[dy, 1, :, la], xa.at[dy], side) for dy in (2, 1, 3, 0)}
    feat_b.wait()
    partial_sums(slice(XL, D))
    far_up = send(part.at[2, 0, :, lb], yfu, up)
    far_down = send(part.at[2, 1, :, lb], yfd, down)
    near_up = {1: send(part.at[1, 1, :, lb], ynu.at[1], up)}
    near_down = {0: send(part.at[3, 0, :, lb], ynd.at[0], down)}

    columns = [pl.ds(j * CHUNK, CHUNK) for j in range(4)]
    cot_in = [local(cot.at[:, :, columns[j]], cn.at[j]) for j in range(4)]
    wgt_in = [local(wgt.at[:, columns[j]], wv.at[j]) for j in range(4)]

    row, lane = iota((576, 128), 0), iota((576, 128), 1)
    which, slot = lax.div(row, 192), lax.div(lax.rem(row, 192), S1)
    half, first = jnp.zeros_like(row), jnp.zeros_like(row)
    for p, (d, h) in enumerate(SLOTS):
        first = jnp.where(slot == p, d, first)
        half = jnp.where(slot == p, h, half)
    second = half * 2 + lax.div(lax.rem(row, S1), S2)
    third = lax.div(lax.rem(row, S2), S3)
    at = {}
    for axis, mine in (("x", x), ("y", y), ("z", z)):
        far = jnp.zeros_like(row)
        for s in range(3):
            far = jnp.where(which == s, (first, second, third)[ORDER[s].index(axis)], far)
        at[axis] = lax.rem(far + mine, 4)
    owner = (lax.div(at["x"], 2) * 2 + core) * 32 + at["z"] * 8 + at["y"] * 2 + lax.rem(at["x"], 2)
    wanted = owner * 9 + which * S3 + lax.rem(row, S3)
    for k in range(D // 128):
        sel[:, 128 * k : 128 * k + 128] = jnp.where(wanted == lane + 128 * k, 1.0, 0.0).astype(BF16)

    def take(dy):
        x_first[dy].wait_recv()
        xa[dy] = add16(xa[dy], part[dy, 0, :, 0:XL])

    take(2)
    far_up2 = send(xa.at[2, :, l1], xfu, up)
    far_up.wait_recv()
    yfu[...] = add16(yfu[...], part[1, 0, :, XL:D])
    near_up[0] = send(yfu, ynu.at[0], up)
    far_down.wait_recv()
    yfd[...] = add16(yfd[...], part[3, 1, :, XL:D])
    near_down[1] = send(yfd, ynd.at[1], down)
    far_down2 = send(xa.at[2, :, l2], xfd, down)
    take(1)
    near_up2 = [send(xa.at[1, :, l2], xnu.at[:, l2], up)]
    take(3)
    near_down2 = [send(xa.at[3, :, l1], xnd.at[:, l1], down)]

    for j in range(4):
        cot_in[j].wait()

        @pl.loop(0, 10)
        def _(i):
            cv[j, pl.ds(pl.multiple_of(i * 16, 16), 16), :] = cn[j, pl.ds(i * 8, 8)].reshape(16, CHUNK)

        tail = jnp.concatenate([cn[j, 80].astype(F32), jnp.zeros((14, CHUNK), F32)], axis=0)
        cv[j, 160:176, :] = tail.astype(BF16)

    far_up2.wait_recv()
    xfu[...] = add16(xfu[...], xa[1, :, 0 : XL // 2])
    near_up2.append(send(xfu, xnu.at[:, l1], up))
    near_up[1].wait_recv()
    near_down[1].wait_recv()
    sb[...] = (
        part[0, 1, :, XL:D].astype(F32) + ynu[1].astype(F32) + ynd[1].astype(F32)
    ).astype(BF16)
    last_x = send(sb, yx, side)
    far_down2.wait_recv()
    xfd[...] = add16(xfd[...], xa[3, :, XL // 2 : XL])
    near_down2.append(send(xfd, xnd.at[:, l2], down))

    def keep(value, lanes):
        value = value.astype(BF16)
        pb[0:160, lanes] = value[0:160]
        tail = jnp.concatenate(
            [value[160:162].astype(F32), jnp.zeros((14, value.shape[1]), F32)], axis=0
        )
        pb[160:176, lanes] = tail.astype(BF16)

    take(0)
    for copy in near_up2 + near_down2:
        copy.wait_recv()
    keep(xa[0].astype(F32) + xnu[...].astype(F32) + xnd[...].astype(F32), slice(0, XL))
    near_up[0].wait_recv()
    near_down[0].wait_recv()
    last_x.wait_recv()
    keep(
        part[0, 0, :, XL:D].astype(F32) + ynu[0].astype(F32) + ynd[0].astype(F32) + yx[...].astype(F32),
        slice(XL, D),
    )
    for copy in wgt_in:
        copy.wait()
    here.settle()


def main_kernel(
    pooled, wv, cv, sel,
    out_proj, out_grad,
    pa, pre, pb, pt, gr, g,
    ru, rd, nu, nd, r1, ru2, rd2, nu2, nd2, r2, r3,
    send_sem, recv_sem,
):
    here = Place(None, send_sem, recv_sem)
    hop, send, settle, twin = here.hop, here.send, here.settle, here.twin
    everybody = here.greet([hop[a][d] for a in "xyz" for d in (1, 2, 3)] + [twin])
    pb[0:PADDED, :] = pooled[...]

    grad_twin = []

    def gelu_rows(values, cotangent):
        square = values * values
        t = jnp.tanh(values * (C0 + (C0 * C1) * square))
        plus = 0.5 * (1.0 + t)
        slope = plus + (0.5 * values) * (1.0 - t * t) * (C0 + (3.0 * C0 * C1) * square)
        return (values * plus).astype(BF16), (cotangent * slope).astype(BF16)

    def product(j):
        pre[j % 2] = jnp.dot(pooled[...], wv[j], preferred_element_type=F32)

    def forward(j):
        for i in range(11):
            rows = slice(16 * i, 16 * i + 16)
            act, grad = gelu_rows(pre[j % 2, rows, :], cv[j, rows, :].astype(F32))
            pa[j, rows, :] = act
            gr[j, rows, :] = grad
        grad_twin.append(send(gr.at[j, pl.ds(0, PADDED)], gr.at[j, pl.ds(PADDED, PADDED)], twin))

    def give(j):
        for i in range(10):
            out_proj[8 * i : 8 * i + 8, :, CHUNK * j : CHUNK * j + CHUNK] = (
                pa[j, 16 * i : 16 * i + 16, :].reshape(8, 2, CHUNK)
            )
        out_proj[80, :, CHUNK * j : CHUNK * j + CHUNK] = pa[j, 160:162, :]

    msg = {}

    def wait(*names):
        for name in names:
            msg[name].wait_recv()

    def add3(a, b, c):
        return a.astype(F32) + b.astype(F32) + c.astype(F32)

    def backward(j):
        grad_twin[j].wait_recv()
        got = jnp.dot(pt[...], gr[j], preferred_element_type=F32)
        for s in range(3):
            for p in range(8):
                base = s * 192 + p * S1
                g[s, j, p] = got[base : base + S1].astype(BF16)
        for s in range(3):
            to = hop[ORDER[s][0]]
            msg["ru", s, j] = send(g.at[s, j, pl.ds(0, 2)], ru.at[s, j], to[1])
            msg["rd", s, j] = send(g.at[s, j, pl.ds(2, 2)], rd.at[s, j], to[3])

    def relay(j):
        for s in range(3):
            to = hop[ORDER[s][0]]
            wait(("ru", s, j))
            ru[s, j, 0] = add16(ru[s, j, 0], g[s, j, 4])
            msg["nu", s, j] = send(ru.at[s, j, 0], nu.at[s, j], to[1])
            wait(("rd", s, j))
            rd[s, j, 0] = add16(rd[s, j, 0], g[s, j, 5])
            msg["nd", s, j] = send(rd.at[s, j, 0], nd.at[s, j], to[3])

    def finish(j):
        q, k = j // 2, j % 2
        for s in range(3):
            wait(("nu", s, j), ("nd", s, j))
            for h, value in enumerate(
                (add3(g[s, j, 6], nu[s, j], rd[s, j, 1]), add3(g[s, j, 7], ru[s, j, 1], nd[s, j]))
            ):
                for b in range(2):
                    slot = SLOTS.index((2 * h + b, k))
                    r1[s, q, slot] = value[S2 * b : S2 * b + S2].astype(BF16)

    def second_stage(q):
        for s in range(3):
            to = hop[ORDER[s][1]]
            msg["ru2", s, q] = send(r1.at[s, q, pl.ds(0, 2)], ru2.at[s, q], to[1])
            msg["rd2", s, q] = send(r1.at[s, q, pl.ds(2, 2)], rd2.at[s, q], to[3])

    def second_relay(q):
        for s in range(3):
            to = hop[ORDER[s][1]]
            wait(("ru2", s, q))
            ru2[s, q, 0] = add16(ru2[s, q, 0], r1[s, q, 4])
            msg["nu2", s, q] = send(ru2.at[s, q, 0], nu2.at[s, q], to[1])
            wait(("rd2", s, q))
            rd2[s, q, 0] = add16(rd2[s, q, 0], r1[s, q, 5])
            msg["nd2", s, q] = send(rd2.at[s, q, 0], nd2.at[s, q], to[3])

    def second_finish(q):
        for s in range(3):
            wait(("nu2", s, q), ("nd2", s, q))
            for k, value in enumerate(
                (add3(r1[s, q, 6], nu2[s, q], rd2[s, q, 1]), add3(r1[s, q, 7], ru2[s, q, 1], nd2[s, q]))
            ):
                for c in range(4):
                    r2[s, c, 2 * q + k] = value[S3 * c : S3 * c + S3].astype(BF16)

    def third_stage():
        for s in range(3):
            to = hop[ORDER[s][2]]
            for d in (2, 1, 3):
                msg["last", s, d] = send(r2.at[s, d], r3.at[s, d], to[d])

    def owned():
        for s in range(3):
            wait(*(("last", s, d) for d in (1, 2, 3)))
            for j in range(4):
                total = r2[s, 0, j].astype(F32)
                for d in (1, 2, 3):
                    total = total + r3[s, d, j].astype(F32)
                out_grad[S3 * s : S3 * s + S3, j * CHUNK : j * CHUNK + CHUNK] = total

    product(0)
    everybody()
    pooled_twin = send(pb.at[pl.ds(0, PADDED)], pb.at[pl.ds(PADDED, PADDED)], twin)
    forward(0)
    product(1)
    forward(1)
    pooled_twin.wait_recv()
    pt[...] = lax.dot_general(
        sel[...], pb[...], (((1,), (1,)), ((), ())), preferred_element_type=F32
    ).astype(BF16)
    product(2)
    backward(0)
    forward(2)
    product(3)
    backward(1)
    forward(3)
    backward(2)
    relay(0)
    backward(3)
    relay(1)
    relay(2)
    finish(0)
    finish(1)
    second_stage(0)
    relay(3)
    give(0)
    finish(2)
    second_relay(0)
    finish(3)
    second_stage(1)
    give(1)
    second_finish(0)
    give(2)
    second_relay(1)
    give(3)
    settle()
    second_finish(1)
    third_stage()
    owned()
    settle()


def hand_over(projected, weight_grad, out_projected, out_grad, sem):
    copies = [pltpu.make_async_copy(weight_grad, out_grad, sem.at[9])]
    for i in range(9):
        rows = pl.ds(9 * i, 9)
        copies.append(pltpu.make_async_copy(projected.at[rows], out_projected.at[rows], sem.at[i]))
    for copy in copies:
        copy.start()
    for copy in copies:
        copy.wait()


def per_device(features, shot_ids, band_width, proj_weight, cotangent):
    frames = jnp.swapaxes(features, 1, 2).reshape(2, TOKS * POOL, D)
    cot = cotangent.transpose(1, 2, 0, 3).reshape(TOKS, 2, H)
    vm = lambda *shape: pltpu.VMEM(shape, BF16)
    sems = lambda n: pltpu.SemaphoreType.DMA((n,))
    any_spec = pl.BlockSpec(memory_space=pl.ANY)
    vmem_spec = pl.BlockSpec(memory_space=pltpu.VMEM)
    pin = lambda space, *arrays: [pltpu.with_memory_space_constraint(a, space) for a in arrays]
    shared = pl.pallas_call(
        pool_kernel,
        out_shape=(vm(PADDED, D), vm(4, D, CHUNK), vm(4, PADDED, CHUNK), vm(576, D)),
        in_specs=[any_spec] * 5,
        out_specs=(vmem_spec,) * 4,
        scratch_shapes=[
            vm(2, TOKS * POOL, D), vm(4, TOKS, 2, CHUNK), vm(256, 256), vm(4, 2, ROWS, D),
            vm(4, ROWS, XL), vm(ROWS, XL // 2), vm(ROWS, XL // 2), vm(ROWS, XL), vm(ROWS, XL),
            vm(ROWS, YL), vm(ROWS, YL), vm(2, ROWS, YL), vm(2, ROWS, YL), vm(ROWS, YL), vm(ROWS, YL),
            pltpu.VMEM(shot_ids.shape, jnp.int32), pltpu.SMEM(band_width.shape, jnp.int32),
            sems(12), sems(24), sems(24),
        ],
        compiler_params=pltpu.CompilerParams(
            collective_id=0, has_side_effects=True, vmem_limit_bytes=24 * 1024 * 1024
        ),
        cost_estimate=pl.CostEstimate(flops=10**9, bytes_accessed=14 * 10**6, transcendentals=0),
    )(*pin(pltpu.HBM, frames, proj_weight, cot, shot_ids, band_width))
    projected, weight_grad = pl.pallas_call(
        main_kernel,
        out_shape=(pltpu.VMEM(cot.shape, BF16), pltpu.VMEM((9, H), F32)),
        in_specs=[vmem_spec] * 4,
        out_specs=(vmem_spec, vmem_spec),
        scratch_shapes=[
            vm(4, PADDED, CHUNK), pltpu.VMEM((2, PADDED, CHUNK), F32),
            vm(2 * PADDED, D), vm(576, 2 * PADDED), vm(4, 2 * PADDED, CHUNK),
            vm(3, 4, 8, S1, CHUNK),
            vm(3, 4, 2, S1, CHUNK), vm(3, 4, 2, S1, CHUNK), vm(3, 4, S1, CHUNK), vm(3, 4, S1, CHUNK),
            vm(3, 2, 8, S2, CHUNK), vm(3, 2, 2, S2, CHUNK), vm(3, 2, 2, S2, CHUNK),
            vm(3, 2, S2, CHUNK), vm(3, 2, S2, CHUNK),
            vm(3, 4, 4, S3, CHUNK), vm(3, 4, 4, S3, CHUNK),
            sems(88), sems(88),
        ],
        compiler_params=pltpu.CompilerParams(
            collective_id=1, has_side_effects=True, vmem_limit_bytes=36 * 1024 * 1024
        ),
        cost_estimate=pl.CostEstimate(flops=3 * 10**9, bytes_accessed=10**6, transcendentals=600000),
    )(*pin(pltpu.VMEM, *shared))
    projected, weight_grad = pl.pallas_call(
        hand_over,
        out_shape=(
            jax.ShapeDtypeStruct(projected.shape, BF16),
            jax.ShapeDtypeStruct(weight_grad.shape, F32),
        ),
        in_specs=[vmem_spec, vmem_spec],
        out_specs=(any_spec, any_spec),
        scratch_shapes=[pltpu.SemaphoreType.DMA((10,))],
    )(*pin(pltpu.VMEM, projected, weight_grad))
    return projected.reshape(1, TOKS, 2, H).transpose(2, 0, 1, 3), weight_grad


def solution(mesh):
    return jax.shard_map(
        per_device,
        mesh=mesh,
        in_specs=(
            P("dp", "tm", None, None),
            P("dp", None),
            P("dp", None),
            P(),
            P("dp", "tm", None, None),
        ),
        out_specs=(P("dp", "tm", None, None), P(("dp", "tm"), None)),
        check_vma=False,
    )
```

```python
import jax
import jax.numpy as jnp
from jax import lax
from jax.experimental import pallas as pl
from jax.experimental.pallas import tpu as pltpu
from jax.sharding import PartitionSpec as P

BLOCK = 64
POOL = 8
DECAY = 16.0
F32, BF16 = jnp.float32, jnp.bfloat16
MESH = pl.DeviceIdType.MESH

D, H, TOKS = 1152, 3584, 81
ROWS = 2 * TOKS
PADDED = 176
XL = 512
YL = D - XL
CHUNK = H // 4
ORDER = (("z", "y", "x"), ("y", "x", "z"), ("x", "z", "y"))
SLOTS = ((2, 0), (1, 1), (2, 1), (3, 0), (1, 0), (3, 1), (0, 0), (0, 1))
S1, S2, S3 = 24, 12, 3
C0 = 0.7978845608028654
C1 = 0.044715


def add16(a, b):
    return (a.astype(F32) + b.astype(F32)).astype(BF16)


class Place:
    def __init__(self, local_sem, send_sem, recv_sem):
        dp, tm = lax.axis_index("dp"), lax.axis_index("tm")
        self.core = lax.rem(dp, 2)
        self.lo = lax.rem(tm, 2)
        self.z, self.y = lax.div(tm, 8), lax.rem(lax.div(tm, 2), 4)
        self.x = lax.div(dp, 2) * 2 + self.lo
        here = {"x": self.x, "y": self.y, "z": self.z}
        self.index = {a: [lax.rem(here[a] + d, 4) for d in range(4)] for a in "xyz"}
        self.hop = {a: [self.dev(**{a: self.index[a][d]}) for d in range(4)] for a in "xyz"}
        self.mate = self.dev(x=self.x + 1 - 2 * self.lo)
        self.twin = self.dev(core=1 - self.core)
        self.sems = local_sem, send_sem, recv_sem
        self.count = [0, 0]
        self.sends = []

    def dev(self, x=None, y=None, z=None, core=None):
        x, y, z, core = (
            mine if other is None else other
            for other, mine in ((x, self.x), (y, self.y), (z, self.z), (core, self.core))
        )
        return (lax.div(x, 2) * 2 + core, z * 8 + y * 2 + lax.rem(x, 2))

    def greet(self, friends):
        barrier = pltpu.get_barrier_semaphore()
        for friend in friends:
            pl.semaphore_signal(barrier, inc=1, device_id=friend, device_id_type=MESH)
        return lambda: pl.semaphore_wait(barrier, len(friends))

    def local(self, src, dst):
        i = self.count[0]
        self.count[0] += 1
        copy = pltpu.make_async_copy(src, dst, self.sems[0].at[i])
        copy.start()
        return copy

    def send(self, src, dst, to):
        i = self.count[1]
        self.count[1] += 1
        copy = pltpu.make_async_remote_copy(
            src_ref=src, dst_ref=dst, send_sem=self.sems[1].at[i], recv_sem=self.sems[2].at[i],
            device_id=to, device_id_type=MESH,
        )
        copy.start()
        self.sends.append(copy)
        return copy

    def settle(self):
        for copy in self.sends:
            copy.wait_send()
        self.sends.clear()


def iota(shape, axis):
    return lax.broadcasted_iota(jnp.int32, shape, axis)


def pool_kernel(
    feat, wgt, cot, shots_in, band_in,
    pb, wv, cv, sel,
    fv, cn, kron, part,
    xa, xfu, xfd, xnu, xnd, yfu, yfd, ynu, ynd, sb, yx,
    ids_v, band_s,
    local_sem, send_sem, recv_sem,
):
    here = Place(local_sem, send_sem, recv_sem)
    core, x, y, z, lo = here.core, here.x, here.y, here.z, here.lo
    hop, local, send = here.hop, here.local, here.send
    la, lb = pl.ds(0, XL), pl.ds(XL, YL)
    ids_in = local(shots_in, ids_v)
    width_in = local(band_in, band_s)
    feat_a = local(feat.at[:, :, la], fv.at[:, :, la])
    feat_b = local(feat.at[:, :, lb], fv.at[:, :, lb])

    everybody = here.greet([hop["y"][1], hop["y"][3], here.mate])

    frame, other = iota((BLOCK, 128), 0), iota((BLOCK, 128), 1)
    distance = jnp.abs(frame - other)
    decay = jnp.exp(-distance.astype(F32) / DECAY)
    ids_in.wait()
    width_in.wait()
    ids = ids_v[...].astype(F32)
    ids = jnp.where(z < 2, ids[:, 0:128], ids[:, 128:256])
    ids = jnp.where(lax.rem(z, 2) == 0, ids, pltpu.roll(ids, 64, 1))
    target_of = iota((256, 128), 0)
    rel = lax.div(target_of, 32)
    target_of = lax.rem(y + lax.div(rel, 2), 4) * 2 + jnp.where(lax.rem(rel, 2) == 0, lo, 1 - lo)
    own_frame = jnp.where(iota((128, 256), 0) == (y * 2 + lo) * POOL + lax.rem(iota((128, 256), 1), 8), 1.0, 0.0)
    own_frame = own_frame.astype(BF16)
    out_row, in_row = iota((256, 256), 0), iota((256, 256), 1)
    same_token = lax.div(lax.rem(out_row, 32), 2) == lax.div(lax.rem(in_row, 128), 8)
    spread = jnp.zeros((256, 256), F32)
    for v in range(2):
        along = jnp.broadcast_to(ids[v : v + 1], (BLOCK, 128))
        down_ids = jnp.sum(jnp.where(frame == other, along, 0.0), axis=1, keepdims=True)
        allowed = (along == down_ids) & (distance <= band_s[v, z]) & (other < BLOCK)
        raw = jnp.where(allowed, decay, 0.0)
        mix = (raw / jnp.sum(raw, axis=1, keepdims=True)).astype(BF16).astype(F32)
        combined = (mix.reshape(8, POOL, 128).sum(axis=1) * 0.125).astype(BF16).astype(F32)
        rows = jnp.zeros((256, 128), F32)
        for p in range(8):
            rows = jnp.where(target_of == p, combined[p : p + 1], rows)
        full = jnp.dot(rows.astype(BF16), own_frame, preferred_element_type=F32)
        mine_too = same_token & (lax.rem(out_row, 2) == v) & (lax.div(in_row, 128) == v)
        spread = jnp.where(mine_too, full, spread)
    kron[...] = spread.astype(BF16)

    def partial_sums(lanes):
        for c in range(6):
            if c < 5:
                blocks = [fv[v, 128 * c : 128 * c + 128, lanes] for v in range(2)]
            else:
                empty = jnp.zeros((120, lanes.stop - lanes.start), BF16)
                blocks = [b for v in range(2) for b in (fv[v, 640:648, lanes], empty)]
            got = jnp.dot(kron[...], jnp.concatenate(blocks, axis=0), preferred_element_type=F32)
            size = 32 if c < 5 else 2
            for r in range(8):
                part[r // 2, r % 2, 32 * c : 32 * c + size, lanes] = got[32 * r : 32 * r + size].astype(BF16)

    l1, l2 = pl.ds(0, XL // 2), pl.ds(XL // 2, XL // 2)
    up, down, side = hop["y"][1], hop["y"][3], here.mate

    feat_a.wait()
    partial_sums(slice(0, XL))
    everybody()
    x_first = {dy: send(part.at[dy, 1, :, la], xa.at[dy], side) for dy in (2, 1, 3, 0)}
    feat_b.wait()
    partial_sums(slice(XL, D))
    far_up = send(part.at[2, 0, :, lb], yfu, up)
    far_down = send(part.at[2, 1, :, lb], yfd, down)
    near_up = {1: send(part.at[1, 1, :, lb], ynu.at[1], up)}
    near_down = {0: send(part.at[3, 0, :, lb], ynd.at[0], down)}

    columns = [pl.ds(j * CHUNK, CHUNK) for j in range(4)]
    cot_in = [local(cot.at[:, :, columns[j]], cn.at[j]) for j in range(4)]
    wgt_in = [local(wgt.at[:, columns[j]], wv.at[j]) for j in range(4)]

    row, lane = iota((576, 128), 0), iota((576, 128), 1)
    which, slot = lax.div(row, 192), lax.div(lax.rem(row, 192), S1)
    half, first = jnp.zeros_like(row), jnp.zeros_like(row)
    for p, (d, h) in enumerate(SLOTS):
        first = jnp.where(slot == p, d, first)
        half = jnp.where(slot == p, h, half)
    second = half * 2 + lax.div(lax.rem(row, S1), S2)
    third = lax.div(lax.rem(row, S2), S3)
    at = {}
    for axis, mine in (("x", x), ("y", y), ("z", z)):
        far = jnp.zeros_like(row)
        for s in range(3):
            far = jnp.where(which == s, (first, second, third)[ORDER[s].index(axis)], far)
        at[axis] = lax.rem(far + mine, 4)
    owner = (lax.div(at["x"], 2) * 2 + core) * 32 + at["z"] * 8 + at["y"] * 2 + lax.rem(at["x"], 2)
    wanted = owner * 9 + which * S3 + lax.rem(row, S3)
    for k in range(D // 128):
        sel[:, 128 * k : 128 * k + 128] = jnp.where(wanted == lane + 128 * k, 1.0, 0.0).astype(BF16)

    def take(dy):
        x_first[dy].wait_recv()
        xa[dy] = add16(xa[dy], part[dy, 0, :, 0:XL])

    take(2)
    far_up2 = send(xa.at[2, :, l1], xfu, up)
    far_up.wait_recv()
    yfu[...] = add16(yfu[...], part[1, 0, :, XL:D])
    near_up[0] = send(yfu, ynu.at[0], up)
    far_down.wait_recv()
    yfd[...] = add16(yfd[...], part[3, 1, :, XL:D])
    near_down[1] = send(yfd, ynd.at[1], down)
    far_down2 = send(xa.at[2, :, l2], xfd, down)
    take(1)
    near_up2 = [send(xa.at[1, :, l2], xnu.at[:, l2], up)]
    take(3)
    near_down2 = [send(xa.at[3, :, l1], xnd.at[:, l1], down)]

    for j in range(4):
        cot_in[j].wait()

        @pl.loop(0, 10)
        def _(i):
            cv[j, pl.ds(pl.multiple_of(i * 16, 16), 16), :] = cn[j, pl.ds(i * 8, 8)].reshape(16, CHUNK)

        tail = jnp.concatenate([cn[j, 80].astype(F32), jnp.zeros((14, CHUNK), F32)], axis=0)
        cv[j, 160:176, :] = tail.astype(BF16)

    far_up2.wait_recv()
    xfu[...] = add16(xfu[...], xa[1, :, 0 : XL // 2])
    near_up2.append(send(xfu, xnu.at[:, l1], up))
    near_up[1].wait_recv()
    near_down[1].wait_recv()
    sb[...] = (
        part[0, 1, :, XL:D].astype(F32) + ynu[1].astype(F32) + ynd[1].astype(F32)
    ).astype(BF16)
    last_x = send(sb, yx, side)
    far_down2.wait_recv()
    xfd[...] = add16(xfd[...], xa[3, :, XL // 2 : XL])
    near_down2.append(send(xfd, xnd.at[:, l2], down))

    def keep(value, lanes):
        value = value.astype(BF16)
        pb[0:160, lanes] = value[0:160]
        tail = jnp.concatenate(
            [value[160:162].astype(F32), jnp.zeros((14, value.shape[1]), F32)], axis=0
        )
        pb[160:176, lanes] = tail.astype(BF16)

    take(0)
    for copy in near_up2 + near_down2:
        copy.wait_recv()
    keep(xa[0].astype(F32) + xnu[...].astype(F32) + xnd[...].astype(F32), slice(0, XL))
    near_up[0].wait_recv()
    near_down[0].wait_recv()
    last_x.wait_recv()
    keep(
        part[0, 0, :, XL:D].astype(F32) + ynu[0].astype(F32) + ynd[0].astype(F32) + yx[...].astype(F32),
        slice(XL, D),
    )
    for copy in wgt_in:
        copy.wait()
    here.settle()


def main_kernel(
    pooled, wv, cv, sel,
    out_proj, out_grad,
    pa, pre, pb, pt, gr, g,
    ru, rd, nu, nd, r1, ru2, rd2, nu2, nd2, r2, r3,
    send_sem, recv_sem,
):
    here = Place(None, send_sem, recv_sem)
    hop, send, settle, twin = here.hop, here.send, here.settle, here.twin
    everybody = here.greet([hop[a][d] for a in "xyz" for d in (1, 2, 3)] + [twin])
    pb[0:PADDED, :] = pooled[...]

    grad_twin = []

    def gelu_rows(values, cotangent):
        square = values * values
        t = jnp.tanh(values * (C0 + (C0 * C1) * square))
        plus = 0.5 * (1.0 + t)
        slope = plus + (0.5 * values) * (1.0 - t * t) * (C0 + (3.0 * C0 * C1) * square)
        return (values * plus).astype(BF16), (cotangent * slope).astype(BF16)

    def product(j):
        pre[j % 2] = jnp.dot(pooled[...], wv[j], preferred_element_type=F32)

    def forward(j):
        for i in range(11):
            rows = slice(16 * i, 16 * i + 16)
            act, grad = gelu_rows(pre[j % 2, rows, :], cv[j, rows, :].astype(F32))
            pa[j, rows, :] = act
            gr[j, rows, :] = grad
        grad_twin.append(send(gr.at[j, pl.ds(0, PADDED)], gr.at[j, pl.ds(PADDED, PADDED)], twin))

    def give(j):
        for i in range(10):
            out_proj[8 * i : 8 * i + 8, :, CHUNK * j : CHUNK * j + CHUNK] = (
                pa[j, 16 * i : 16 * i + 16, :].reshape(8, 2, CHUNK)
            )
        out_proj[80, :, CHUNK * j : CHUNK * j + CHUNK] = pa[j, 160:162, :]

    msg = {}

    def wait(*names):
        for name in names:
            msg[name].wait_recv()

    def add3(a, b, c):
        return a.astype(F32) + b.astype(F32) + c.astype(F32)

    def backward(j):
        grad_twin[j].wait_recv()
        got = jnp.dot(pt[...], gr[j], preferred_element_type=F32)
        for s in range(3):
            for p in range(8):
                base = s * 192 + p * S1
                g[s, j, p] = got[base : base + S1].astype(BF16)
        for s in range(3):
            to = hop[ORDER[s][0]]
            msg["ru", s, j] = send(g.at[s, j, pl.ds(0, 2)], ru.at[s, j], to[1])
            msg["rd", s, j] = send(g.at[s, j, pl.ds(2, 2)], rd.at[s, j], to[3])

    def relay(j):
        for s in range(3):
            to = hop[ORDER[s][0]]
            wait(("ru", s, j))
            ru[s, j, 0] = add16(ru[s, j, 0], g[s, j, 4])
            msg["nu", s, j] = send(ru.at[s, j, 0], nu.at[s, j], to[1])
            wait(("rd", s, j))
            rd[s, j, 0] = add16(rd[s, j, 0], g[s, j, 5])
            msg["nd", s, j] = send(rd.at[s, j, 0], nd.at[s, j], to[3])

    def finish(j):
        q, k = j // 2, j % 2
        for s in range(3):
            wait(("nu", s, j), ("nd", s, j))
            for h, value in enumerate(
                (add3(g[s, j, 6], nu[s, j], rd[s, j, 1]), add3(g[s, j, 7], ru[s, j, 1], nd[s, j]))
            ):
                for b in range(2):
                    slot = SLOTS.index((2 * h + b, k))
                    r1[s, q, slot] = value[S2 * b : S2 * b + S2].astype(BF16)

    def second_stage(q):
        for s in range(3):
            to = hop[ORDER[s][1]]
            msg["ru2", s, q] = send(r1.at[s, q, pl.ds(0, 2)], ru2.at[s, q], to[1])
            msg["rd2", s, q] = send(r1.at[s, q, pl.ds(2, 2)], rd2.at[s, q], to[3])

    def second_relay(q):
        for s in range(3):
            to = hop[ORDER[s][1]]
            wait(("ru2", s, q))
            ru2[s, q, 0] = add16(ru2[s, q, 0], r1[s, q, 4])
            msg["nu2", s, q] = send(ru2.at[s, q, 0], nu2.at[s, q], to[1])
            wait(("rd2", s, q))
            rd2[s, q, 0] = add16(rd2[s, q, 0], r1[s, q, 5])
            msg["nd2", s, q] = send(rd2.at[s, q, 0], nd2.at[s, q], to[3])

    def second_finish(q):
        for s in range(3):
            wait(("nu2", s, q), ("nd2", s, q))
            for k, value in enumerate(
                (add3(r1[s, q, 6], nu2[s, q], rd2[s, q, 1]), add3(r1[s, q, 7], ru2[s, q, 1], nd2[s, q]))
            ):
                for c in range(4):
                    r2[s, c, 2 * q + k] = value[S3 * c : S3 * c + S3].astype(BF16)

    def third_stage():
        for s in range(3):
            to = hop[ORDER[s][2]]
            for d in (2, 1, 3):
                msg["last", s, d] = send(r2.at[s, d], r3.at[s, d], to[d])

    def owned():
        for s in range(3):
            wait(*(("last", s, d) for d in (1, 2, 3)))
            for j in range(4):
                total = r2[s, 0, j].astype(F32)
                for d in (1, 2, 3):
                    total = total + r3[s, d, j].astype(F32)
                out_grad[S3 * s : S3 * s + S3, j * CHUNK : j * CHUNK + CHUNK] = total

    product(0)
    everybody()
    pooled_twin = send(pb.at[pl.ds(0, PADDED)], pb.at[pl.ds(PADDED, PADDED)], twin)
    forward(0)
    for j in (1, 2, 3):
        product(j)
        forward(j)
    pooled_twin.wait_recv()
    pt[...] = lax.dot_general(
        sel[...], pb[...], (((1,), (1,)), ((), ())), preferred_element_type=F32
    ).astype(BF16)
    backward(0)
    backward(1)
    backward(2)
    relay(0)
    backward(3)
    give(0)
    relay(1)
    give(1)
    relay(2)
    give(2)
    relay(3)
    give(3)
    finish(0)
    finish(1)
    second_stage(0)
    finish(2)
    second_relay(0)
    finish(3)
    second_stage(1)
    second_finish(0)
    second_relay(1)
    settle()
    second_finish(1)
    third_stage()
    owned()
    settle()


def hand_over(projected, weight_grad, out_projected, out_grad, sem):
    copies = [pltpu.make_async_copy(weight_grad, out_grad, sem.at[9])]
    for i in range(9):
        rows = pl.ds(9 * i, 9)
        copies.append(pltpu.make_async_copy(projected.at[rows], out_projected.at[rows], sem.at[i]))
    for copy in copies:
        copy.start()
    for copy in copies:
        copy.wait()


def per_device(features, shot_ids, band_width, proj_weight, cotangent):
    frames = jnp.swapaxes(features, 1, 2).reshape(2, TOKS * POOL, D)
    cot = cotangent.transpose(1, 2, 0, 3).reshape(TOKS, 2, H)
    vm = lambda *shape: pltpu.VMEM(shape, BF16)
    sems = lambda n: pltpu.SemaphoreType.DMA((n,))
    any_spec = pl.BlockSpec(memory_space=pl.ANY)
    vmem_spec = pl.BlockSpec(memory_space=pltpu.VMEM)
    pin = lambda space, *arrays: [pltpu.with_memory_space_constraint(a, space) for a in arrays]
    shared = pl.pallas_call(
        pool_kernel,
        out_shape=(vm(PADDED, D), vm(4, D, CHUNK), vm(4, PADDED, CHUNK), vm(576, D)),
        in_specs=[any_spec] * 5,
        out_specs=(vmem_spec,) * 4,
        scratch_shapes=[
            vm(2, TOKS * POOL, D), vm(4, TOKS, 2, CHUNK), vm(256, 256), vm(4, 2, ROWS, D),
            vm(4, ROWS, XL), vm(ROWS, XL // 2), vm(ROWS, XL // 2), vm(ROWS, XL), vm(ROWS, XL),
            vm(ROWS, YL), vm(ROWS, YL), vm(2, ROWS, YL), vm(2, ROWS, YL), vm(ROWS, YL), vm(ROWS, YL),
            pltpu.VMEM(shot_ids.shape, jnp.int32), pltpu.SMEM(band_width.shape, jnp.int32),
            sems(12), sems(24), sems(24),
        ],
        compiler_params=pltpu.CompilerParams(
            collective_id=0, has_side_effects=True, vmem_limit_bytes=24 * 1024 * 1024
        ),
        cost_estimate=pl.CostEstimate(flops=10**9, bytes_accessed=14 * 10**6, transcendentals=0),
    )(*pin(pltpu.HBM, frames, proj_weight, cot, shot_ids, band_width))
    projected, weight_grad = pl.pallas_call(
        main_kernel,
        out_shape=(pltpu.VMEM(cot.shape, BF16), pltpu.VMEM((9, H), F32)),
        in_specs=[vmem_spec] * 4,
        out_specs=(vmem_spec, vmem_spec),
        scratch_shapes=[
            vm(4, PADDED, CHUNK), pltpu.VMEM((2, PADDED, CHUNK), F32),
            vm(2 * PADDED, D), vm(576, 2 * PADDED), vm(4, 2 * PADDED, CHUNK),
            vm(3, 4, 8, S1, CHUNK),
            vm(3, 4, 2, S1, CHUNK), vm(3, 4, 2, S1, CHUNK), vm(3, 4, S1, CHUNK), vm(3, 4, S1, CHUNK),
            vm(3, 2, 8, S2, CHUNK), vm(3, 2, 2, S2, CHUNK), vm(3, 2, 2, S2, CHUNK),
            vm(3, 2, S2, CHUNK), vm(3, 2, S2, CHUNK),
            vm(3, 4, 4, S3, CHUNK), vm(3, 4, 4, S3, CHUNK),
            sems(88), sems(88),
        ],
        compiler_params=pltpu.CompilerParams(
            collective_id=1, has_side_effects=True, vmem_limit_bytes=36 * 1024 * 1024
        ),
        cost_estimate=pl.CostEstimate(flops=3 * 10**9, bytes_accessed=10**6, transcendentals=600000),
    )(*pin(pltpu.VMEM, *shared))
    projected, weight_grad = pl.pallas_call(
        hand_over,
        out_shape=(
            jax.ShapeDtypeStruct(projected.shape, BF16),
            jax.ShapeDtypeStruct(weight_grad.shape, F32),
        ),
        in_specs=[vmem_spec, vmem_spec],
        out_specs=(any_spec, any_spec),
        scratch_shapes=[pltpu.SemaphoreType.DMA((10,))],
    )(*pin(pltpu.VMEM, projected, weight_grad))
    return projected.reshape(1, TOKS, 2, H).transpose(2, 0, 1, 3), weight_grad


def solution(mesh):
    return jax.shard_map(
        per_device,
        mesh=mesh,
        in_specs=(
            P("dp", "tm", None, None),
            P("dp", None),
            P("dp", None),
            P(),
            P("dp", "tm", None, None),
        ),
        out_specs=(P("dp", "tm", None, None), P(("dp", "tm"), None)),
        check_vma=False,
    )
```

```python
import jax
import jax.numpy as jnp
from jax import lax
from jax.experimental import pallas as pl
from jax.experimental.pallas import tpu as pltpu
from jax.sharding import PartitionSpec as P

BLOCK = 64
POOL = 8
DECAY = 16.0
F32, BF16 = jnp.float32, jnp.bfloat16
MESH = pl.DeviceIdType.MESH

D, H, TOKS = 1152, 3584, 81
ROWS = 2 * TOKS
PADDED = 176
XL = 512
YL = D - XL
CHUNK = H // 4
ORDER = (("z", "y", "x"), ("y", "x", "z"), ("x", "z", "y"))
SLOTS = ((2, 0), (1, 1), (2, 1), (3, 0), (1, 0), (3, 1), (0, 0), (0, 1))
S1, S2, S3 = 24, 12, 3
C0 = 0.7978845608028654
C1 = 0.044715


def add16(a, b):
    return a + b


class Place:
    def __init__(self, local_sem, send_sem, recv_sem):
        dp, tm = lax.axis_index("dp"), lax.axis_index("tm")
        self.core = lax.rem(dp, 2)
        self.lo = lax.rem(tm, 2)
        self.z, self.y = lax.div(tm, 8), lax.rem(lax.div(tm, 2), 4)
        self.x = lax.div(dp, 2) * 2 + self.lo
        here = {"x": self.x, "y": self.y, "z": self.z}
        self.index = {a: [lax.rem(here[a] + d, 4) for d in range(4)] for a in "xyz"}
        self.hop = {a: [self.dev(**{a: self.index[a][d]}) for d in range(4)] for a in "xyz"}
        self.mate = self.dev(x=self.x + 1 - 2 * self.lo)
        self.twin = self.dev(core=1 - self.core)
        self.sems = local_sem, send_sem, recv_sem
        self.count = [0, 0]
        self.sends = []

    def dev(self, x=None, y=None, z=None, core=None):
        x, y, z, core = (
            mine if other is None else other
            for other, mine in ((x, self.x), (y, self.y), (z, self.z), (core, self.core))
        )
        return (lax.div(x, 2) * 2 + core, z * 8 + y * 2 + lax.rem(x, 2))

    def greet(self, friends):
        barrier = pltpu.get_barrier_semaphore()
        for friend in friends:
            pl.semaphore_signal(barrier, inc=1, device_id=friend, device_id_type=MESH)
        return lambda: pl.semaphore_wait(barrier, len(friends))

    def local(self, src, dst):
        i = self.count[0]
        self.count[0] += 1
        copy = pltpu.make_async_copy(src, dst, self.sems[0].at[i])
        copy.start()
        return copy

    def send(self, src, dst, to):
        i = self.count[1]
        self.count[1] += 1
        copy = pltpu.make_async_remote_copy(
            src_ref=src, dst_ref=dst, send_sem=self.sems[1].at[i], recv_sem=self.sems[2].at[i],
            device_id=to, device_id_type=MESH,
        )
        copy.start()
        self.sends.append(copy)
        return copy

    def settle(self):
        for copy in self.sends:
            copy.wait_send()
        self.sends.clear()


def iota(shape, axis):
    return lax.broadcasted_iota(jnp.int32, shape, axis)


def kernel(
    feat, wgt, cot, shots_in, band_in,
    out_proj, out_grad,
    wv, cv, sel, fv, cn, kron, part,
    xa, xfu, xfd, xnu, xnd, yfu, yfd, ynu, ynd, sb, yx,
    ids_v, band_s,
    pa, pre, pb, pt, gr, g,
    ru, rd, nu, nd, r1, ru2, rd2, nu2, nd2, r2, r3,
    local_sem, send_sem, recv_sem,
):
    here = Place(local_sem, send_sem, recv_sem)
    core, x, y, z, lo = here.core, here.x, here.y, here.z, here.lo
    hop, local, send, settle, twin = here.hop, here.local, here.send, here.settle, here.twin
    la, lb = pl.ds(0, XL), pl.ds(XL, YL)
    ids_in = local(shots_in, ids_v)
    width_in = local(band_in, band_s)
    feat_a = local(feat.at[:, :, la], fv.at[:, :, la])
    feat_b = local(feat.at[:, :, lb], fv.at[:, :, lb])

    everybody = here.greet([hop[a][d] for a in "xyz" for d in (1, 2, 3)] + [twin])

    frame, other = iota((BLOCK, 128), 0), iota((BLOCK, 128), 1)
    distance = jnp.abs(frame - other)
    decay = jnp.exp(-distance.astype(F32) / DECAY)
    ids_in.wait()
    width_in.wait()
    ids = ids_v[...].astype(F32)
    ids = jnp.where(z < 2, ids[:, 0:128], ids[:, 128:256])
    ids = jnp.where(lax.rem(z, 2) == 0, ids, pltpu.roll(ids, 64, 1))
    target_of = iota((256, 128), 0)
    rel = lax.div(target_of, 32)
    target_of = lax.rem(y + lax.div(rel, 2), 4) * 2 + jnp.where(lax.rem(rel, 2) == 0, lo, 1 - lo)
    own_frame = jnp.where(iota((128, 256), 0) == (y * 2 + lo) * POOL + lax.rem(iota((128, 256), 1), 8), 1.0, 0.0)
    own_frame = own_frame.astype(BF16)
    out_row, in_row = iota((256, 256), 0), iota((256, 256), 1)
    same_token = lax.div(lax.rem(out_row, 32), 2) == lax.div(lax.rem(in_row, 128), 8)
    spread = jnp.zeros((256, 256), F32)
    for v in range(2):
        along = jnp.broadcast_to(ids[v : v + 1], (BLOCK, 128))
        down_ids = jnp.sum(jnp.where(frame == other, along, 0.0), axis=1, keepdims=True)
        allowed = (along == down_ids) & (distance <= band_s[v, z]) & (other < BLOCK)
        raw = jnp.where(allowed, decay, 0.0)
        mix = (raw / jnp.sum(raw, axis=1, keepdims=True)).astype(BF16).astype(F32)
        combined = (mix.reshape(8, POOL, 128).sum(axis=1) * 0.125).astype(BF16).astype(F32)
        rows = jnp.zeros((256, 128), F32)
        for p in range(8):
            rows = jnp.where(target_of == p, combined[p : p + 1], rows)
        full = jnp.dot(rows.astype(BF16), own_frame, preferred_element_type=F32)
        mine_too = same_token & (lax.rem(out_row, 2) == v) & (lax.div(in_row, 128) == v)
        spread = jnp.where(mine_too, full, spread)
    kron[...] = spread.astype(BF16)

    def partial_sums(lanes):
        for c in range(6):
            if c < 5:
                blocks = [fv[v, 128 * c : 128 * c + 128, lanes] for v in range(2)]
            else:
                empty = jnp.zeros((120, lanes.stop - lanes.start), BF16)
                blocks = [b for v in range(2) for b in (fv[v, 640:648, lanes], empty)]
            got = jnp.dot(kron[...], jnp.concatenate(blocks, axis=0), preferred_element_type=F32)
            size = 32 if c < 5 else 2
            for r in range(8):
                part[r // 2, r % 2, 32 * c : 32 * c + size, lanes] = got[32 * r : 32 * r + size].astype(BF16)

    l1, l2 = pl.ds(0, XL // 2), pl.ds(XL // 2, XL // 2)
    up, down, side = hop["y"][1], hop["y"][3], here.mate

    feat_a.wait()
    partial_sums(slice(0, XL))
    everybody()
    x_first = {dy: send(part.at[dy, 1, :, la], xa.at[dy], side) for dy in (2, 1, 3, 0)}
    feat_b.wait()
    partial_sums(slice(XL, D))
    far_up = send(part.at[2, 0, :, lb], yfu, up)
    far_down = send(part.at[2, 1, :, lb], yfd, down)
    near_up = {1: send(part.at[1, 1, :, lb], ynu.at[1], up)}
    near_down = {0: send(part.at[3, 0, :, lb], ynd.at[0], down)}

    columns = [pl.ds(j * CHUNK, CHUNK) for j in range(4)]
    cot_in = [local(cot.at[:, :, columns[j]], cn.at[j]) for j in range(4)]
    wgt_in = [local(wgt.at[:, columns[j]], wv.at[j]) for j in range(4)]

    row, lane = iota((576, 128), 0), iota((576, 128), 1)
    which, slot = lax.div(row, 192), lax.div(lax.rem(row, 192), S1)
    half, first = jnp.zeros_like(row), jnp.zeros_like(row)
    for p, (d, h) in enumerate(SLOTS):
        first = jnp.where(slot == p, d, first)
        half = jnp.where(slot == p, h, half)
    second = half * 2 + lax.div(lax.rem(row, S1), S2)
    third = lax.div(lax.rem(row, S2), S3)
    at = {}
    for axis, mine in (("x", x), ("y", y), ("z", z)):
        far = jnp.zeros_like(row)
        for s in range(3):
            far = jnp.where(which == s, (first, second, third)[ORDER[s].index(axis)], far)
        at[axis] = lax.rem(far + mine, 4)
    owner = (lax.div(at["x"], 2) * 2 + core) * 32 + at["z"] * 8 + at["y"] * 2 + lax.rem(at["x"], 2)
    wanted = owner * 9 + which * S3 + lax.rem(row, S3)
    for k in range(D // 128):
        sel[:, 128 * k : 128 * k + 128] = jnp.where(wanted == lane + 128 * k, 1.0, 0.0).astype(BF16)

    def take(dy):
        x_first[dy].wait_recv()
        xa[dy] = add16(xa[dy], part[dy, 0, :, 0:XL])

    take(2)
    far_up2 = send(xa.at[2, :, l1], xfu, up)
    far_up.wait_recv()
    yfu[...] = add16(yfu[...], part[1, 0, :, XL:D])
    near_up[0] = send(yfu, ynu.at[0], up)
    far_down.wait_recv()
    yfd[...] = add16(yfd[...], part[3, 1, :, XL:D])
    near_down[1] = send(yfd, ynd.at[1], down)
    far_down2 = send(xa.at[2, :, l2], xfd, down)
    take(1)
    near_up2 = [send(xa.at[1, :, l2], xnu.at[:, l2], up)]
    take(3)
    near_down2 = [send(xa.at[3, :, l1], xnd.at[:, l1], down)]

    for j in range(4):
        cot_in[j].wait()

        @pl.loop(0, 10)
        def _(i):
            cv[j, pl.ds(pl.multiple_of(i * 16, 16), 16), :] = cn[j, pl.ds(i * 8, 8)].reshape(16, CHUNK)

        tail = jnp.concatenate([cn[j, 80].astype(F32), jnp.zeros((14, CHUNK), F32)], axis=0)
        cv[j, 160:176, :] = tail.astype(BF16)

    far_up2.wait_recv()
    xfu[...] = add16(xfu[...], xa[1, :, 0 : XL // 2])
    near_up2.append(send(xfu, xnu.at[:, l1], up))
    near_up[1].wait_recv()
    near_down[1].wait_recv()
    sb[...] = (
        part[0, 1, :, XL:D].astype(F32) + ynu[1].astype(F32) + ynd[1].astype(F32)
    ).astype(BF16)
    last_x = send(sb, yx, side)
    far_down2.wait_recv()
    xfd[...] = add16(xfd[...], xa[3, :, XL // 2 : XL])
    near_down2.append(send(xfd, xnd.at[:, l2], down))

    def keep(value, lanes):
        value = value.astype(BF16)
        pb[0:160, lanes] = value[0:160]
        tail = jnp.concatenate(
            [value[160:162].astype(F32), jnp.zeros((14, value.shape[1]), F32)], axis=0
        )
        pb[160:176, lanes] = tail.astype(BF16)

    take(0)
    for copy in near_up2 + near_down2:
        copy.wait_recv()
    keep(xa[0].astype(F32) + xnu[...].astype(F32) + xnd[...].astype(F32), slice(0, XL))
    near_up[0].wait_recv()
    near_down[0].wait_recv()
    last_x.wait_recv()
    keep(
        part[0, 0, :, XL:D].astype(F32) + ynu[0].astype(F32) + ynd[0].astype(F32) + yx[...].astype(F32),
        slice(XL, D),
    )
    pooled_twin = send(pb.at[pl.ds(0, PADDED)], pb.at[pl.ds(PADDED, PADDED)], twin)

    grad_twin = []

    def gelu_rows(values, cotangent):
        square = values * values
        t = jnp.tanh(values * (C0 + (C0 * C1) * square))
        plus = 0.5 * (1.0 + t)
        slope = plus + (0.5 * values) * (1.0 - t * t) * (C0 + (3.0 * C0 * C1) * square)
        return (values * plus).astype(BF16), (cotangent * slope).astype(BF16)

    def product(j):
        pre[j % 2] = jnp.dot(pb[0:PADDED, :], wv[j], preferred_element_type=F32)

    def forward(j):
        for i in range(11):
            rows = slice(16 * i, 16 * i + 16)
            act, grad = gelu_rows(pre[j % 2, rows, :], cv[j, rows, :].astype(F32))
            pa[j, rows, :] = act
            gr[j, rows, :] = grad

    def share(j):
        grad_twin.append(send(gr.at[j, pl.ds(0, PADDED)], gr.at[j, pl.ds(PADDED, PADDED)], twin))

    def give(j):
        for i in range(10):
            out_proj[8 * i : 8 * i + 8, :, CHUNK * j : CHUNK * j + CHUNK] = (
                pa[j, 16 * i : 16 * i + 16, :].reshape(8, 2, CHUNK)
            )
        out_proj[80, :, CHUNK * j : CHUNK * j + CHUNK] = pa[j, 160:162, :]

    msg = {}

    def wait(*names):
        for name in names:
            msg[name].wait_recv()

    def add3(a, b, c):
        return a.astype(F32) + b.astype(F32) + c.astype(F32)

    def backward(j):
        grad_twin[j].wait_recv()
        got = jnp.dot(pt[...], gr[j], preferred_element_type=F32)
        for s in range(3):
            for p in range(8):
                base = s * 192 + p * S1
                g[s, j, p] = got[base : base + S1].astype(BF16)
        for s in range(3):
            to = hop[ORDER[s][0]]
            msg["ru", s, j] = send(g.at[s, j, pl.ds(0, 2)], ru.at[s, j], to[1])
            msg["rd", s, j] = send(g.at[s, j, pl.ds(2, 2)], rd.at[s, j], to[3])

    def relay(j):
        for s in range(3):
            to = hop[ORDER[s][0]]
            wait(("ru", s, j))
            ru[s, j, 0] = add16(ru[s, j, 0], g[s, j, 4])
            msg["nu", s, j] = send(ru.at[s, j, 0], nu.at[s, j], to[1])
            wait(("rd", s, j))
            rd[s, j, 0] = add16(rd[s, j, 0], g[s, j, 5])
            msg["nd", s, j] = send(rd.at[s, j, 0], nd.at[s, j], to[3])

    def finish(j):
        q, k = j // 2, j % 2
        for s in range(3):
            wait(("nu", s, j), ("nd", s, j))
            for h, value in enumerate(
                (add3(g[s, j, 6], nu[s, j], rd[s, j, 1]), add3(g[s, j, 7], ru[s, j, 1], nd[s, j]))
            ):
                for b in range(2):
                    slot = SLOTS.index((2 * h + b, k))
                    r1[s, q, slot] = value[S2 * b : S2 * b + S2].astype(BF16)

    def second_stage(q):
        for s in range(3):
            to = hop[ORDER[s][1]]
            msg["ru2", s, q] = send(r1.at[s, q, pl.ds(0, 2)], ru2.at[s, q], to[1])
            msg["rd2", s, q] = send(r1.at[s, q, pl.ds(2, 2)], rd2.at[s, q], to[3])

    def second_relay(q):
        for s in range(3):
            to = hop[ORDER[s][1]]
            wait(("ru2", s, q))
            ru2[s, q, 0] = add16(ru2[s, q, 0], r1[s, q, 4])
            msg["nu2", s, q] = send(ru2.at[s, q, 0], nu2.at[s, q], to[1])
            wait(("rd2", s, q))
            rd2[s, q, 0] = add16(rd2[s, q, 0], r1[s, q, 5])
            msg["nd2", s, q] = send(rd2.at[s, q, 0], nd2.at[s, q], to[3])

    def second_finish(q):
        for s in range(3):
            wait(("nu2", s, q), ("nd2", s, q))
            for k, value in enumerate(
                (add3(r1[s, q, 6], nu2[s, q], rd2[s, q, 1]), add3(r1[s, q, 7], ru2[s, q, 1], nd2[s, q]))
            ):
                for c in range(4):
                    r2[s, c, 2 * q + k] = value[S3 * c : S3 * c + S3].astype(BF16)

    def third_stage():
        for s in range(3):
            to = hop[ORDER[s][2]]
            for d in (2, 1, 3):
                msg["last", s, d] = send(r2.at[s, d], r3.at[s, d], to[d])

    def owned():
        for s in range(3):
            wait(*(("last", s, d) for d in (1, 2, 3)))
            for j in range(4):
                total = r2[s, 0, j].astype(F32)
                for d in (1, 2, 3):
                    total = total + r3[s, d, j].astype(F32)
                out_grad[S3 * s : S3 * s + S3, j * CHUNK : j * CHUNK + CHUNK] = total

    settle()
    for copy in wgt_in:
        copy.wait()
    product(0)
    for j in range(3):
        product(j + 1)
        forward(j)
        share(j)
    forward(3)
    share(3)
    pooled_twin.wait_recv()
    pt[...] = lax.dot_general(
        sel[...], pb[...], (((1,), (1,)), ((), ())), preferred_element_type=F32
    ).astype(BF16)
    backward(0)
    backward(1)
    backward(2)
    relay(0)
    backward(3)
    relay(1)
    relay(2)
    finish(0)
    relay(3)
    finish(1)
    second_stage(0)
    finish(2)
    second_relay(0)
    finish(3)
    second_stage(1)
    give(0)
    give(1)
    second_finish(0)
    second_relay(1)
    give(2)
    settle()
    second_finish(1)
    third_stage()
    give(3)
    owned()
    settle()


def hand_over(projected, weight_grad, out_projected, out_grad, sem):
    copies = [pltpu.make_async_copy(weight_grad, out_grad, sem.at[9])]
    for i in range(9):
        rows = pl.ds(9 * i, 9)
        copies.append(pltpu.make_async_copy(projected.at[rows], out_projected.at[rows], sem.at[i]))
    for copy in copies:
        copy.start()
    for copy in copies:
        copy.wait()


def per_device(features, shot_ids, band_width, proj_weight, cotangent):
    frames = jnp.swapaxes(features, 1, 2).reshape(2, TOKS * POOL, D)
    cot = cotangent.transpose(1, 2, 0, 3).reshape(TOKS, 2, H)
    vm = lambda *shape: pltpu.VMEM(shape, BF16)
    sems = lambda n: pltpu.SemaphoreType.DMA((n,))
    any_spec = pl.BlockSpec(memory_space=pl.ANY)
    vmem_spec = pl.BlockSpec(memory_space=pltpu.VMEM)
    pin = lambda space, *arrays: [pltpu.with_memory_space_constraint(a, space) for a in arrays]
    projected, weight_grad = pl.pallas_call(
        kernel,
        out_shape=(pltpu.VMEM(cot.shape, BF16), pltpu.VMEM((9, H), F32)),
        in_specs=[any_spec] * 5,
        out_specs=(vmem_spec, vmem_spec),
        scratch_shapes=[
            vm(4, D, CHUNK), vm(4, PADDED, CHUNK), vm(576, D),
            vm(2, TOKS * POOL, D), vm(4, TOKS, 2, CHUNK), vm(256, 256), vm(4, 2, ROWS, D),
            vm(4, ROWS, XL), vm(ROWS, XL // 2), vm(ROWS, XL // 2), vm(ROWS, XL), vm(ROWS, XL),
            vm(ROWS, YL), vm(ROWS, YL), vm(2, ROWS, YL), vm(2, ROWS, YL), vm(ROWS, YL), vm(ROWS, YL),
            pltpu.VMEM(shot_ids.shape, jnp.int32), pltpu.SMEM(band_width.shape, jnp.int32),
            vm(4, PADDED, CHUNK), pltpu.VMEM((2, PADDED, CHUNK), F32),
            vm(2 * PADDED, D), vm(576, 2 * PADDED), vm(4, 2 * PADDED, CHUNK),
            vm(3, 4, 8, S1, CHUNK),
            vm(3, 4, 2, S1, CHUNK), vm(3, 4, 2, S1, CHUNK), vm(3, 4, S1, CHUNK), vm(3, 4, S1, CHUNK),
            vm(3, 2, 8, S2, CHUNK), vm(3, 2, 2, S2, CHUNK), vm(3, 2, 2, S2, CHUNK),
            vm(3, 2, S2, CHUNK), vm(3, 2, S2, CHUNK),
            vm(3, 4, 4, S3, CHUNK), vm(3, 4, 4, S3, CHUNK),
            sems(12), sems(108), sems(108),
        ],
        compiler_params=pltpu.CompilerParams(
            collective_id=0, has_side_effects=True, vmem_limit_bytes=50 * 1024 * 1024
        ),
        cost_estimate=pl.CostEstimate(
            flops=4 * 10**9, bytes_accessed=14 * 10**6, transcendentals=600000
        ),
    )(*pin(pltpu.HBM, frames, proj_weight, cot, shot_ids, band_width))
    projected, weight_grad = pl.pallas_call(
        hand_over,
        out_shape=(
            jax.ShapeDtypeStruct(projected.shape, BF16),
            jax.ShapeDtypeStruct(weight_grad.shape, F32),
        ),
        in_specs=[vmem_spec, vmem_spec],
        out_specs=(any_spec, any_spec),
        scratch_shapes=[pltpu.SemaphoreType.DMA((10,))],
    )(*pin(pltpu.VMEM, projected, weight_grad))
    return projected.reshape(1, TOKS, 2, H).transpose(2, 0, 1, 3), weight_grad


def solution(mesh):
    return jax.shard_map(
        per_device,
        mesh=mesh,
        in_specs=(
            P("dp", "tm", None, None),
            P("dp", None),
            P("dp", None),
            P(),
            P("dp", "tm", None, None),
        ),
        out_specs=(P("dp", "tm", None, None), P(("dp", "tm"), None)),
        check_vma=False,
    )
```

```python
import jax
import jax.numpy as jnp
from jax import lax
from jax.experimental import pallas as pl
from jax.experimental.pallas import tpu as pltpu
from jax.sharding import PartitionSpec as P

BLOCK = 64
POOL = 8
DECAY = 16.0
F32, BF16 = jnp.float32, jnp.bfloat16
MESH = pl.DeviceIdType.MESH

D, H, TOKS = 1152, 3584, 81
ROWS = 2 * TOKS
PADDED = 176
XL = 512
YL = D - XL
CHUNK = H // 4
ORDER = (("z", "y", "x"), ("y", "x", "z"), ("x", "z", "y"))
SLOTS = ((2, 0), (1, 1), (2, 1), (3, 0), (1, 0), (3, 1), (0, 0), (0, 1))
S1, S2, S3 = 24, 12, 3
C0 = 0.7978845608028654
C1 = 0.044715


def add16(a, b):
    return a + b


class Place:
    def __init__(self, local_sem, send_sem, recv_sem):
        dp, tm = lax.axis_index("dp"), lax.axis_index("tm")
        self.core = lax.rem(dp, 2)
        self.lo = lax.rem(tm, 2)
        self.z, self.y = lax.div(tm, 8), lax.rem(lax.div(tm, 2), 4)
        self.x = lax.div(dp, 2) * 2 + self.lo
        here = {"x": self.x, "y": self.y, "z": self.z}
        self.index = {a: [lax.rem(here[a] + d, 4) for d in range(4)] for a in "xyz"}
        self.hop = {a: [self.dev(**{a: self.index[a][d]}) for d in range(4)] for a in "xyz"}
        self.mate = self.dev(x=self.x + 1 - 2 * self.lo)
        self.twin = self.dev(core=1 - self.core)
        self.sems = local_sem, send_sem, recv_sem
        self.count = [0, 0]
        self.sends = []

    def dev(self, x=None, y=None, z=None, core=None):
        x, y, z, core = (
            mine if other is None else other
            for other, mine in ((x, self.x), (y, self.y), (z, self.z), (core, self.core))
        )
        return (lax.div(x, 2) * 2 + core, z * 8 + y * 2 + lax.rem(x, 2))

    def greet(self, friends):
        barrier = pltpu.get_barrier_semaphore()
        for friend in friends:
            pl.semaphore_signal(barrier, inc=1, device_id=friend, device_id_type=MESH)
        return lambda: pl.semaphore_wait(barrier, len(friends))

    def local(self, src, dst):
        i = self.count[0]
        self.count[0] += 1
        copy = pltpu.make_async_copy(src, dst, self.sems[0].at[i])
        copy.start()
        return copy

    def send(self, src, dst, to):
        i = self.count[1]
        self.count[1] += 1
        copy = pltpu.make_async_remote_copy(
            src_ref=src, dst_ref=dst, send_sem=self.sems[1].at[i], recv_sem=self.sems[2].at[i],
            device_id=to, device_id_type=MESH,
        )
        copy.start()
        self.sends.append(copy)
        return copy

    def settle(self):
        for copy in self.sends:
            copy.wait_send()
        self.sends.clear()


def iota(shape, axis):
    return lax.broadcasted_iota(jnp.int32, shape, axis)


def kernel(
    feat, wgt, cot, shots_in, band_in,
    out_proj, out_grad,
    wv, cv, sel, fv, cn, kron, part,
    xa, xfu, xfd, xnu, xnd, yfu, yfd, ynu, ynd, sb, yx,
    ids_v, band_s,
    pa, pre, pb, pt, gr, g,
    ru, rd, nu, nd, r1, in2, r2, r3,
    local_sem, send_sem, recv_sem,
):
    here = Place(local_sem, send_sem, recv_sem)
    core, x, y, z, lo = here.core, here.x, here.y, here.z, here.lo
    hop, local, send, settle, twin = here.hop, here.local, here.send, here.settle, here.twin
    la, lb = pl.ds(0, XL), pl.ds(XL, YL)
    ids_in = local(shots_in, ids_v)
    width_in = local(band_in, band_s)
    feat_a = local(feat.at[:, :, la], fv.at[:, :, la])
    feat_b = local(feat.at[:, :, lb], fv.at[:, :, lb])

    everybody = here.greet([hop[a][d] for a in "xyz" for d in (1, 2, 3)] + [twin])

    frame, other = iota((BLOCK, 128), 0), iota((BLOCK, 128), 1)
    distance = jnp.abs(frame - other)
    decay = jnp.exp(-distance.astype(F32) / DECAY)
    ids_in.wait()
    width_in.wait()
    ids = ids_v[...].astype(F32)
    ids = jnp.where(z < 2, ids[:, 0:128], ids[:, 128:256])
    ids = jnp.where(lax.rem(z, 2) == 0, ids, pltpu.roll(ids, 64, 1))
    target_of = iota((256, 128), 0)
    rel = lax.div(target_of, 32)
    target_of = lax.rem(y + lax.div(rel, 2), 4) * 2 + jnp.where(lax.rem(rel, 2) == 0, lo, 1 - lo)
    own_frame = jnp.where(iota((128, 256), 0) == (y * 2 + lo) * POOL + lax.rem(iota((128, 256), 1), 8), 1.0, 0.0)
    own_frame = own_frame.astype(BF16)
    out_row, in_row = iota((256, 256), 0), iota((256, 256), 1)
    same_token = lax.div(lax.rem(out_row, 32), 2) == lax.div(lax.rem(in_row, 128), 8)
    spread = jnp.zeros((256, 256), F32)
    for v in range(2):
        along = jnp.broadcast_to(ids[v : v + 1], (BLOCK, 128))
        down_ids = jnp.sum(jnp.where(frame == other, along, 0.0), axis=1, keepdims=True)
        allowed = (along == down_ids) & (distance <= band_s[v, z]) & (other < BLOCK)
        raw = jnp.where(allowed, decay, 0.0)
        mix = (raw / jnp.sum(raw, axis=1, keepdims=True)).astype(BF16).astype(F32)
        combined = (mix.reshape(8, POOL, 128).sum(axis=1) * 0.125).astype(BF16).astype(F32)
        rows = jnp.zeros((256, 128), F32)
        for p in range(8):
            rows = jnp.where(target_of == p, combined[p : p + 1], rows)
        full = jnp.dot(rows.astype(BF16), own_frame, preferred_element_type=F32)
        mine_too = same_token & (lax.rem(out_row, 2) == v) & (lax.div(in_row, 128) == v)
        spread = jnp.where(mine_too, full, spread)
    kron[...] = spread.astype(BF16)

    def partial_sums(lanes):
        for c in range(6):
            if c < 5:
                blocks = [fv[v, 128 * c : 128 * c + 128, lanes] for v in range(2)]
            else:
                empty = jnp.zeros((120, lanes.stop - lanes.start), BF16)
                blocks = [b for v in range(2) for b in (fv[v, 640:648, lanes], empty)]
            got = jnp.dot(kron[...], jnp.concatenate(blocks, axis=0), preferred_element_type=F32)
            size = 32 if c < 5 else 2
            for r in range(8):
                part[r // 2, r % 2, 32 * c : 32 * c + size, lanes] = got[32 * r : 32 * r + size].astype(BF16)

    l1, l2 = pl.ds(0, XL // 2), pl.ds(XL // 2, XL // 2)
    up, down, side = hop["y"][1], hop["y"][3], here.mate

    feat_a.wait()
    partial_sums(slice(0, XL))
    everybody()
    x_first = {dy: send(part.at[dy, 1, :, la], xa.at[dy], side) for dy in (2, 1, 3, 0)}
    feat_b.wait()
    partial_sums(slice(XL, D))
    far_up = send(part.at[2, 0, :, lb], yfu, up)
    far_down = send(part.at[2, 1, :, lb], yfd, down)
    near_up = {1: send(part.at[1, 1, :, lb], ynu.at[1], up)}
    near_down = {0: send(part.at[3, 0, :, lb], ynd.at[0], down)}

    columns = [pl.ds(j * CHUNK, CHUNK) for j in range(4)]
    cot_in = [local(cot.at[:, :, columns[j]], cn.at[j]) for j in range(4)]
    wgt_in = [local(wgt.at[:, columns[j]], wv.at[j]) for j in range(4)]

    row, lane = iota((576, 128), 0), iota((576, 128), 1)
    which, slot = lax.div(row, 192), lax.div(lax.rem(row, 192), S1)
    half, first = jnp.zeros_like(row), jnp.zeros_like(row)
    for p, (d, h) in enumerate(SLOTS):
        first = jnp.where(slot == p, d, first)
        half = jnp.where(slot == p, h, half)
    second = half * 2 + lax.div(lax.rem(row, S1), S2)
    third = lax.div(lax.rem(row, S2), S3)
    at = {}
    for axis, mine in (("x", x), ("y", y), ("z", z)):
        far = jnp.zeros_like(row)
        for s in range(3):
            far = jnp.where(which == s, (first, second, third)[ORDER[s].index(axis)], far)
        at[axis] = lax.rem(far + mine, 4)
    owner = (lax.div(at["x"], 2) * 2 + core) * 32 + at["z"] * 8 + at["y"] * 2 + lax.rem(at["x"], 2)
    wanted = owner * 9 + which * S3 + lax.rem(row, S3)
    for k in range(D // 128):
        sel[:, 128 * k : 128 * k + 128] = jnp.where(wanted == lane + 128 * k, 1.0, 0.0).astype(BF16)

    def take(dy):
        x_first[dy].wait_recv()
        xa[dy] = add16(xa[dy], part[dy, 0, :, 0:XL])

    take(2)
    far_up2 = send(xa.at[2, :, l1], xfu, up)
    far_up.wait_recv()
    yfu[...] = add16(yfu[...], part[1, 0, :, XL:D])
    near_up[0] = send(yfu, ynu.at[0], up)
    far_down.wait_recv()
    yfd[...] = add16(yfd[...], part[3, 1, :, XL:D])
    near_down[1] = send(yfd, ynd.at[1], down)
    far_down2 = send(xa.at[2, :, l2], xfd, down)
    take(1)
    near_up2 = [send(xa.at[1, :, l2], xnu.at[:, l2], up)]
    take(3)
    near_down2 = [send(xa.at[3, :, l1], xnd.at[:, l1], down)]

    for j in range(4):
        cot_in[j].wait()

        @pl.loop(0, 10)
        def _(i):
            cv[j, pl.ds(pl.multiple_of(i * 16, 16), 16), :] = cn[j, pl.ds(i * 8, 8)].reshape(16, CHUNK)

        tail = jnp.concatenate([cn[j, 80].astype(F32), jnp.zeros((14, CHUNK), F32)], axis=0)
        cv[j, 160:176, :] = tail.astype(BF16)

    far_up2.wait_recv()
    xfu[...] = add16(xfu[...], xa[1, :, 0 : XL // 2])
    near_up2.append(send(xfu, xnu.at[:, l1], up))
    near_up[1].wait_recv()
    near_down[1].wait_recv()
    sb[...] = (
        part[0, 1, :, XL:D].astype(F32) + ynu[1].astype(F32) + ynd[1].astype(F32)
    ).astype(BF16)
    last_x = send(sb, yx, side)
    far_down2.wait_recv()
    xfd[...] = add16(xfd[...], xa[3, :, XL // 2 : XL])
    near_down2.append(send(xfd, xnd.at[:, l2], down))

    def keep(value, lanes):
        value = value.astype(BF16)
        pb[0:160, lanes] = value[0:160]
        tail = jnp.concatenate(
            [value[160:162].astype(F32), jnp.zeros((14, value.shape[1]), F32)], axis=0
        )
        pb[160:176, lanes] = tail.astype(BF16)

    take(0)
    for copy in near_up2 + near_down2:
        copy.wait_recv()
    keep(xa[0].astype(F32) + xnu[...].astype(F32) + xnd[...].astype(F32), slice(0, XL))
    near_up[0].wait_recv()
    near_down[0].wait_recv()
    last_x.wait_recv()
    keep(
        part[0, 0, :, XL:D].astype(F32) + ynu[0].astype(F32) + ynd[0].astype(F32) + yx[...].astype(F32),
        slice(XL, D),
    )
    pooled_twin = send(pb.at[pl.ds(0, PADDED)], pb.at[pl.ds(PADDED, PADDED)], twin)

    grad_twin = []

    def gelu_rows(values, cotangent):
        square = values * values
        t = jnp.tanh(values * (C0 + (C0 * C1) * square))
        plus = 0.5 * (1.0 + t)
        slope = plus + (0.5 * values) * (1.0 - t * t) * (C0 + (3.0 * C0 * C1) * square)
        return (values * plus).astype(BF16), (cotangent * slope).astype(BF16)

    def product(j):
        pre[j % 2] = jnp.dot(pb[0:PADDED, :], wv[j], preferred_element_type=F32)

    def forward(j):
        for i in range(11):
            rows = slice(16 * i, 16 * i + 16)
            act, grad = gelu_rows(pre[j % 2, rows, :], cv[j, rows, :].astype(F32))
            pa[j, rows, :] = act
            gr[j, rows, :] = grad

    def share(j):
        grad_twin.append(send(gr.at[j, pl.ds(0, PADDED)], gr.at[j, pl.ds(PADDED, PADDED)], twin))

    def give(j):
        for i in range(10):
            out_proj[8 * i : 8 * i + 8, :, CHUNK * j : CHUNK * j + CHUNK] = (
                pa[j, 16 * i : 16 * i + 16, :].reshape(8, 2, CHUNK)
            )
        out_proj[80, :, CHUNK * j : CHUNK * j + CHUNK] = pa[j, 160:162, :]

    msg = {}

    def wait(*names):
        for name in names:
            msg[name].wait_recv()

    def add3(a, b, c):
        return a.astype(F32) + b.astype(F32) + c.astype(F32)

    def backward(j):
        grad_twin[j].wait_recv()
        got = jnp.dot(pt[...], gr[j], preferred_element_type=F32)
        for s in range(3):
            for p in range(8):
                base = s * 192 + p * S1
                g[s, j, p] = got[base : base + S1].astype(BF16)
        for s in range(3):
            to = hop[ORDER[s][0]]
            msg["ru", s, j] = send(g.at[s, j, pl.ds(0, 2)], ru.at[s, j], to[1])
            msg["rd", s, j] = send(g.at[s, j, pl.ds(2, 2)], rd.at[s, j], to[3])

    def relay(j):
        for s in range(3):
            to = hop[ORDER[s][0]]
            wait(("ru", s, j))
            ru[s, j, 0] = add16(ru[s, j, 0], g[s, j, 4])
            msg["nu", s, j] = send(ru.at[s, j, 0], nu.at[s, j], to[1])
            wait(("rd", s, j))
            rd[s, j, 0] = add16(rd[s, j, 0], g[s, j, 5])
            msg["nd", s, j] = send(rd.at[s, j, 0], nd.at[s, j], to[3])

    def finish(j):
        for s in range(3):
            wait(("nu", s, j), ("nd", s, j))
            for h, value in enumerate(
                (add3(g[s, j, 6], nu[s, j], rd[s, j, 1]), add3(g[s, j, 7], ru[s, j, 1], nd[s, j]))
            ):
                for b in range(2):
                    r1[s, 2 * h + b, j] = value[S2 * b : S2 * b + S2].astype(BF16)

    def second_stage(q):
        steps = pl.ds(2 * q, 2)
        for d in (2, 1, 3):
            for s in range(3):
                msg["second", s, q, d] = send(r1.at[s, d, steps], in2.at[s, d, steps], hop[ORDER[s][1]][d])

    def second_finish(q):
        for s in range(3):
            wait(*(("second", s, q, d) for d in (1, 2, 3)))
            for j in (2 * q, 2 * q + 1):
                value = add3(r1[s, 0, j], in2[s, 1, j], in2[s, 3, j]) + in2[s, 2, j].astype(F32)
                for c in range(4):
                    r2[s, c, j] = value[S3 * c : S3 * c + S3].astype(BF16)

    def third_stage():
        for s in range(3):
            to = hop[ORDER[s][2]]
            for d in (2, 1, 3):
                msg["last", s, d] = send(r2.at[s, d], r3.at[s, d], to[d])

    def owned():
        for s in range(3):
            wait(*(("last", s, d) for d in (1, 2, 3)))
            for j in range(4):
                total = r2[s, 0, j].astype(F32)
                for d in (1, 2, 3):
                    total = total + r3[s, d, j].astype(F32)
                out_grad[S3 * s : S3 * s + S3, j * CHUNK : j * CHUNK + CHUNK] = total

    settle()
    for copy in wgt_in:
        copy.wait()

    def step(j):
        product(j)
        forward(j)
        share(j)

    step(0)
    step(1)
    pooled_twin.wait_recv()
    pt[...] = lax.dot_general(
        sel[...], pb[...], (((1,), (1,)), ((), ())), preferred_element_type=F32
    ).astype(BF16)
    backward(0)
    step(2)
    backward(1)
    step(3)
    relay(0)
    backward(2)
    relay(1)
    backward(3)
    give(0)
    relay(2)
    give(1)
    finish(0)
    finish(1)
    second_stage(0)
    relay(3)
    give(2)
    finish(2)
    finish(3)
    second_stage(1)
    second_finish(0)
    settle()
    second_finish(1)
    third_stage()
    give(3)
    owned()
    settle()


def hand_over(projected, weight_grad, out_projected, out_grad, sem):
    copies = [pltpu.make_async_copy(weight_grad, out_grad, sem.at[9])]
    for i in range(9):
        rows = pl.ds(9 * i, 9)
        copies.append(pltpu.make_async_copy(projected.at[rows], out_projected.at[rows], sem.at[i]))
    for copy in copies:
        copy.start()
    for copy in copies:
        copy.wait()


def per_device(features, shot_ids, band_width, proj_weight, cotangent):
    frames = jnp.swapaxes(features, 1, 2).reshape(2, TOKS * POOL, D)
    cot = cotangent.transpose(1, 2, 0, 3).reshape(TOKS, 2, H)
    vm = lambda *shape: pltpu.VMEM(shape, BF16)
    sems = lambda n: pltpu.SemaphoreType.DMA((n,))
    any_spec = pl.BlockSpec(memory_space=pl.ANY)
    vmem_spec = pl.BlockSpec(memory_space=pltpu.VMEM)
    pin = lambda space, *arrays: [pltpu.with_memory_space_constraint(a, space) for a in arrays]
    projected, weight_grad = pl.pallas_call(
        kernel,
        out_shape=(pltpu.VMEM(cot.shape, BF16), pltpu.VMEM((9, H), F32)),
        in_specs=[any_spec] * 5,
        out_specs=(vmem_spec, vmem_spec),
        scratch_shapes=[
            vm(4, D, CHUNK), vm(4, PADDED, CHUNK), vm(576, D),
            vm(2, TOKS * POOL, D), vm(4, TOKS, 2, CHUNK), vm(256, 256), vm(4, 2, ROWS, D),
            vm(4, ROWS, XL), vm(ROWS, XL // 2), vm(ROWS, XL // 2), vm(ROWS, XL), vm(ROWS, XL),
            vm(ROWS, YL), vm(ROWS, YL), vm(2, ROWS, YL), vm(2, ROWS, YL), vm(ROWS, YL), vm(ROWS, YL),
            pltpu.VMEM(shot_ids.shape, jnp.int32), pltpu.SMEM(band_width.shape, jnp.int32),
            vm(4, PADDED, CHUNK), pltpu.VMEM((2, PADDED, CHUNK), F32),
            vm(2 * PADDED, D), vm(576, 2 * PADDED), vm(4, 2 * PADDED, CHUNK),
            vm(3, 4, 8, S1, CHUNK),
            vm(3, 4, 2, S1, CHUNK), vm(3, 4, 2, S1, CHUNK), vm(3, 4, S1, CHUNK), vm(3, 4, S1, CHUNK),
            vm(3, 4, 4, S2, CHUNK), vm(3, 4, 4, S2, CHUNK),
            vm(3, 4, 4, S3, CHUNK), vm(3, 4, 4, S3, CHUNK),
            sems(12), sems(108), sems(108),
        ],
        compiler_params=pltpu.CompilerParams(
            collective_id=0, has_side_effects=True, vmem_limit_bytes=50 * 1024 * 1024
        ),
        cost_estimate=pl.CostEstimate(
            flops=4 * 10**9, bytes_accessed=14 * 10**6, transcendentals=600000
        ),
    )(*pin(pltpu.HBM, frames, proj_weight, cot, shot_ids, band_width))
    projected, weight_grad = pl.pallas_call(
        hand_over,
        out_shape=(
            jax.ShapeDtypeStruct(projected.shape, BF16),
            jax.ShapeDtypeStruct(weight_grad.shape, F32),
        ),
        in_specs=[vmem_spec, vmem_spec],
        out_specs=(any_spec, any_spec),
        scratch_shapes=[pltpu.SemaphoreType.DMA((10,))],
    )(*pin(pltpu.VMEM, projected, weight_grad))
    return projected.reshape(1, TOKS, 2, H).transpose(2, 0, 1, 3), weight_grad


def solution(mesh):
    return jax.shard_map(
        per_device,
        mesh=mesh,
        in_specs=(
            P("dp", "tm", None, None),
            P("dp", None),
            P("dp", None),
            P(),
            P("dp", "tm", None, None),
        ),
        out_specs=(P("dp", "tm", None, None), P(("dp", "tm"), None)),
        check_vma=False,
    )
```

```python
import jax
import jax.numpy as jnp
from jax import lax
from jax.experimental import pallas as pl
from jax.experimental.pallas import tpu as pltpu
from jax.sharding import PartitionSpec as P

BLOCK = 64
POOL = 8
DECAY = 16.0
F32, BF16 = jnp.float32, jnp.bfloat16
MESH = pl.DeviceIdType.MESH

D, H, TOKS = 1152, 3584, 81
ROWS = 2 * TOKS
PADDED = 176
XL = 512
YL = D - XL
STEPS = ((0, 1024), (1024, 1024), (2048, 1024), (3072, 512))
WIDEST = 1024
GROUPS = ((0, 3072), (3072, 512))
ORDER = (("z", "y", "x"), ("y", "x", "z"), ("x", "z", "y"))
SLOTS = ((2, 0), (1, 1), (2, 1), (3, 0), (1, 0), (3, 1), (0, 0), (0, 1))
S1, S2, S3 = 24, 12, 3
C0 = 0.7978845608028654
C1 = 0.044715


def add16(a, b):
    return a + b


class Place:
    def __init__(self, local_sem, send_sem, recv_sem):
        dp, tm = lax.axis_index("dp"), lax.axis_index("tm")
        self.core = lax.rem(dp, 2)
        self.lo = lax.rem(tm, 2)
        self.z, self.y = lax.div(tm, 8), lax.rem(lax.div(tm, 2), 4)
        self.x = lax.div(dp, 2) * 2 + self.lo
        here = {"x": self.x, "y": self.y, "z": self.z}
        self.index = {a: [lax.rem(here[a] + d, 4) for d in range(4)] for a in "xyz"}
        self.hop = {a: [self.dev(**{a: self.index[a][d]}) for d in range(4)] for a in "xyz"}
        self.mate = self.dev(x=self.x + 1 - 2 * self.lo)
        self.twin = self.dev(core=1 - self.core)
        self.sems = local_sem, send_sem, recv_sem
        self.count = [0, 0]
        self.sends = []

    def dev(self, x=None, y=None, z=None, core=None):
        x, y, z, core = (
            mine if other is None else other
            for other, mine in ((x, self.x), (y, self.y), (z, self.z), (core, self.core))
        )
        return (lax.div(x, 2) * 2 + core, z * 8 + y * 2 + lax.rem(x, 2))

    def greet(self, friends):
        barrier = pltpu.get_barrier_semaphore()
        for friend in friends:
            pl.semaphore_signal(barrier, inc=1, device_id=friend, device_id_type=MESH)
        return lambda: pl.semaphore_wait(barrier, len(friends))

    def local(self, src, dst):
        i = self.count[0]
        self.count[0] += 1
        copy = pltpu.make_async_copy(src, dst, self.sems[0].at[i])
        copy.start()
        return copy

    def send(self, src, dst, to):
        i = self.count[1]
        self.count[1] += 1
        copy = pltpu.make_async_remote_copy(
            src_ref=src, dst_ref=dst, send_sem=self.sems[1].at[i], recv_sem=self.sems[2].at[i],
            device_id=to, device_id_type=MESH,
        )
        copy.start()
        self.sends.append(copy)
        return copy

    def settle(self):
        for copy in self.sends:
            copy.wait_send()
        self.sends.clear()


def iota(shape, axis):
    return lax.broadcasted_iota(jnp.int32, shape, axis)


def kernel(
    feat, wgt, cot, shots_in, band_in,
    out_proj, out_grad,
    wv, cv, sel, fv, cn, kron, part,
    xa, xfu, xfd, xnu, xnd, yfu, yfd, ynu, ynd, sb, yx,
    ids_v, band_s,
    pa, pre, pb, pt, gr, g,
    ru, rd, nu, nd, r1, in2, r2, r3,
    local_sem, send_sem, recv_sem,
):
    here = Place(local_sem, send_sem, recv_sem)
    core, x, y, z, lo = here.core, here.x, here.y, here.z, here.lo
    hop, local, send, settle, twin = here.hop, here.local, here.send, here.settle, here.twin
    la, lb = pl.ds(0, XL), pl.ds(XL, YL)
    ids_in = local(shots_in, ids_v)
    width_in = local(band_in, band_s)
    feat_a = local(feat.at[:, :, la], fv.at[:, :, la])
    feat_b = local(feat.at[:, :, lb], fv.at[:, :, lb])

    everybody = here.greet([hop[a][d] for a in "xyz" for d in (1, 2, 3)] + [twin])

    frame, other = iota((BLOCK, 128), 0), iota((BLOCK, 128), 1)
    distance = jnp.abs(frame - other)
    decay = jnp.exp(-distance.astype(F32) / DECAY)
    ids_in.wait()
    width_in.wait()
    ids = ids_v[...].astype(F32)
    ids = jnp.where(z < 2, ids[:, 0:128], ids[:, 128:256])
    ids = jnp.where(lax.rem(z, 2) == 0, ids, pltpu.roll(ids, 64, 1))
    target_of = iota((256, 128), 0)
    rel = lax.div(target_of, 32)
    target_of = lax.rem(y + lax.div(rel, 2), 4) * 2 + jnp.where(lax.rem(rel, 2) == 0, lo, 1 - lo)
    own_frame = jnp.where(iota((128, 256), 0) == (y * 2 + lo) * POOL + lax.rem(iota((128, 256), 1), 8), 1.0, 0.0)
    own_frame = own_frame.astype(BF16)
    out_row, in_row = iota((256, 256), 0), iota((256, 256), 1)
    same_token = lax.div(lax.rem(out_row, 32), 2) == lax.div(lax.rem(in_row, 128), 8)
    spread = jnp.zeros((256, 256), F32)
    for v in range(2):
        along = jnp.broadcast_to(ids[v : v + 1], (BLOCK, 128))
        down_ids = jnp.sum(jnp.where(frame == other, along, 0.0), axis=1, keepdims=True)
        allowed = (along == down_ids) & (distance <= band_s[v, z]) & (other < BLOCK)
        raw = jnp.where(allowed, decay, 0.0)
        mix = (raw / jnp.sum(raw, axis=1, keepdims=True)).astype(BF16).astype(F32)
        combined = (mix.reshape(8, POOL, 128).sum(axis=1) * 0.125).astype(BF16).astype(F32)
        rows = jnp.zeros((256, 128), F32)
        for p in range(8):
            rows = jnp.where(target_of == p, combined[p : p + 1], rows)
        full = jnp.dot(rows.astype(BF16), own_frame, preferred_element_type=F32)
        mine_too = same_token & (lax.rem(out_row, 2) == v) & (lax.div(in_row, 128) == v)
        spread = jnp.where(mine_too, full, spread)
    kron[...] = spread.astype(BF16)

    def partial_sums(lanes):
        for c in range(6):
            if c < 5:
                blocks = [fv[v, 128 * c : 128 * c + 128, lanes] for v in range(2)]
            else:
                empty = jnp.zeros((120, lanes.stop - lanes.start), BF16)
                blocks = [b for v in range(2) for b in (fv[v, 640:648, lanes], empty)]
            got = jnp.dot(kron[...], jnp.concatenate(blocks, axis=0), preferred_element_type=F32)
            size = 32 if c < 5 else 2
            for r in range(8):
                part[r // 2, r % 2, 32 * c : 32 * c + size, lanes] = got[32 * r : 32 * r + size].astype(BF16)

    l1, l2 = pl.ds(0, XL // 2), pl.ds(XL // 2, XL // 2)
    up, down, side = hop["y"][1], hop["y"][3], here.mate

    feat_a.wait()
    partial_sums(slice(0, XL // 2))
    everybody()
    x_first = {dy: [send(part.at[dy, 1, :, l1], xa.at[dy, :, l1], side)] for dy in (2, 1, 3, 0)}
    feat_b.wait()
    partial_sums(slice(XL, D))
    far_up = send(part.at[2, 0, :, lb], yfu, up)
    far_down = send(part.at[2, 1, :, lb], yfd, down)
    near_up = {1: send(part.at[1, 1, :, lb], ynu.at[1], up)}
    near_down = {0: send(part.at[3, 0, :, lb], ynd.at[0], down)}
    partial_sums(slice(XL // 2, XL))
    for dy in (2, 1, 3, 0):
        x_first[dy].append(send(part.at[dy, 1, :, l2], xa.at[dy, :, l2], side))

    cols = [slice(c, c + w) for c, w in STEPS]
    window = [pl.ds(c, w) for c, w in STEPS]
    cot_in = local(cot, cn)
    wgt_in = [local(wgt.at[:, c], wv.at[:, c]) for c in window]

    row, lane = iota((576, 128), 0), iota((576, 128), 1)
    which, slot = lax.div(row, 192), lax.div(lax.rem(row, 192), S1)
    half, first = jnp.zeros_like(row), jnp.zeros_like(row)
    for p, (d, h) in enumerate(SLOTS):
        first = jnp.where(slot == p, d, first)
        half = jnp.where(slot == p, h, half)
    second = half * 2 + lax.div(lax.rem(row, S1), S2)
    third = lax.div(lax.rem(row, S2), S3)
    at = {}
    for axis, mine in (("x", x), ("y", y), ("z", z)):
        far = jnp.zeros_like(row)
        for s in range(3):
            far = jnp.where(which == s, (first, second, third)[ORDER[s].index(axis)], far)
        at[axis] = lax.rem(far + mine, 4)
    owner = (lax.div(at["x"], 2) * 2 + core) * 32 + at["z"] * 8 + at["y"] * 2 + lax.rem(at["x"], 2)
    wanted = owner * 9 + which * S3 + lax.rem(row, S3)
    for k in range(D // 128):
        sel[:, 128 * k : 128 * k + 128] = jnp.where(wanted == lane + 128 * k, 1.0, 0.0).astype(BF16)

    def take(dy):
        for copy in x_first[dy]:
            copy.wait_recv()
        xa[dy] = add16(xa[dy], part[dy, 0, :, 0:XL])

    take(2)
    far_up2 = send(xa.at[2, :, l1], xfu, up)
    far_up.wait_recv()
    yfu[...] = add16(yfu[...], part[1, 0, :, XL:D])
    near_up[0] = send(yfu, ynu.at[0], up)
    far_down.wait_recv()
    yfd[...] = add16(yfd[...], part[3, 1, :, XL:D])
    near_down[1] = send(yfd, ynd.at[1], down)
    far_down2 = send(xa.at[2, :, l2], xfd, down)
    take(1)
    near_up2 = [send(xa.at[1, :, l2], xnu.at[:, l2], up)]
    take(3)
    near_down2 = [send(xa.at[3, :, l1], xnd.at[:, l1], down)]

    cot_in.wait()

    @pl.loop(0, 10)
    def _(i):
        cv[pl.ds(pl.multiple_of(i * 16, 16), 16), :] = cn[pl.ds(i * 8, 8)].reshape(16, H)

    cot_tail = jnp.concatenate([cn[80].astype(F32), jnp.zeros((14, H), F32)], axis=0)
    cv[160:176, :] = cot_tail.astype(BF16)

    far_up2.wait_recv()
    xfu[...] = add16(xfu[...], xa[1, :, 0 : XL // 2])
    near_up2.append(send(xfu, xnu.at[:, l1], up))
    near_up[1].wait_recv()
    near_down[1].wait_recv()
    sb[...] = (
        part[0, 1, :, XL:D].astype(F32) + ynu[1].astype(F32) + ynd[1].astype(F32)
    ).astype(BF16)
    last_x = send(sb, yx, side)
    far_down2.wait_recv()
    xfd[...] = add16(xfd[...], xa[3, :, XL // 2 : XL])
    near_down2.append(send(xfd, xnd.at[:, l2], down))

    def keep(value, lanes):
        value = value.astype(BF16)
        pb[0:160, lanes] = value[0:160]
        tail = jnp.concatenate(
            [value[160:162].astype(F32), jnp.zeros((14, value.shape[1]), F32)], axis=0
        )
        pb[160:176, lanes] = tail.astype(BF16)

    take(0)
    for copy in near_up2 + near_down2:
        copy.wait_recv()
    keep(xa[0].astype(F32) + xnu[...].astype(F32) + xnd[...].astype(F32), slice(0, XL))
    near_up[0].wait_recv()
    near_down[0].wait_recv()
    last_x.wait_recv()
    keep(
        part[0, 0, :, XL:D].astype(F32) + ynu[0].astype(F32) + ynd[0].astype(F32) + yx[...].astype(F32),
        slice(XL, D),
    )
    pooled_twin = send(pb.at[pl.ds(0, PADDED)], pb.at[pl.ds(PADDED, PADDED)], twin)

    grad_twin = []

    def gelu_rows(values, cotangent):
        square = values * values
        t = jnp.tanh(values * (C0 + (C0 * C1) * square))
        plus = 0.5 * (1.0 + t)
        slope = plus + (0.5 * values) * (1.0 - t * t) * (C0 + (3.0 * C0 * C1) * square)
        return (values * plus).astype(BF16), (cotangent * slope).astype(BF16)

    def product(j):
        pre[j % 2, :, 0 : STEPS[j][1]] = jnp.dot(pb[0:PADDED, :], wv[:, cols[j]], preferred_element_type=F32)

    def forward(j):
        for i in range(11):
            rows = slice(16 * i, 16 * i + 16)
            act, grad = gelu_rows(pre[j % 2, rows, 0 : STEPS[j][1]], cv[rows, cols[j]].astype(F32))
            pa[rows, cols[j]] = act
            gr[rows, cols[j]] = grad

    def share(j):
        grad_twin.append(
            send(gr.at[pl.ds(0, PADDED), window[j]], gr.at[pl.ds(PADDED, PADDED), window[j]], twin)
        )

    def give(j):
        for i in range(10):
            rows = pa[16 * i : 16 * i + 16, cols[j]]
            out_proj[8 * i : 8 * i + 8, :, cols[j]] = rows.reshape(8, 2, STEPS[j][1])
        out_proj[80, :, cols[j]] = pa[160:162, cols[j]]

    msg = {}

    def wait(*names):
        for name in names:
            msg[name].wait_recv()

    def add3(a, b, c):
        return a.astype(F32) + b.astype(F32) + c.astype(F32)

    def backward(j):
        grad_twin[j].wait_recv()
        got = jnp.dot(pt[...], gr[:, cols[j]], preferred_element_type=F32)
        for s in range(3):
            for p in range(8):
                base = s * 192 + p * S1
                g[s, p, :, cols[j]] = got[base : base + S1].astype(BF16)
        c = window[j]
        for s in range(3):
            to = hop[ORDER[s][0]]
            msg["ru", s, j] = send(g.at[s, pl.ds(0, 2), :, c], ru.at[s, :, :, c], to[1])
            msg["rd", s, j] = send(g.at[s, pl.ds(2, 2), :, c], rd.at[s, :, :, c], to[3])

    def relay(j):
        c, w = cols[j], window[j]
        for s in range(3):
            to = hop[ORDER[s][0]]
            wait(("ru", s, j))
            ru[s, 0, :, c] = add16(ru[s, 0, :, c], g[s, 4, :, c])
            msg["nu", s, j] = send(ru.at[s, 0, :, w], nu.at[s, :, w], to[1])
            wait(("rd", s, j))
            rd[s, 0, :, c] = add16(rd[s, 0, :, c], g[s, 5, :, c])
            msg["nd", s, j] = send(rd.at[s, 0, :, w], nd.at[s, :, w], to[3])

    def finish(j):
        c = cols[j]
        for s in range(3):
            wait(("nu", s, j), ("nd", s, j))
            for h, value in enumerate(
                (
                    add3(g[s, 6, :, c], nu[s, :, c], rd[s, 1, :, c]),
                    add3(g[s, 7, :, c], ru[s, 1, :, c], nd[s, :, c]),
                )
            ):
                for b in range(2):
                    r1[s, 2 * h + b, :, c] = value[S2 * b : S2 * b + S2].astype(BF16)

    def second_stage(q):
        c = pl.ds(*GROUPS[q])
        for d in (2, 1, 3):
            for s in range(3):
                to = hop[ORDER[s][1]][d]
                msg["second", s, q, d] = send(r1.at[s, d, :, c], in2.at[s, d, :, c], to)

    def third_stage(q):
        c = slice(GROUPS[q][0], sum(GROUPS[q]))
        for s in range(3):
            wait(*(("second", s, q, d) for d in (1, 2, 3)))
            value = add3(r1[s, 0, :, c], in2[s, 1, :, c], in2[s, 3, :, c]) + in2[s, 2, :, c].astype(F32)
            for d in range(4):
                r2[s, d, :, c] = value[S3 * d : S3 * d + S3].astype(BF16)
            w = pl.ds(*GROUPS[q])
            for d in (2, 1, 3):
                msg["last", s, q, d] = send(r2.at[s, d, :, w], r3.at[s, d, :, w], hop[ORDER[s][2]][d])

    def owned(q):
        c = slice(GROUPS[q][0], sum(GROUPS[q]))
        for s in range(3):
            wait(*(("last", s, q, d) for d in (1, 2, 3)))
            total = r2[s, 0, :, c].astype(F32)
            for d in (1, 2, 3):
                total = total + r3[s, d, :, c].astype(F32)
            out_grad[S3 * s : S3 * s + S3, c] = total

    settle()
    for copy in wgt_in:
        copy.wait()

    def step(j):
        product(j)
        forward(j)
        share(j)

    step(0)
    step(1)
    pooled_twin.wait_recv()
    pt[...] = lax.dot_general(
        sel[...], pb[...], (((1,), (1,)), ((), ())), preferred_element_type=F32
    ).astype(BF16)
    backward(0)
    step(2)
    backward(1)
    step(3)
    relay(0)
    backward(2)
    relay(1)
    backward(3)
    relay(2)
    finish(0)
    relay(3)
    finish(1)
    finish(2)
    second_stage(0)
    give(0)
    finish(3)
    second_stage(1)
    give(1)
    third_stage(0)
    give(2)
    settle()
    third_stage(1)
    give(3)
    owned(0)
    owned(1)
    settle()


def hand_over(projected, weight_grad, out_projected, out_grad, sem):
    copies = [pltpu.make_async_copy(weight_grad, out_grad, sem.at[9])]
    for i in range(9):
        rows = pl.ds(9 * i, 9)
        copies.append(pltpu.make_async_copy(projected.at[rows], out_projected.at[rows], sem.at[i]))
    for copy in copies:
        copy.start()
    for copy in copies:
        copy.wait()


def per_device(features, shot_ids, band_width, proj_weight, cotangent):
    frames = jnp.swapaxes(features, 1, 2).reshape(2, TOKS * POOL, D)
    cot = cotangent.transpose(1, 2, 0, 3).reshape(TOKS, 2, H)
    vm = lambda *shape: pltpu.VMEM(shape, BF16)
    sems = lambda n: pltpu.SemaphoreType.DMA((n,))
    any_spec = pl.BlockSpec(memory_space=pl.ANY)
    vmem_spec = pl.BlockSpec(memory_space=pltpu.VMEM)
    pin = lambda space, *arrays: [pltpu.with_memory_space_constraint(a, space) for a in arrays]
    projected, weight_grad = pl.pallas_call(
        kernel,
        out_shape=(pltpu.VMEM(cot.shape, BF16), pltpu.VMEM((9, H), F32)),
        in_specs=[any_spec] * 5,
        out_specs=(vmem_spec, vmem_spec),
        scratch_shapes=[
            vm(D, H), vm(PADDED, H), vm(576, D),
            vm(2, TOKS * POOL, D), vm(TOKS, 2, H), vm(256, 256), vm(4, 2, ROWS, D),
            vm(4, ROWS, XL), vm(ROWS, XL // 2), vm(ROWS, XL // 2), vm(ROWS, XL), vm(ROWS, XL),
            vm(ROWS, YL), vm(ROWS, YL), vm(2, ROWS, YL), vm(2, ROWS, YL), vm(ROWS, YL), vm(ROWS, YL),
            pltpu.VMEM(shot_ids.shape, jnp.int32), pltpu.SMEM(band_width.shape, jnp.int32),
            vm(PADDED, H), pltpu.VMEM((2, PADDED, WIDEST), F32),
            vm(2 * PADDED, D), vm(576, 2 * PADDED), vm(2 * PADDED, H),
            vm(3, 8, S1, H), vm(3, 2, S1, H), vm(3, 2, S1, H), vm(3, S1, H), vm(3, S1, H),
            vm(3, 4, S2, H), vm(3, 4, S2, H), vm(3, 4, S3, H), vm(3, 4, S3, H),
            sems(12), sems(128), sems(128),
        ],
        compiler_params=pltpu.CompilerParams(
            collective_id=0, has_side_effects=True, vmem_limit_bytes=50 * 1024 * 1024
        ),
        cost_estimate=pl.CostEstimate(
            flops=4 * 10**9, bytes_accessed=14 * 10**6, transcendentals=600000
        ),
    )(*pin(pltpu.HBM, frames, proj_weight, cot, shot_ids, band_width))
    projected, weight_grad = pl.pallas_call(
        hand_over,
        out_shape=(
            jax.ShapeDtypeStruct(projected.shape, BF16),
            jax.ShapeDtypeStruct(weight_grad.shape, F32),
        ),
        in_specs=[vmem_spec, vmem_spec],
        out_specs=(any_spec, any_spec),
        scratch_shapes=[pltpu.SemaphoreType.DMA((10,))],
    )(*pin(pltpu.VMEM, projected, weight_grad))
    return projected.reshape(1, TOKS, 2, H).transpose(2, 0, 1, 3), weight_grad


def solution(mesh):
    return jax.shard_map(
        per_device,
        mesh=mesh,
        in_specs=(
            P("dp", "tm", None, None),
            P("dp", None),
            P("dp", None),
            P(),
            P("dp", "tm", None, None),
        ),
        out_specs=(P("dp", "tm", None, None), P(("dp", "tm"), None)),
        check_vma=False,
    )
```

```python
import jax
import jax.numpy as jnp
from jax import lax
from jax.experimental import pallas as pl
from jax.experimental.pallas import tpu as pltpu
from jax.sharding import PartitionSpec as P

BLOCK = 64
POOL = 8
DECAY = 16.0
F32, BF16 = jnp.float32, jnp.bfloat16
MESH = pl.DeviceIdType.MESH

D, H, TOKS = 1152, 3584, 81
ROWS = 2 * TOKS
PADDED = 176
XL = 512
YL = D - XL
MINE = H // 2
STEPS = ((0, 512), (512, 512), (1024, 512), (1536, 256))
WIDEST = 512
GROUPS = ((0, 1536), (1536, 256))
DEPTH = 256
ORDER = (("z", "y", "x"), ("y", "x", "z"), ("x", "z", "y"))
SLOTS = ((2, 0), (1, 1), (2, 1), (3, 0), (1, 0), (3, 1), (0, 0), (0, 1))
S1, S2, S3 = 48, 24, 6
C0 = 0.7978845608028654
C1 = 0.044715


def add16(a, b):
    return a + b


class Place:
    def __init__(self, local_sem, send_sem, recv_sem):
        dp, tm = lax.axis_index("dp"), lax.axis_index("tm")
        self.core = lax.rem(dp, 2)
        self.lo = lax.rem(tm, 2)
        self.z, self.y = lax.div(tm, 8), lax.rem(lax.div(tm, 2), 4)
        self.x = lax.div(dp, 2) * 2 + self.lo
        here = {"x": self.x, "y": self.y, "z": self.z}
        self.index = {a: [lax.rem(here[a] + d, 4) for d in range(4)] for a in "xyz"}
        self.hop = {a: [self.dev(**{a: self.index[a][d]}) for d in range(4)] for a in "xyz"}
        self.mate = self.dev(x=self.x + 1 - 2 * self.lo)
        self.twin = self.dev(core=1 - self.core)
        self.sems = local_sem, send_sem, recv_sem
        self.count = [0, 0]
        self.sends = []

    def dev(self, x=None, y=None, z=None, core=None):
        x, y, z, core = (
            mine if other is None else other
            for other, mine in ((x, self.x), (y, self.y), (z, self.z), (core, self.core))
        )
        return (lax.div(x, 2) * 2 + core, z * 8 + y * 2 + lax.rem(x, 2))

    def greet(self, friends):
        barrier = pltpu.get_barrier_semaphore()
        for friend in friends:
            pl.semaphore_signal(barrier, inc=1, device_id=friend, device_id_type=MESH)
        return lambda: pl.semaphore_wait(barrier, len(friends))

    def local(self, src, dst):
        i = self.count[0]
        self.count[0] += 1
        copy = pltpu.make_async_copy(src, dst, self.sems[0].at[i])
        copy.start()
        return copy

    def send(self, src, dst, to):
        i = self.count[1]
        self.count[1] += 1
        copy = pltpu.make_async_remote_copy(
            src_ref=src, dst_ref=dst, send_sem=self.sems[1].at[i], recv_sem=self.sems[2].at[i],
            device_id=to, device_id_type=MESH,
        )
        copy.start()
        self.sends.append(copy)
        return copy

    def settle(self):
        for copy in self.sends:
            copy.wait_send()
        self.sends.clear()


def iota(shape, axis):
    return lax.broadcasted_iota(jnp.int32, shape, axis)


def kernel(
    feat, wgt, cot, shots_in, band_in,
    out_proj, out_grad,
    wv, cv, cx, sel, fv, cn, kron, part,
    xa, xfu, xfd, xnu, xnd, yfu, yfd, ynu, ynd, sb, yx,
    ids_v, band_s,
    pa, px, pre, pb, pt, gr, g,
    ru, rd, nu, nd, r1, in2, r2, r3, own, fin, fin_twin,
    local_sem, send_sem, recv_sem,
):
    here = Place(local_sem, send_sem, recv_sem)
    core, x, y, z, lo = here.core, here.x, here.y, here.z, here.lo
    hop, local, send, settle, twin = here.hop, here.local, here.send, here.settle, here.twin
    la, lb = pl.ds(0, XL), pl.ds(XL, YL)
    ids_in = local(shots_in, ids_v)
    width_in = local(band_in, band_s)
    feat_a = local(feat.at[:, :, la], fv.at[:, :, la])
    feat_b = local(feat.at[:, :, lb], fv.at[:, :, lb])

    everybody = here.greet([hop[a][d] for a in "xyz" for d in (1, 2, 3)] + [twin])

    frame, other = iota((BLOCK, 128), 0), iota((BLOCK, 128), 1)
    distance = jnp.abs(frame - other)
    decay = jnp.exp(-distance.astype(F32) / DECAY)
    ids_in.wait()
    width_in.wait()
    ids = ids_v[...].astype(F32)
    ids = jnp.where(z < 2, ids[:, 0:128], ids[:, 128:256])
    ids = jnp.where(lax.rem(z, 2) == 0, ids, pltpu.roll(ids, 64, 1))
    target_of = iota((256, 128), 0)
    rel = lax.div(target_of, 32)
    target_of = lax.rem(y + lax.div(rel, 2), 4) * 2 + jnp.where(lax.rem(rel, 2) == 0, lo, 1 - lo)
    own_frame = jnp.where(iota((128, 256), 0) == (y * 2 + lo) * POOL + lax.rem(iota((128, 256), 1), 8), 1.0, 0.0)
    own_frame = own_frame.astype(BF16)
    out_row, in_row = iota((256, 256), 0), iota((256, 256), 1)
    same_token = lax.div(lax.rem(out_row, 32), 2) == lax.div(lax.rem(in_row, 128), 8)
    spread = jnp.zeros((256, 256), F32)
    for v in range(2):
        along = jnp.broadcast_to(ids[v : v + 1], (BLOCK, 128))
        down_ids = jnp.sum(jnp.where(frame == other, along, 0.0), axis=1, keepdims=True)
        allowed = (along == down_ids) & (distance <= band_s[v, z]) & (other < BLOCK)
        raw = jnp.where(allowed, decay, 0.0)
        mix = (raw / jnp.sum(raw, axis=1, keepdims=True)).astype(BF16).astype(F32)
        combined = (mix.reshape(8, POOL, 128).sum(axis=1) * 0.125).astype(BF16).astype(F32)
        rows = jnp.zeros((256, 128), F32)
        for p in range(8):
            rows = jnp.where(target_of == p, combined[p : p + 1], rows)
        full = jnp.dot(rows.astype(BF16), own_frame, preferred_element_type=F32)
        mine_too = same_token & (lax.rem(out_row, 2) == v) & (lax.div(in_row, 128) == v)
        spread = jnp.where(mine_too, full, spread)
    kron[...] = spread.astype(BF16)

    def partial_sums(lanes):
        for c in range(6):
            if c < 5:
                blocks = [fv[v, 128 * c : 128 * c + 128, lanes] for v in range(2)]
            else:
                empty = jnp.zeros((120, lanes.stop - lanes.start), BF16)
                blocks = [b for v in range(2) for b in (fv[v, 640:648, lanes], empty)]
            got = jnp.dot(kron[...], jnp.concatenate(blocks, axis=0), preferred_element_type=F32)
            size = 32 if c < 5 else 2
            for r in range(8):
                part[r // 2, r % 2, 32 * c : 32 * c + size, lanes] = got[32 * r : 32 * r + size].astype(BF16)

    l1, l2 = pl.ds(0, XL // 2), pl.ds(XL // 2, XL // 2)
    up, down, side = hop["y"][1], hop["y"][3], here.mate

    feat_a.wait()
    partial_sums(slice(0, XL))
    everybody()
    x_first = {dy: send(part.at[dy, 1, :, la], xa.at[dy], side) for dy in (2, 1, 3, 0)}
    feat_b.wait()
    partial_sums(slice(XL, D))
    far_up = send(part.at[2, 0, :, lb], yfu, up)
    far_down = send(part.at[2, 1, :, lb], yfd, down)
    near_up = {1: send(part.at[1, 1, :, lb], ynu.at[1], up)}
    near_down = {0: send(part.at[3, 0, :, lb], ynd.at[0], down)}

    cols = [slice(c, c + w) for c, w in STEPS]
    window = [pl.ds(c, w) for c, w in STEPS]
    mine, theirs = pl.multiple_of(core * MINE, 128), pl.multiple_of((1 - core) * MINE, 128)
    cot_in = [local(cot.at[:, :, pl.ds(first, MINE)], cn.at[h]) for h, first in enumerate((theirs, mine))]
    wgt_in = [local(wgt.at[:, pl.ds(pl.multiple_of(mine + c, 128), w)], wv.at[:, pl.ds(c, w)]) for c, w in STEPS]

    row, lane = iota((D, 128), 0), iota((D, 128), 1)
    which, slot = lax.div(row, 8 * S1), lax.div(lax.rem(row, 8 * S1), S1)
    half, first = jnp.zeros_like(row), jnp.zeros_like(row)
    for p, (d, h) in enumerate(SLOTS):
        first = jnp.where(slot == p, d, first)
        half = jnp.where(slot == p, h, half)
    second = half * 2 + lax.div(lax.rem(row, S1), S2)
    third = lax.div(lax.rem(row, S2), S3)
    at = {}
    for axis, place in (("x", x), ("y", y), ("z", z)):
        far = jnp.zeros_like(row)
        for s in range(3):
            far = jnp.where(which == s, (first, second, third)[ORDER[s].index(axis)], far)
        at[axis] = lax.rem(far + place, 4)
    keeper = jnp.where(lax.rem(row, S3) < 3, 0, 1)
    owner = (lax.div(at["x"], 2) * 2 + keeper) * 32 + at["z"] * 8 + at["y"] * 2 + lax.rem(at["x"], 2)
    wanted = owner * 9 + which * 3 + lax.rem(row, 3)
    for k in range(D // 128):
        sel[:, 128 * k : 128 * k + 128] = jnp.where(wanted == lane + 128 * k, 1.0, 0.0).astype(BF16)

    def take(dy):
        x_first[dy].wait_recv()
        xa[dy] = add16(xa[dy], part[dy, 0, :, 0:XL])

    take(2)
    far_up2 = send(xa.at[2, :, l1], xfu, up)
    far_up.wait_recv()
    yfu[...] = add16(yfu[...], part[1, 0, :, XL:D])
    near_up[0] = send(yfu, ynu.at[0], up)
    far_down.wait_recv()
    yfd[...] = add16(yfd[...], part[3, 1, :, XL:D])
    near_down[1] = send(yfd, ynd.at[1], down)
    far_down2 = send(xa.at[2, :, l2], xfd, down)
    take(1)
    near_up2 = [send(xa.at[1, :, l2], xnu.at[:, l2], up)]
    take(3)
    near_down2 = [send(xa.at[3, :, l1], xnd.at[:, l1], down)]

    for h, dst in enumerate((cx, cv)):
        cot_in[h].wait()

        @pl.loop(0, 10)
        def _(i):
            dst[pl.ds(pl.multiple_of(i * 16, 16), 16), :] = cn[h, pl.ds(i * 8, 8)].reshape(16, MINE)

        cot_tail = jnp.concatenate([cn[h, 80].astype(F32), jnp.zeros((14, MINE), F32)], axis=0)
        dst[160:176, :] = cot_tail.astype(BF16)
        if h == 0:
            cot_twin = send(cx, cv.at[pl.ds(PADDED, PADDED)], twin)
    for k in range(2):
        gr[DEPTH * k + PADDED : DEPTH * k + DEPTH, :] = jnp.zeros((DEPTH - PADDED, MINE), BF16)
    pt[:, 128:256] = jnp.zeros((D, 128), BF16)

    far_up2.wait_recv()
    xfu[...] = add16(xfu[...], xa[1, :, 0 : XL // 2])
    near_up2.append(send(xfu, xnu.at[:, l1], up))
    near_up[1].wait_recv()
    near_down[1].wait_recv()
    sb[...] = (
        part[0, 1, :, XL:D].astype(F32) + ynu[1].astype(F32) + ynd[1].astype(F32)
    ).astype(BF16)
    last_x = send(sb, yx, side)
    far_down2.wait_recv()
    xfd[...] = add16(xfd[...], xa[3, :, XL // 2 : XL])
    near_down2.append(send(xfd, xnd.at[:, l2], down))

    def keep(value, lanes):
        value = value.astype(BF16)
        pb[0:160, lanes] = value[0:160]
        tail = jnp.concatenate(
            [value[160:162].astype(F32), jnp.zeros((14, value.shape[1]), F32)], axis=0
        )
        pb[160:176, lanes] = tail.astype(BF16)

    take(0)
    for copy in near_up2 + near_down2:
        copy.wait_recv()
    keep(xa[0].astype(F32) + xnu[...].astype(F32) + xnd[...].astype(F32), slice(0, XL))
    near_up[0].wait_recv()
    near_down[0].wait_recv()
    last_x.wait_recv()
    keep(
        part[0, 0, :, XL:D].astype(F32) + ynu[0].astype(F32) + ynd[0].astype(F32) + yx[...].astype(F32),
        slice(XL, D),
    )
    pooled_twin = send(pb.at[pl.ds(0, PADDED)], pb.at[pl.ds(PADDED, PADDED)], twin)

    pt[:, 0:PADDED] = lax.dot_general(
        sel[...], pb[0:PADDED, :], (((1,), (1,)), ((), ())), preferred_element_type=F32
    ).astype(BF16)
    rows_twin = send(pt.at[:, pl.ds(0, DEPTH)], pt.at[:, pl.ds(DEPTH, DEPTH)], twin)

    act_twin = []

    def gelu_rows(values, cotangent):
        square = values * values
        t = jnp.tanh(values * (C0 + (C0 * C1) * square))
        plus = 0.5 * (1.0 + t)
        slope = plus + (0.5 * values) * (1.0 - t * t) * (C0 + (3.0 * C0 * C1) * square)
        return (values * plus).astype(BF16), (cotangent * slope).astype(BF16)

    def product(j):
        pre[j % 2, :, 0 : STEPS[j][1]] = jnp.dot(pb[...], wv[:, cols[j]], preferred_element_type=F32)

    def forward(j):
        for i in range(22):
            rows = slice(16 * i, 16 * i + 16)
            base = 16 * i if i < 11 else 16 * i - PADDED + DEPTH
            act, grad = gelu_rows(pre[j % 2, rows, 0 : STEPS[j][1]], cv[rows, cols[j]].astype(F32))
            pa[rows, cols[j]] = act
            gr[base : base + 16, cols[j]] = grad
        act_twin.append(send(pa.at[pl.ds(PADDED, PADDED), window[j]], px.at[:, window[j]], twin))

    def give(j, from_twin):
        if from_twin:
            act_twin[j].wait_recv()
        c, w = STEPS[j]
        source, first = (px, theirs) if from_twin else (pa, mine)
        columns = pl.ds(pl.multiple_of(first + c, 128), w)
        for i in range(10):
            rows = source[16 * i : 16 * i + 16, cols[j]]
            out_proj[8 * i : 8 * i + 8, :, columns] = rows.reshape(8, 2, w)
        out_proj[80, :, columns] = source[160:162, cols[j]]

    msg = {}

    def wait(*names):
        for name in names:
            msg[name].wait_recv()

    def add3(a, b, c):
        return a.astype(F32) + b.astype(F32) + c.astype(F32)

    def backward(j):
        got = jnp.dot(pt[...], gr[:, cols[j]], preferred_element_type=F32)
        for s in range(3):
            for p in range(8):
                base = (s * 8 + p) * S1
                g[s, p, :, cols[j]] = got[base : base + S1].astype(BF16)
        c = window[j]
        for s in range(3):
            to = hop[ORDER[s][0]]
            msg["ru", s, j] = send(g.at[s, pl.ds(0, 2), :, c], ru.at[s, :, :, c], to[1])
            msg["rd", s, j] = send(g.at[s, pl.ds(2, 2), :, c], rd.at[s, :, :, c], to[3])

    def relay(j):
        c, w = cols[j], window[j]
        for s in range(3):
            to = hop[ORDER[s][0]]
            wait(("ru", s, j))
            ru[s, 0, :, c] = add16(ru[s, 0, :, c], g[s, 4, :, c])
            msg["nu", s, j] = send(ru.at[s, 0, :, w], nu.at[s, :, w], to[1])
            wait(("rd", s, j))
            rd[s, 0, :, c] = add16(rd[s, 0, :, c], g[s, 5, :, c])
            msg["nd", s, j] = send(rd.at[s, 0, :, w], nd.at[s, :, w], to[3])

    def finish(j):
        c = cols[j]
        for s in range(3):
            wait(("nu", s, j), ("nd", s, j))
            for h, value in enumerate(
                (
                    add3(g[s, 6, :, c], nu[s, :, c], rd[s, 1, :, c]),
                    add3(g[s, 7, :, c], ru[s, 1, :, c], nd[s, :, c]),
                )
            ):
                for b in range(2):
                    r1[s, 2 * h + b, :, c] = value[S2 * b : S2 * b + S2].astype(BF16)

    def second_stage(q):
        c = pl.ds(*GROUPS[q])
        for d in (2, 1, 3):
            for s in range(3):
                to = hop[ORDER[s][1]][d]
                msg["second", s, q, d] = send(r1.at[s, d, :, c], in2.at[s, d, :, c], to)

    def third_stage(q):
        c = slice(GROUPS[q][0], sum(GROUPS[q]))
        for s in range(3):
            wait(*(("second", s, q, d) for d in (1, 2, 3)))
            value = add3(r1[s, 0, :, c], in2[s, 1, :, c], in2[s, 3, :, c]) + in2[s, 2, :, c].astype(F32)
            for d in range(4):
                r2[s, d, :, c] = value[S3 * d : S3 * d + S3].astype(BF16)
            w = pl.ds(*GROUPS[q])
            for d in (2, 1, 3):
                msg["last", s, q, d] = send(r2.at[s, d, :, w], r3.at[s, d, :, w], hop[ORDER[s][2]][d])

    def owned(q):
        c = slice(GROUPS[q][0], sum(GROUPS[q]))
        for s in range(3):
            wait(*(("last", s, q, d) for d in (1, 2, 3)))
            total = r2[s, 0, :, c].astype(F32)
            for d in (1, 2, 3):
                total = total + r3[s, d, :, c].astype(F32)
            own[s, :, c] = jnp.where(core == 0, total[0:3], total[3:6])
            fin[s, :, c] = jnp.where(core == 0, total[3:6], total[0:3]).astype(BF16)
        w = pl.ds(*GROUPS[q])
        msg["swap", q] = send(fin.at[:, :, w], fin_twin.at[:, :, w], twin)

    def swapped(q):
        c = slice(GROUPS[q][0], sum(GROUPS[q]))
        wait(("swap", q))
        for s in range(3):
            here_half, there_half = own[s, :, c], fin_twin[s, :, c].astype(F32)
            rows = slice(3 * s, 3 * s + 3)
            out_grad[rows, c] = jnp.where(core == 0, here_half, there_half)
            out_grad[rows, slice(c.start + MINE, c.stop + MINE)] = jnp.where(core == 0, there_half, here_half)

    for copy in wgt_in:
        copy.wait()
    cot_twin.wait_recv()
    pooled_twin.wait_recv()
    product(0)
    forward(0)
    rows_twin.wait_recv()
    backward(0)
    product(1)
    forward(1)
    backward(1)
    product(2)
    forward(2)
    relay(0)
    backward(2)
    product(3)
    forward(3)
    relay(1)
    backward(3)
    relay(2)
    finish(0)
    relay(3)
    finish(1)
    finish(2)
    second_stage(0)
    give(0, False)
    give(1, False)
    finish(3)
    second_stage(1)
    give(2, False)
    give(3, False)
    third_stage(0)
    give(0, True)
    give(1, True)
    settle()
    third_stage(1)
    owned(0)
    give(2, True)
    owned(1)
    give(3, True)
    swapped(0)
    swapped(1)
    settle()


def hand_over(projected, weight_grad, out_projected, out_grad, sem):
    copies = [pltpu.make_async_copy(weight_grad, out_grad, sem.at[9])]
    for i in range(9):
        rows = pl.ds(9 * i, 9)
        copies.append(pltpu.make_async_copy(projected.at[rows], out_projected.at[rows], sem.at[i]))
    for copy in copies:
        copy.start()
    for copy in copies:
        copy.wait()


def per_device(features, shot_ids, band_width, proj_weight, cotangent):
    frames = jnp.swapaxes(features, 1, 2).reshape(2, TOKS * POOL, D)
    cot = cotangent.transpose(1, 2, 0, 3).reshape(TOKS, 2, H)
    vm = lambda *shape: pltpu.VMEM(shape, BF16)
    sems = lambda n: pltpu.SemaphoreType.DMA((n,))
    any_spec = pl.BlockSpec(memory_space=pl.ANY)
    vmem_spec = pl.BlockSpec(memory_space=pltpu.VMEM)
    pin = lambda space, *arrays: [pltpu.with_memory_space_constraint(a, space) for a in arrays]
    projected, weight_grad = pl.pallas_call(
        kernel,
        out_shape=(pltpu.VMEM(cot.shape, BF16), pltpu.VMEM((9, H), F32)),
        in_specs=[any_spec] * 5,
        out_specs=(vmem_spec, vmem_spec),
        scratch_shapes=[
            vm(D, MINE), vm(2 * PADDED, MINE), vm(PADDED, MINE), vm(D, D),
            vm(2, TOKS * POOL, D), vm(2, TOKS, 2, MINE), vm(256, 256), vm(4, 2, ROWS, D),
            vm(4, ROWS, XL), vm(ROWS, XL // 2), vm(ROWS, XL // 2), vm(ROWS, XL), vm(ROWS, XL),
            vm(ROWS, YL), vm(ROWS, YL), vm(2, ROWS, YL), vm(2, ROWS, YL), vm(ROWS, YL), vm(ROWS, YL),
            pltpu.VMEM(shot_ids.shape, jnp.int32), pltpu.SMEM(band_width.shape, jnp.int32),
            vm(2 * PADDED, MINE), vm(PADDED, MINE), pltpu.VMEM((2, 2 * PADDED, WIDEST), F32),
            vm(2 * PADDED, D), vm(D, 2 * DEPTH), vm(2 * DEPTH, MINE),
            vm(3, 8, S1, MINE), vm(3, 2, S1, MINE), vm(3, 2, S1, MINE), vm(3, S1, MINE), vm(3, S1, MINE),
            vm(3, 4, S2, MINE), vm(3, 4, S2, MINE), vm(3, 4, S3, MINE), vm(3, 4, S3, MINE),
            pltpu.VMEM((3, 3, MINE), F32), vm(3, 3, MINE), vm(3, 3, MINE),
            sems(12), sems(128), sems(128),
        ],
        compiler_params=pltpu.CompilerParams(
            collective_id=0, has_side_effects=True, vmem_limit_bytes=50 * 1024 * 1024
        ),
        cost_estimate=pl.CostEstimate(
            flops=4 * 10**9, bytes_accessed=14 * 10**6, transcendentals=600000
        ),
    )(*pin(pltpu.HBM, frames, proj_weight, cot, shot_ids, band_width))
    projected, weight_grad = pl.pallas_call(
        hand_over,
        out_shape=(
            jax.ShapeDtypeStruct(projected.shape, BF16),
            jax.ShapeDtypeStruct(weight_grad.shape, F32),
        ),
        in_specs=[vmem_spec, vmem_spec],
        out_specs=(any_spec, any_spec),
        scratch_shapes=[pltpu.SemaphoreType.DMA((10,))],
    )(*pin(pltpu.VMEM, projected, weight_grad))
    return projected.reshape(1, TOKS, 2, H).transpose(2, 0, 1, 3), weight_grad


def solution(mesh):
    return jax.shard_map(
        per_device,
        mesh=mesh,
        in_specs=(
            P("dp", "tm", None, None),
            P("dp", None),
            P("dp", None),
            P(),
            P("dp", "tm", None, None),
        ),
        out_specs=(P("dp", "tm", None, None), P(("dp", "tm"), None)),
        check_vma=False,
    )
```

```python
import jax
import jax.numpy as jnp
from jax import lax
from jax.experimental import pallas as pl
from jax.experimental.pallas import tpu as pltpu
from jax.sharding import PartitionSpec as P

BLOCK = 64
POOL = 8
DECAY = 16.0
F32, BF16 = jnp.float32, jnp.bfloat16
MESH = pl.DeviceIdType.MESH

D, H, TOKS = 1152, 3584, 81
ROWS = 2 * TOKS
PADDED = 176
XL = 512
YL = D - XL
CHUNK = H // 4
ORDER = (("z", "y", "x"), ("y", "x", "z"), ("x", "z", "y"))
SLOTS = ((2, 0), (1, 1), (2, 1), (3, 0), (1, 0), (3, 1), (0, 0), (0, 1))
S1, S2, S3 = 24, 12, 3
C0 = 0.7978845608028654
C1 = 0.044715


def add16(a, b):
    return a + b


class Place:
    def __init__(self, local_sem, send_sem, recv_sem):
        dp, tm = lax.axis_index("dp"), lax.axis_index("tm")
        self.core = lax.rem(dp, 2)
        self.lo = lax.rem(tm, 2)
        self.z, self.y = lax.div(tm, 8), lax.rem(lax.div(tm, 2), 4)
        self.x = lax.div(dp, 2) * 2 + self.lo
        here = {"x": self.x, "y": self.y, "z": self.z}
        self.index = {a: [lax.rem(here[a] + d, 4) for d in range(4)] for a in "xyz"}
        self.hop = {a: [self.dev(**{a: self.index[a][d]}) for d in range(4)] for a in "xyz"}
        self.mate = self.dev(x=self.x + 1 - 2 * self.lo)
        self.twin = self.dev(core=1 - self.core)
        self.sems = local_sem, send_sem, recv_sem
        self.count = [0, 0]
        self.sends = []

    def dev(self, x=None, y=None, z=None, core=None):
        x, y, z, core = (
            mine if other is None else other
            for other, mine in ((x, self.x), (y, self.y), (z, self.z), (core, self.core))
        )
        return (lax.div(x, 2) * 2 + core, z * 8 + y * 2 + lax.rem(x, 2))

    def greet(self, friends):
        barrier = pltpu.get_barrier_semaphore()
        for friend in friends:
            pl.semaphore_signal(barrier, inc=1, device_id=friend, device_id_type=MESH)
        return lambda: pl.semaphore_wait(barrier, len(friends))

    def local(self, src, dst):
        i = self.count[0]
        self.count[0] += 1
        copy = pltpu.make_async_copy(src, dst, self.sems[0].at[i])
        copy.start()
        return copy

    def send(self, src, dst, to):
        i = self.count[1]
        self.count[1] += 1
        copy = pltpu.make_async_remote_copy(
            src_ref=src, dst_ref=dst, send_sem=self.sems[1].at[i], recv_sem=self.sems[2].at[i],
            device_id=to, device_id_type=MESH,
        )
        copy.start()
        self.sends.append(copy)
        return copy

    def settle(self):
        for copy in self.sends:
            copy.wait_send()
        self.sends.clear()


def iota(shape, axis):
    return lax.broadcasted_iota(jnp.int32, shape, axis)


def kernel(
    feat, wgt, cot, shots_in, band_in,
    out_proj, out_grad,
    wv, cv, sel, fv, cn, kron, part,
    xa, xfu, xfd, xnu, xnd, yfu, yfd, ynu, ynd, sb, yx,
    ids_v, band_s,
    pa, pre, pb, pt, gr, g,
    ru, rd, nu, nd, r1, in2, r2, r3,
    local_sem, send_sem, recv_sem,
):
    here = Place(local_sem, send_sem, recv_sem)
    core, x, y, z, lo = here.core, here.x, here.y, here.z, here.lo
    hop, local, send, settle, twin = here.hop, here.local, here.send, here.settle, here.twin
    la, lb = pl.ds(0, XL), pl.ds(XL, YL)
    ids_in = local(shots_in, ids_v)
    width_in = local(band_in, band_s)
    feat_a = local(feat.at[:, :, la], fv.at[:, :, la])
    feat_b = local(feat.at[:, :, lb], fv.at[:, :, lb])

    everybody = here.greet([hop[a][d] for a in "xyz" for d in (1, 2, 3)] + [twin])

    frame, other = iota((BLOCK, 128), 0), iota((BLOCK, 128), 1)
    distance = jnp.abs(frame - other)
    decay = jnp.exp(-distance.astype(F32) / DECAY)
    ids_in.wait()
    width_in.wait()
    ids = ids_v[...].astype(F32)
    ids = jnp.where(z < 2, ids[:, 0:128], ids[:, 128:256])
    ids = jnp.where(lax.rem(z, 2) == 0, ids, pltpu.roll(ids, 64, 1))
    target_of = iota((256, 128), 0)
    rel = lax.div(target_of, 32)
    target_of = lax.rem(y + lax.div(rel, 2), 4) * 2 + jnp.where(lax.rem(rel, 2) == 0, lo, 1 - lo)
    own_frame = jnp.where(iota((128, 256), 0) == (y * 2 + lo) * POOL + lax.rem(iota((128, 256), 1), 8), 1.0, 0.0)
    own_frame = own_frame.astype(BF16)
    out_row, in_row = iota((256, 256), 0), iota((256, 256), 1)
    same_token = lax.div(lax.rem(out_row, 32), 2) == lax.div(lax.rem(in_row, 128), 8)
    spread = jnp.zeros((256, 256), F32)
    for v in range(2):
        along = jnp.broadcast_to(ids[v : v + 1], (BLOCK, 128))
        down_ids = jnp.sum(jnp.where(frame == other, along, 0.0), axis=1, keepdims=True)
        allowed = (along == down_ids) & (distance <= band_s[v, z]) & (other < BLOCK)
        raw = jnp.where(allowed, decay, 0.0)
        mix = (raw / jnp.sum(raw, axis=1, keepdims=True)).astype(BF16).astype(F32)
        combined = (mix.reshape(8, POOL, 128).sum(axis=1) * 0.125).astype(BF16).astype(F32)
        rows = jnp.zeros((256, 128), F32)
        for p in range(8):
            rows = jnp.where(target_of == p, combined[p : p + 1], rows)
        full = jnp.dot(rows.astype(BF16), own_frame, preferred_element_type=F32)
        mine_too = same_token & (lax.rem(out_row, 2) == v) & (lax.div(in_row, 128) == v)
        spread = jnp.where(mine_too, full, spread)
    kron[...] = spread.astype(BF16)

    def partial_sums(lanes):
        for c in range(6):
            if c < 5:
                blocks = [fv[v, 128 * c : 128 * c + 128, lanes] for v in range(2)]
            else:
                empty = jnp.zeros((120, lanes.stop - lanes.start), BF16)
                blocks = [b for v in range(2) for b in (fv[v, 640:648, lanes], empty)]
            got = jnp.dot(kron[...], jnp.concatenate(blocks, axis=0), preferred_element_type=F32)
            size = 32 if c < 5 else 2
            for r in range(8):
                part[r // 2, r % 2, 32 * c : 32 * c + size, lanes] = got[32 * r : 32 * r + size].astype(BF16)

    l1, l2 = pl.ds(0, XL // 2), pl.ds(XL // 2, XL // 2)
    up, down, side = hop["y"][1], hop["y"][3], here.mate

    feat_a.wait()
    partial_sums(slice(0, XL))
    everybody()
    x_first = {dy: send(part.at[dy, 1, :, la], xa.at[dy], side) for dy in (2, 1, 3, 0)}
    feat_b.wait()
    partial_sums(slice(XL, D))
    far_up = send(part.at[2, 0, :, lb], yfu, up)
    far_down = send(part.at[2, 1, :, lb], yfd, down)
    near_up = {1: send(part.at[1, 1, :, lb], ynu.at[1], up)}
    near_down = {0: send(part.at[3, 0, :, lb], ynd.at[0], down)}

    columns = [pl.ds(j * CHUNK, CHUNK) for j in range(4)]
    cot_in = [local(cot.at[:, :, columns[j]], cn.at[j]) for j in range(4)]
    wgt_in = [local(wgt.at[:, columns[j]], wv.at[j]) for j in range(4)]

    row, lane = iota((576, 128), 0), iota((576, 128), 1)
    which, slot = lax.div(row, 192), lax.div(lax.rem(row, 192), S1)
    half, first = jnp.zeros_like(row), jnp.zeros_like(row)
    for p, (d, h) in enumerate(SLOTS):
        first = jnp.where(slot == p, d, first)
        half = jnp.where(slot == p, h, half)
    second = half * 2 + lax.div(lax.rem(row, S1), S2)
    third = lax.div(lax.rem(row, S2), S3)
    at = {}
    for axis, mine in (("x", x), ("y", y), ("z", z)):
        far = jnp.zeros_like(row)
        for s in range(3):
            far = jnp.where(which == s, (first, second, third)[ORDER[s].index(axis)], far)
        at[axis] = lax.rem(far + mine, 4)
    owner = (lax.div(at["x"], 2) * 2 + core) * 32 + at["z"] * 8 + at["y"] * 2 + lax.rem(at["x"], 2)
    wanted = owner * 9 + which * S3 + lax.rem(row, S3)
    for k in range(D // 128):
        sel[:, 128 * k : 128 * k + 128] = jnp.where(wanted == lane + 128 * k, 1.0, 0.0).astype(BF16)

    def take(dy):
        x_first[dy].wait_recv()
        xa[dy] = add16(xa[dy], part[dy, 0, :, 0:XL])

    take(2)
    far_up2 = send(xa.at[2, :, l1], xfu, up)
    far_up.wait_recv()
    yfu[...] = add16(yfu[...], part[1, 0, :, XL:D])
    near_up[0] = send(yfu, ynu.at[0], up)
    far_down.wait_recv()
    yfd[...] = add16(yfd[...], part[3, 1, :, XL:D])
    near_down[1] = send(yfd, ynd.at[1], down)
    far_down2 = send(xa.at[2, :, l2], xfd, down)
    take(1)
    near_up2 = [send(xa.at[1, :, l2], xnu.at[:, l2], up)]
    take(3)
    near_down2 = [send(xa.at[3, :, l1], xnd.at[:, l1], down)]

    for j in range(4):
        cot_in[j].wait()

        @pl.loop(0, 10)
        def _(i):
            cv[j, pl.ds(pl.multiple_of(i * 16, 16), 16), :] = cn[j, pl.ds(i * 8, 8)].reshape(16, CHUNK)

        tail = jnp.concatenate([cn[j, 80].astype(F32), jnp.zeros((14, CHUNK), F32)], axis=0)
        cv[j, 160:176, :] = tail.astype(BF16)

    far_up2.wait_recv()
    xfu[...] = add16(xfu[...], xa[1, :, 0 : XL // 2])
    near_up2.append(send(xfu, xnu.at[:, l1], up))
    near_up[1].wait_recv()
    near_down[1].wait_recv()
    sb[...] = (
        part[0, 1, :, XL:D].astype(F32) + ynu[1].astype(F32) + ynd[1].astype(F32)
    ).astype(BF16)
    last_x = send(sb, yx, side)
    far_down2.wait_recv()
    xfd[...] = add16(xfd[...], xa[3, :, XL // 2 : XL])
    near_down2.append(send(xfd, xnd.at[:, l2], down))

    def keep(value, lanes):
        value = value.astype(BF16)
        pb[0:160, lanes] = value[0:160]
        tail = jnp.concatenate(
            [value[160:162].astype(F32), jnp.zeros((14, value.shape[1]), F32)], axis=0
        )
        pb[160:176, lanes] = tail.astype(BF16)

    take(0)
    for copy in near_up2 + near_down2:
        copy.wait_recv()
    keep(xa[0].astype(F32) + xnu[...].astype(F32) + xnd[...].astype(F32), slice(0, XL))
    near_up[0].wait_recv()
    near_down[0].wait_recv()
    last_x.wait_recv()
    keep(
        part[0, 0, :, XL:D].astype(F32) + ynu[0].astype(F32) + ynd[0].astype(F32) + yx[...].astype(F32),
        slice(XL, D),
    )
    pooled_twin = send(pb.at[pl.ds(0, PADDED)], pb.at[pl.ds(PADDED, PADDED)], twin)

    grad_twin = []

    def gelu_rows(values, cotangent):
        square = values * values
        t = jnp.tanh(values * (C0 + (C0 * C1) * square))
        plus = 0.5 * (1.0 + t)
        slope = plus + (0.5 * values) * (1.0 - t * t) * (C0 + (3.0 * C0 * C1) * square)
        return (values * plus).astype(BF16), (cotangent * slope).astype(BF16)

    def product(j):
        pre[j % 2] = jnp.dot(pb[0:PADDED, :], wv[j], preferred_element_type=F32)

    def forward(j):
        for i in range(11):
            rows = slice(16 * i, 16 * i + 16)
            act, grad = gelu_rows(pre[j % 2, rows, :], cv[j, rows, :].astype(F32))
            pa[j, rows, :] = act
            gr[j, rows, :] = grad

    def share(j):
        grad_twin.append(send(gr.at[j, pl.ds(0, PADDED)], gr.at[j, pl.ds(PADDED, PADDED)], twin))

    def give(j):
        for i in range(10):
            out_proj[8 * i : 8 * i + 8, :, CHUNK * j : CHUNK * j + CHUNK] = (
                pa[j, 16 * i : 16 * i + 16, :].reshape(8, 2, CHUNK)
            )
        out_proj[80, :, CHUNK * j : CHUNK * j + CHUNK] = pa[j, 160:162, :]

    msg = {}

    def wait(*names):
        for name in names:
            msg[name].wait_recv()

    def add3(a, b, c):
        return a.astype(F32) + b.astype(F32) + c.astype(F32)

    def backward(j):
        grad_twin[j].wait_recv()
        got = jnp.dot(pt[...], gr[j], preferred_element_type=F32)
        for s in range(3):
            for p in range(8):
                base = s * 192 + p * S1
                g[s, j, p] = got[base : base + S1].astype(BF16)
        for s in range(3):
            to = hop[ORDER[s][0]]
            msg["ru", s, j] = send(g.at[s, j, pl.ds(0, 2)], ru.at[s, j], to[1])
            msg["rd", s, j] = send(g.at[s, j, pl.ds(2, 2)], rd.at[s, j], to[3])

    def relay(j):
        for s in range(3):
            to = hop[ORDER[s][0]]
            wait(("ru", s, j))
            ru[s, j, 0] = add16(ru[s, j, 0], g[s, j, 4])
            msg["nu", s, j] = send(ru.at[s, j, 0], nu.at[s, j], to[1])
            wait(("rd", s, j))
            rd[s, j, 0] = add16(rd[s, j, 0], g[s, j, 5])
            msg["nd", s, j] = send(rd.at[s, j, 0], nd.at[s, j], to[3])

    def finish(j):
        for s in range(3):
            wait(("nu", s, j), ("nd", s, j))
            for h, value in enumerate(
                (add3(g[s, j, 6], nu[s, j], rd[s, j, 1]), add3(g[s, j, 7], ru[s, j, 1], nd[s, j]))
            ):
                for b in range(2):
                    r1[s, 2 * h + b, j] = value[S2 * b : S2 * b + S2].astype(BF16)

    def second_stage(q):
        steps = pl.ds(2 * q, 2)
        for d in (2, 1, 3):
            for s in range(3):
                msg["second", s, q, d] = send(r1.at[s, d, steps], in2.at[s, d, steps], hop[ORDER[s][1]][d])

    def second_finish(q):
        for s in range(3):
            wait(*(("second", s, q, d) for d in (1, 2, 3)))
            for j in (2 * q, 2 * q + 1):
                value = add3(r1[s, 0, j], in2[s, 1, j], in2[s, 3, j]) + in2[s, 2, j].astype(F32)
                for c in range(4):
                    r2[s, c, j] = value[S3 * c : S3 * c + S3].astype(BF16)

    def third_stage(q):
        steps = pl.ds(2 * q, 2)
        for s in range(3):
            to = hop[ORDER[s][2]]
            for d in (2, 1, 3):
                msg["last", s, q, d] = send(r2.at[s, d, steps], r3.at[s, d, steps], to[d])

    def owned(q):
        for s in range(3):
            wait(*(("last", s, q, d) for d in (1, 2, 3)))
            for j in (2 * q, 2 * q + 1):
                total = r2[s, 0, j].astype(F32)
                for d in (1, 2, 3):
                    total = total + r3[s, d, j].astype(F32)
                out_grad[S3 * s : S3 * s + S3, j * CHUNK : j * CHUNK + CHUNK] = total

    settle()
    for copy in wgt_in:
        copy.wait()

    def step(j):
        product(j)
        forward(j)
        share(j)

    step(0)
    step(1)
    pooled_twin.wait_recv()
    pt[...] = lax.dot_general(
        sel[...], pb[...], (((1,), (1,)), ((), ())), preferred_element_type=F32
    ).astype(BF16)
    backward(0)
    step(2)
    backward(1)
    step(3)
    relay(0)
    backward(2)
    relay(1)
    backward(3)
    relay(2)
    finish(0)
    finish(1)
    second_stage(0)
    relay(3)
    finish(2)
    give(0)
    finish(3)
    second_stage(1)
    second_finish(0)
    third_stage(0)
    give(1)
    settle()
    second_finish(1)
    third_stage(1)
    give(2)
    owned(0)
    give(3)
    owned(1)
    settle()


def hand_over(projected, weight_grad, out_projected, out_grad, sem):
    copies = [pltpu.make_async_copy(weight_grad, out_grad, sem.at[9])]
    for i in range(9):
        rows = pl.ds(9 * i, 9)
        copies.append(pltpu.make_async_copy(projected.at[rows], out_projected.at[rows], sem.at[i]))
    for copy in copies:
        copy.start()
    for copy in copies:
        copy.wait()


def per_device(features, shot_ids, band_width, proj_weight, cotangent):
    frames = jnp.swapaxes(features, 1, 2).reshape(2, TOKS * POOL, D)
    cot = cotangent.transpose(1, 2, 0, 3).reshape(TOKS, 2, H)
    vm = lambda *shape: pltpu.VMEM(shape, BF16)
    sems = lambda n: pltpu.SemaphoreType.DMA((n,))
    any_spec = pl.BlockSpec(memory_space=pl.ANY)
    vmem_spec = pl.BlockSpec(memory_space=pltpu.VMEM)
    pin = lambda space, *arrays: [pltpu.with_memory_space_constraint(a, space) for a in arrays]
    projected, weight_grad = pl.pallas_call(
        kernel,
        out_shape=(pltpu.VMEM(cot.shape, BF16), pltpu.VMEM((9, H), F32)),
        in_specs=[any_spec] * 5,
        out_specs=(vmem_spec, vmem_spec),
        scratch_shapes=[
            vm(4, D, CHUNK), vm(4, PADDED, CHUNK), vm(576, D),
            vm(2, TOKS * POOL, D), vm(4, TOKS, 2, CHUNK), vm(256, 256), vm(4, 2, ROWS, D),
            vm(4, ROWS, XL), vm(ROWS, XL // 2), vm(ROWS, XL // 2), vm(ROWS, XL), vm(ROWS, XL),
            vm(ROWS, YL), vm(ROWS, YL), vm(2, ROWS, YL), vm(2, ROWS, YL), vm(ROWS, YL), vm(ROWS, YL),
            pltpu.VMEM(shot_ids.shape, jnp.int32), pltpu.SMEM(band_width.shape, jnp.int32),
            vm(4, PADDED, CHUNK), pltpu.VMEM((2, PADDED, CHUNK), F32),
            vm(2 * PADDED, D), vm(576, 2 * PADDED), vm(4, 2 * PADDED, CHUNK),
            vm(3, 4, 8, S1, CHUNK),
            vm(3, 4, 2, S1, CHUNK), vm(3, 4, 2, S1, CHUNK), vm(3, 4, S1, CHUNK), vm(3, 4, S1, CHUNK),
            vm(3, 4, 4, S2, CHUNK), vm(3, 4, 4, S2, CHUNK),
            vm(3, 4, 4, S3, CHUNK), vm(3, 4, 4, S3, CHUNK),
            sems(12), sems(128), sems(128),
        ],
        compiler_params=pltpu.CompilerParams(
            collective_id=0, has_side_effects=True, vmem_limit_bytes=50 * 1024 * 1024
        ),
        cost_estimate=pl.CostEstimate(
            flops=4 * 10**9, bytes_accessed=14 * 10**6, transcendentals=600000
        ),
    )(*pin(pltpu.HBM, frames, proj_weight, cot, shot_ids, band_width))
    projected, weight_grad = pl.pallas_call(
        hand_over,
        out_shape=(
            jax.ShapeDtypeStruct(projected.shape, BF16),
            jax.ShapeDtypeStruct(weight_grad.shape, F32),
        ),
        in_specs=[vmem_spec, vmem_spec],
        out_specs=(any_spec, any_spec),
        scratch_shapes=[pltpu.SemaphoreType.DMA((10,))],
    )(*pin(pltpu.VMEM, projected, weight_grad))
    return projected.reshape(1, TOKS, 2, H).transpose(2, 0, 1, 3), weight_grad


def solution(mesh):
    return jax.shard_map(
        per_device,
        mesh=mesh,
        in_specs=(
            P("dp", "tm", None, None),
            P("dp", None),
            P("dp", None),
            P(),
            P("dp", "tm", None, None),
        ),
        out_specs=(P("dp", "tm", None, None), P(("dp", "tm"), None)),
        check_vma=False,
    )
```

```python
import jax
import jax.numpy as jnp
from jax import lax
from jax.experimental import pallas as pl
from jax.experimental.pallas import tpu as pltpu
from jax.sharding import PartitionSpec as P

BLOCK = 64
POOL = 8
DECAY = 16.0
F32, BF16 = jnp.float32, jnp.bfloat16
MESH = pl.DeviceIdType.MESH

D, H, TOKS = 1152, 3584, 81
ROWS = 2 * TOKS
PADDED = 176
XL = 512
YL = D - XL
CHUNK = H // 4
ORDER = (("z", "y", "x"), ("y", "x", "z"), ("x", "z", "y"))
SLOTS = tuple((d, h) for d in range(4) for h in range(2))
S1, S2, S3 = 24, 12, 3
C0 = 0.7978845608028654
C1 = 0.044715


def add16(a, b):
    return a + b


class Place:
    def __init__(self, local_sem, send_sem, recv_sem):
        dp, tm = lax.axis_index("dp"), lax.axis_index("tm")
        self.core = lax.rem(dp, 2)
        self.lo = lax.rem(tm, 2)
        self.z, self.y = lax.div(tm, 8), lax.rem(lax.div(tm, 2), 4)
        self.x = lax.div(dp, 2) * 2 + self.lo
        here = {"x": self.x, "y": self.y, "z": self.z}
        self.index = {a: [lax.rem(here[a] + d, 4) for d in range(4)] for a in "xyz"}
        self.hop = {a: [self.dev(**{a: self.index[a][d]}) for d in range(4)] for a in "xyz"}
        self.mate = self.dev(x=self.x + 1 - 2 * self.lo)
        self.twin = self.dev(core=1 - self.core)
        self.sems = local_sem, send_sem, recv_sem
        self.count = [0, 0]
        self.sends = []

    def dev(self, x=None, y=None, z=None, core=None):
        x, y, z, core = (
            mine if other is None else other
            for other, mine in ((x, self.x), (y, self.y), (z, self.z), (core, self.core))
        )
        return (lax.div(x, 2) * 2 + core, z * 8 + y * 2 + lax.rem(x, 2))

    def greet(self, friends):
        barrier = pltpu.get_barrier_semaphore()
        for friend in friends:
            pl.semaphore_signal(barrier, inc=1, device_id=friend, device_id_type=MESH)
        return lambda: pl.semaphore_wait(barrier, len(friends))

    def local(self, src, dst):
        i = self.count[0]
        self.count[0] += 1
        copy = pltpu.make_async_copy(src, dst, self.sems[0].at[i])
        copy.start()
        return copy

    def send(self, src, dst, to):
        i = self.count[1]
        self.count[1] += 1
        copy = pltpu.make_async_remote_copy(
            src_ref=src, dst_ref=dst, send_sem=self.sems[1].at[i], recv_sem=self.sems[2].at[i],
            device_id=to, device_id_type=MESH,
        )
        copy.start()
        self.sends.append(copy)
        return copy

    def settle(self):
        for copy in self.sends:
            copy.wait_send()
        self.sends.clear()


def iota(shape, axis):
    return lax.broadcasted_iota(jnp.int32, shape, axis)


def kernel(
    feat, wgt, cot, shots_in, band_in,
    out_proj, out_grad,
    wv, cv, sel, fv, cn, kron, part,
    xa, xfu, xfd, xnu, xnd, yfu, yfd, ynu, ynd, sb, yx,
    ids_v, band_s,
    pa, pre, pb, pt, gr, g,
    in1, r1, in2, r2, r3,
    local_sem, send_sem, recv_sem,
):
    here = Place(local_sem, send_sem, recv_sem)
    core, x, y, z, lo = here.core, here.x, here.y, here.z, here.lo
    hop, local, send, settle, twin = here.hop, here.local, here.send, here.settle, here.twin
    la, lb = pl.ds(0, XL), pl.ds(XL, YL)
    ids_in = local(shots_in, ids_v)
    width_in = local(band_in, band_s)
    feat_a = local(feat.at[:, :, la], fv.at[:, :, la])
    feat_b = local(feat.at[:, :, lb], fv.at[:, :, lb])

    everybody = here.greet([hop[a][d] for a in "xyz" for d in (1, 2, 3)] + [twin])

    frame, other = iota((BLOCK, 128), 0), iota((BLOCK, 128), 1)
    distance = jnp.abs(frame - other)
    decay = jnp.exp(-distance.astype(F32) / DECAY)
    ids_in.wait()
    width_in.wait()
    ids = ids_v[...].astype(F32)
    ids = jnp.where(z < 2, ids[:, 0:128], ids[:, 128:256])
    ids = jnp.where(lax.rem(z, 2) == 0, ids, pltpu.roll(ids, 64, 1))
    target_of = iota((256, 128), 0)
    rel = lax.div(target_of, 32)
    target_of = lax.rem(y + lax.div(rel, 2), 4) * 2 + jnp.where(lax.rem(rel, 2) == 0, lo, 1 - lo)
    own_frame = jnp.where(iota((128, 256), 0) == (y * 2 + lo) * POOL + lax.rem(iota((128, 256), 1), 8), 1.0, 0.0)
    own_frame = own_frame.astype(BF16)
    out_row, in_row = iota((256, 256), 0), iota((256, 256), 1)
    same_token = lax.div(lax.rem(out_row, 32), 2) == lax.div(lax.rem(in_row, 128), 8)
    spread = jnp.zeros((256, 256), F32)
    for v in range(2):
        along = jnp.broadcast_to(ids[v : v + 1], (BLOCK, 128))
        down_ids = jnp.sum(jnp.where(frame == other, along, 0.0), axis=1, keepdims=True)
        allowed = (along == down_ids) & (distance <= band_s[v, z]) & (other < BLOCK)
        raw = jnp.where(allowed, decay, 0.0)
        mix = (raw / jnp.sum(raw, axis=1, keepdims=True)).astype(BF16).astype(F32)
        combined = (mix.reshape(8, POOL, 128).sum(axis=1) * 0.125).astype(BF16).astype(F32)
        rows = jnp.zeros((256, 128), F32)
        for p in range(8):
            rows = jnp.where(target_of == p, combined[p : p + 1], rows)
        full = jnp.dot(rows.astype(BF16), own_frame, preferred_element_type=F32)
        mine_too = same_token & (lax.rem(out_row, 2) == v) & (lax.div(in_row, 128) == v)
        spread = jnp.where(mine_too, full, spread)
    kron[...] = spread.astype(BF16)

    def partial_sums(lanes):
        for c in range(6):
            if c < 5:
                blocks = [fv[v, 128 * c : 128 * c + 128, lanes] for v in range(2)]
            else:
                empty = jnp.zeros((120, lanes.stop - lanes.start), BF16)
                blocks = [b for v in range(2) for b in (fv[v, 640:648, lanes], empty)]
            got = jnp.dot(kron[...], jnp.concatenate(blocks, axis=0), preferred_element_type=F32)
            size = 32 if c < 5 else 2
            for r in range(8):
                part[r // 2, r % 2, 32 * c : 32 * c + size, lanes] = got[32 * r : 32 * r + size].astype(BF16)

    l1, l2 = pl.ds(0, XL // 2), pl.ds(XL // 2, XL // 2)
    up, down, side = hop["y"][1], hop["y"][3], here.mate

    feat_a.wait()
    partial_sums(slice(0, XL))
    everybody()
    x_first = {dy: send(part.at[dy, 1, :, la], xa.at[dy], side) for dy in (2, 1, 3, 0)}
    feat_b.wait()
    partial_sums(slice(XL, D))
    far_up = send(part.at[2, 0, :, lb], yfu, up)
    far_down = send(part.at[2, 1, :, lb], yfd, down)
    near_up = {1: send(part.at[1, 1, :, lb], ynu.at[1], up)}
    near_down = {0: send(part.at[3, 0, :, lb], ynd.at[0], down)}

    columns = [pl.ds(j * CHUNK, CHUNK) for j in range(4)]
    cot_in = [local(cot.at[:, :, columns[j]], cn.at[j]) for j in range(4)]
    wgt_in = [local(wgt.at[:, columns[j]], wv.at[j]) for j in range(4)]

    row, lane = iota((576, 128), 0), iota((576, 128), 1)
    which, slot = lax.div(row, 192), lax.div(lax.rem(row, 192), S1)
    half, first = jnp.zeros_like(row), jnp.zeros_like(row)
    for p, (d, h) in enumerate(SLOTS):
        first = jnp.where(slot == p, d, first)
        half = jnp.where(slot == p, h, half)
    second = half * 2 + lax.div(lax.rem(row, S1), S2)
    third = lax.div(lax.rem(row, S2), S3)
    at = {}
    for axis, mine in (("x", x), ("y", y), ("z", z)):
        far = jnp.zeros_like(row)
        for s in range(3):
            far = jnp.where(which == s, (first, second, third)[ORDER[s].index(axis)], far)
        at[axis] = lax.rem(far + mine, 4)
    owner = (lax.div(at["x"], 2) * 2 + core) * 32 + at["z"] * 8 + at["y"] * 2 + lax.rem(at["x"], 2)
    wanted = owner * 9 + which * S3 + lax.rem(row, S3)
    for k in range(D // 128):
        sel[:, 128 * k : 128 * k + 128] = jnp.where(wanted == lane + 128 * k, 1.0, 0.0).astype(BF16)

    def take(dy):
        x_first[dy].wait_recv()
        xa[dy] = add16(xa[dy], part[dy, 0, :, 0:XL])

    take(2)
    far_up2 = send(xa.at[2, :, l1], xfu, up)
    far_up.wait_recv()
    yfu[...] = add16(yfu[...], part[1, 0, :, XL:D])
    near_up[0] = send(yfu, ynu.at[0], up)
    far_down.wait_recv()
    yfd[...] = add16(yfd[...], part[3, 1, :, XL:D])
    near_down[1] = send(yfd, ynd.at[1], down)
    far_down2 = send(xa.at[2, :, l2], xfd, down)
    take(1)
    near_up2 = [send(xa.at[1, :, l2], xnu.at[:, l2], up)]
    take(3)
    near_down2 = [send(xa.at[3, :, l1], xnd.at[:, l1], down)]

    for j in range(4):
        cot_in[j].wait()

        @pl.loop(0, 10)
        def _(i):
            cv[j, pl.ds(pl.multiple_of(i * 16, 16), 16), :] = cn[j, pl.ds(i * 8, 8)].reshape(16, CHUNK)

        tail = jnp.concatenate([cn[j, 80].astype(F32), jnp.zeros((14, CHUNK), F32)], axis=0)
        cv[j, 160:176, :] = tail.astype(BF16)

    far_up2.wait_recv()
    xfu[...] = add16(xfu[...], xa[1, :, 0 : XL // 2])
    near_up2.append(send(xfu, xnu.at[:, l1], up))
    near_up[1].wait_recv()
    near_down[1].wait_recv()
    sb[...] = (
        part[0, 1, :, XL:D].astype(F32) + ynu[1].astype(F32) + ynd[1].astype(F32)
    ).astype(BF16)
    last_x = send(sb, yx, side)
    far_down2.wait_recv()
    xfd[...] = add16(xfd[...], xa[3, :, XL // 2 : XL])
    near_down2.append(send(xfd, xnd.at[:, l2], down))

    def keep(value, lanes):
        value = value.astype(BF16)
        pb[0:160, lanes] = value[0:160]
        tail = jnp.concatenate(
            [value[160:162].astype(F32), jnp.zeros((14, value.shape[1]), F32)], axis=0
        )
        pb[160:176, lanes] = tail.astype(BF16)

    take(0)
    for copy in near_up2 + near_down2:
        copy.wait_recv()
    keep(xa[0].astype(F32) + xnu[...].astype(F32) + xnd[...].astype(F32), slice(0, XL))
    near_up[0].wait_recv()
    near_down[0].wait_recv()
    last_x.wait_recv()
    keep(
        part[0, 0, :, XL:D].astype(F32) + ynu[0].astype(F32) + ynd[0].astype(F32) + yx[...].astype(F32),
        slice(XL, D),
    )
    pooled_twin = send(pb.at[pl.ds(0, PADDED)], pb.at[pl.ds(PADDED, PADDED)], twin)

    grad_twin = []

    def gelu_rows(values, cotangent):
        square = values * values
        t = jnp.tanh(values * (C0 + (C0 * C1) * square))
        plus = 0.5 * (1.0 + t)
        slope = plus + (0.5 * values) * (1.0 - t * t) * (C0 + (3.0 * C0 * C1) * square)
        return (values * plus).astype(BF16), (cotangent * slope).astype(BF16)

    def product(j):
        pre[j % 2] = jnp.dot(pb[0:PADDED, :], wv[j], preferred_element_type=F32)

    def forward(j):
        for i in range(11):
            rows = slice(16 * i, 16 * i + 16)
            act, grad = gelu_rows(pre[j % 2, rows, :], cv[j, rows, :].astype(F32))
            pa[j, rows, :] = act
            gr[j, rows, :] = grad

    def share(j):
        grad_twin.append(send(gr.at[j, pl.ds(0, PADDED)], gr.at[j, pl.ds(PADDED, PADDED)], twin))

    def give(j):
        for i in range(10):
            out_proj[8 * i : 8 * i + 8, :, CHUNK * j : CHUNK * j + CHUNK] = (
                pa[j, 16 * i : 16 * i + 16, :].reshape(8, 2, CHUNK)
            )
        out_proj[80, :, CHUNK * j : CHUNK * j + CHUNK] = pa[j, 160:162, :]

    msg = {}

    def wait(*names):
        for name in names:
            msg[name].wait_recv()

    def add3(a, b, c):
        return a.astype(F32) + b.astype(F32) + c.astype(F32)

    def backward(j):
        grad_twin[j].wait_recv()
        got = jnp.dot(pt[...], gr[j], preferred_element_type=F32)
        for s in range(3):
            for p in range(8):
                base = s * 192 + p * S1
                g[s, j, p] = got[base : base + S1].astype(BF16)
        for d in (2, 1, 3):
            for s in range(3):
                to = hop[ORDER[s][0]][d]
                msg["first", s, j, d] = send(g.at[s, j, pl.ds(2 * d, 2)], in1.at[s, j, d], to)

    def finish(j):
        for s in range(3):
            wait(*(("first", s, j, d) for d in (1, 2, 3)))
            for h in range(2):
                value = add3(g[s, j, h], in1[s, j, 1, h], in1[s, j, 3, h]) + in1[s, j, 2, h].astype(F32)
                for b in range(2):
                    r1[s, 2 * h + b, j] = value[S2 * b : S2 * b + S2].astype(BF16)

    def second_stage(q):
        steps = pl.ds(2 * q, 2)
        for d in (2, 1, 3):
            for s in range(3):
                msg["second", s, q, d] = send(r1.at[s, d, steps], in2.at[s, d, steps], hop[ORDER[s][1]][d])

    def second_finish(q):
        for s in range(3):
            wait(*(("second", s, q, d) for d in (1, 2, 3)))
            for j in (2 * q, 2 * q + 1):
                value = add3(r1[s, 0, j], in2[s, 1, j], in2[s, 3, j]) + in2[s, 2, j].astype(F32)
                for c in range(4):
                    r2[s, c, j] = value[S3 * c : S3 * c + S3].astype(BF16)

    def third_stage(q):
        steps = pl.ds(2 * q, 2)
        for s in range(3):
            to = hop[ORDER[s][2]]
            for d in (2, 1, 3):
                msg["last", s, q, d] = send(r2.at[s, d, steps], r3.at[s, d, steps], to[d])

    def owned(q):
        for s in range(3):
            wait(*(("last", s, q, d) for d in (1, 2, 3)))
            for j in (2 * q, 2 * q + 1):
                total = r2[s, 0, j].astype(F32)
                for d in (1, 2, 3):
                    total = total + r3[s, d, j].astype(F32)
                out_grad[S3 * s : S3 * s + S3, j * CHUNK : j * CHUNK + CHUNK] = total

    settle()
    for copy in wgt_in:
        copy.wait()

    def step(j):
        product(j)
        forward(j)
        share(j)

    step(0)
    step(1)
    pooled_twin.wait_recv()
    pt[...] = lax.dot_general(
        sel[...], pb[...], (((1,), (1,)), ((), ())), preferred_element_type=F32
    ).astype(BF16)
    backward(0)
    step(2)
    backward(1)
    step(3)
    backward(2)
    backward(3)
    finish(0)
    finish(1)
    second_stage(0)
    finish(2)
    give(0)
    finish(3)
    second_stage(1)
    second_finish(0)
    third_stage(0)
    give(1)
    settle()
    second_finish(1)
    third_stage(1)
    give(2)
    owned(0)
    give(3)
    owned(1)
    settle()


def hand_over(projected, weight_grad, out_projected, out_grad, sem):
    copies = [pltpu.make_async_copy(weight_grad, out_grad, sem.at[9])]
    for i in range(9):
        rows = pl.ds(9 * i, 9)
        copies.append(pltpu.make_async_copy(projected.at[rows], out_projected.at[rows], sem.at[i]))
    for copy in copies:
        copy.start()
    for copy in copies:
        copy.wait()


def per_device(features, shot_ids, band_width, proj_weight, cotangent):
    frames = jnp.swapaxes(features, 1, 2).reshape(2, TOKS * POOL, D)
    cot = cotangent.transpose(1, 2, 0, 3).reshape(TOKS, 2, H)
    vm = lambda *shape: pltpu.VMEM(shape, BF16)
    sems = lambda n: pltpu.SemaphoreType.DMA((n,))
    any_spec = pl.BlockSpec(memory_space=pl.ANY)
    vmem_spec = pl.BlockSpec(memory_space=pltpu.VMEM)
    pin = lambda space, *arrays: [pltpu.with_memory_space_constraint(a, space) for a in arrays]
    projected, weight_grad = pl.pallas_call(
        kernel,
        out_shape=(pltpu.VMEM(cot.shape, BF16), pltpu.VMEM((9, H), F32)),
        in_specs=[any_spec] * 5,
        out_specs=(vmem_spec, vmem_spec),
        scratch_shapes=[
            vm(4, D, CHUNK), vm(4, PADDED, CHUNK), vm(576, D),
            vm(2, TOKS * POOL, D), vm(4, TOKS, 2, CHUNK), vm(256, 256), vm(4, 2, ROWS, D),
            vm(4, ROWS, XL), vm(ROWS, XL // 2), vm(ROWS, XL // 2), vm(ROWS, XL), vm(ROWS, XL),
            vm(ROWS, YL), vm(ROWS, YL), vm(2, ROWS, YL), vm(2, ROWS, YL), vm(ROWS, YL), vm(ROWS, YL),
            pltpu.VMEM(shot_ids.shape, jnp.int32), pltpu.SMEM(band_width.shape, jnp.int32),
            vm(4, PADDED, CHUNK), pltpu.VMEM((2, PADDED, CHUNK), F32),
            vm(2 * PADDED, D), vm(576, 2 * PADDED), vm(4, 2 * PADDED, CHUNK),
            vm(3, 4, 8, S1, CHUNK),
            vm(3, 4, 4, 2, S1, CHUNK),
            vm(3, 4, 4, S2, CHUNK), vm(3, 4, 4, S2, CHUNK),
            vm(3, 4, 4, S3, CHUNK), vm(3, 4, 4, S3, CHUNK),
            sems(12), sems(128), sems(128),
        ],
        compiler_params=pltpu.CompilerParams(
            collective_id=0, has_side_effects=True, vmem_limit_bytes=50 * 1024 * 1024
        ),
        cost_estimate=pl.CostEstimate(
            flops=4 * 10**9, bytes_accessed=14 * 10**6, transcendentals=600000
        ),
    )(*pin(pltpu.HBM, frames, proj_weight, cot, shot_ids, band_width))
    projected, weight_grad = pl.pallas_call(
        hand_over,
        out_shape=(
            jax.ShapeDtypeStruct(projected.shape, BF16),
            jax.ShapeDtypeStruct(weight_grad.shape, F32),
        ),
        in_specs=[vmem_spec, vmem_spec],
        out_specs=(any_spec, any_spec),
        scratch_shapes=[pltpu.SemaphoreType.DMA((10,))],
    )(*pin(pltpu.VMEM, projected, weight_grad))
    return projected.reshape(1, TOKS, 2, H).transpose(2, 0, 1, 3), weight_grad


def solution(mesh):
    return jax.shard_map(
        per_device,
        mesh=mesh,
        in_specs=(
            P("dp", "tm", None, None),
            P("dp", None),
            P("dp", None),
            P(),
            P("dp", "tm", None, None),
        ),
        out_specs=(P("dp", "tm", None, None), P(("dp", "tm"), None)),
        check_vma=False,
    )
```

```python
import jax
import jax.numpy as jnp
from jax import lax
from jax.experimental import pallas as pl
from jax.experimental.pallas import tpu as pltpu
from jax.sharding import PartitionSpec as P

BLOCK = 64
POOL = 8
DECAY = 16.0
F32, BF16 = jnp.float32, jnp.bfloat16
MESH = pl.DeviceIdType.MESH

D, H, TOKS = 1152, 3584, 81
ROWS = 2 * TOKS
PADDED = 176
XL = 512
YL = D - XL
CHUNK = H // 4
ORDER = (("z", "y", "x"), ("y", "x", "z"), ("x", "z", "y"))
SLOTS = ((2, 0), (1, 1), (2, 1), (3, 0), (1, 0), (3, 1), (0, 0), (0, 1))
S1, S2, S3 = 24, 12, 3
C0 = 0.7978845608028654
C1 = 0.044715


def add16(a, b):
    return a + b


class Place:
    def __init__(self, local_sem, send_sem, recv_sem):
        dp, tm = lax.axis_index("dp"), lax.axis_index("tm")
        self.core = lax.rem(dp, 2)
        self.lo = lax.rem(tm, 2)
        self.z, self.y = lax.div(tm, 8), lax.rem(lax.div(tm, 2), 4)
        self.x = lax.div(dp, 2) * 2 + self.lo
        here = {"x": self.x, "y": self.y, "z": self.z}
        self.index = {a: [lax.rem(here[a] + d, 4) for d in range(4)] for a in "xyz"}
        self.hop = {a: [self.dev(**{a: self.index[a][d]}) for d in range(4)] for a in "xyz"}
        self.mate = self.dev(x=self.x + 1 - 2 * self.lo)
        self.twin = self.dev(core=1 - self.core)
        self.sems = local_sem, send_sem, recv_sem
        self.count = [0, 0]
        self.sends = []

    def dev(self, x=None, y=None, z=None, core=None):
        x, y, z, core = (
            mine if other is None else other
            for other, mine in ((x, self.x), (y, self.y), (z, self.z), (core, self.core))
        )
        return (lax.div(x, 2) * 2 + core, z * 8 + y * 2 + lax.rem(x, 2))

    def greet(self, friends):
        barrier = pltpu.get_barrier_semaphore()
        for friend in friends:
            pl.semaphore_signal(barrier, inc=1, device_id=friend, device_id_type=MESH)
        return lambda: pl.semaphore_wait(barrier, len(friends))

    def local(self, src, dst):
        i = self.count[0]
        self.count[0] += 1
        copy = pltpu.make_async_copy(src, dst, self.sems[0].at[i])
        copy.start()
        return copy

    def send(self, src, dst, to):
        i = self.count[1]
        self.count[1] += 1
        copy = pltpu.make_async_remote_copy(
            src_ref=src, dst_ref=dst, send_sem=self.sems[1].at[i], recv_sem=self.sems[2].at[i],
            device_id=to, device_id_type=MESH,
        )
        copy.start()
        self.sends.append(copy)
        return copy

    def settle(self):
        for copy in self.sends:
            copy.wait_send()
        self.sends.clear()


def iota(shape, axis):
    return lax.broadcasted_iota(jnp.int32, shape, axis)


def kernel(
    feat, wgt, cot, shots_in, band_in,
    out_proj, out_grad,
    wv, cv, sel, fv, cn, kron, part,
    xa, xfu, xfd, xnu, xnd, yfu, yfd, ynu, ynd, sb, yx,
    ids_v, band_s,
    pa, pre, pb, pt, gr, g,
    ru, rd, nu, nd, r1, in2, r2, r3,
    local_sem, send_sem, recv_sem,
):
    here = Place(local_sem, send_sem, recv_sem)
    core, x, y, z, lo = here.core, here.x, here.y, here.z, here.lo
    hop, local, send, settle, twin = here.hop, here.local, here.send, here.settle, here.twin
    la, lb = pl.ds(0, XL), pl.ds(XL, YL)
    ids_in = local(shots_in, ids_v)
    width_in = local(band_in, band_s)
    feat_a = local(feat.at[:, :, la], fv.at[:, :, la])
    feat_b = local(feat.at[:, :, lb], fv.at[:, :, lb])

    everybody = here.greet([hop[a][d] for a in "xyz" for d in (1, 2, 3)] + [twin])

    frame, other = iota((BLOCK, 128), 0), iota((BLOCK, 128), 1)
    distance = jnp.abs(frame - other)
    decay = jnp.exp(-distance.astype(F32) / DECAY)
    ids_in.wait()
    width_in.wait()
    ids = ids_v[...].astype(F32)
    ids = jnp.where(z < 2, ids[:, 0:128], ids[:, 128:256])
    ids = jnp.where(lax.rem(z, 2) == 0, ids, pltpu.roll(ids, 64, 1))
    target_of = iota((256, 128), 0)
    rel = lax.div(target_of, 32)
    target_of = lax.rem(y + lax.div(rel, 2), 4) * 2 + jnp.where(lax.rem(rel, 2) == 0, lo, 1 - lo)
    own_frame = jnp.where(iota((128, 256), 0) == (y * 2 + lo) * POOL + lax.rem(iota((128, 256), 1), 8), 1.0, 0.0)
    own_frame = own_frame.astype(BF16)
    out_row, in_row = iota((256, 256), 0), iota((256, 256), 1)
    same_token = lax.div(lax.rem(out_row, 32), 2) == lax.div(lax.rem(in_row, 128), 8)
    spread = jnp.zeros((256, 256), F32)
    for v in range(2):
        along = jnp.broadcast_to(ids[v : v + 1], (BLOCK, 128))
        down_ids = jnp.sum(jnp.where(frame == other, along, 0.0), axis=1, keepdims=True)
        allowed = (along == down_ids) & (distance <= band_s[v, z]) & (other < BLOCK)
        raw = jnp.where(allowed, decay, 0.0)
        mix = (raw / jnp.sum(raw, axis=1, keepdims=True)).astype(BF16).astype(F32)
        combined = (mix.reshape(8, POOL, 128).sum(axis=1) * 0.125).astype(BF16).astype(F32)
        rows = jnp.zeros((256, 128), F32)
        for p in range(8):
            rows = jnp.where(target_of == p, combined[p : p + 1], rows)
        full = jnp.dot(rows.astype(BF16), own_frame, preferred_element_type=F32)
        mine_too = same_token & (lax.rem(out_row, 2) == v) & (lax.div(in_row, 128) == v)
        spread = jnp.where(mine_too, full, spread)
    kron[...] = spread.astype(BF16)

    def partial_sums(lanes):
        for c in range(6):
            if c < 5:
                blocks = [fv[v, 128 * c : 128 * c + 128, lanes] for v in range(2)]
            else:
                empty = jnp.zeros((120, lanes.stop - lanes.start), BF16)
                blocks = [b for v in range(2) for b in (fv[v, 640:648, lanes], empty)]
            got = jnp.dot(kron[...], jnp.concatenate(blocks, axis=0), preferred_element_type=F32)
            size = 32 if c < 5 else 2
            for r in range(8):
                part[r // 2, r % 2, 32 * c : 32 * c + size, lanes] = got[32 * r : 32 * r + size].astype(BF16)

    l1, l2 = pl.ds(0, XL // 2), pl.ds(XL // 2, XL // 2)
    up, down, side = hop["y"][1], hop["y"][3], here.mate

    feat_a.wait()
    partial_sums(slice(0, XL))
    everybody()
    x_first = {dy: send(part.at[dy, 1, :, la], xa.at[dy], side) for dy in (2, 1, 3, 0)}
    feat_b.wait()
    partial_sums(slice(XL, D))
    far_up = send(part.at[2, 0, :, lb], yfu, up)
    far_down = send(part.at[2, 1, :, lb], yfd, down)
    near_up = {1: send(part.at[1, 1, :, lb], ynu.at[1], up)}
    near_down = {0: send(part.at[3, 0, :, lb], ynd.at[0], down)}

    columns = [pl.ds(j * CHUNK, CHUNK) for j in range(4)]
    cot_in = [local(cot.at[:, :, columns[j]], cn.at[j]) for j in range(4)]
    wgt_in = [local(wgt.at[:, columns[j]], wv.at[j]) for j in range(4)]

    row, lane = iota((576, 128), 0), iota((576, 128), 1)
    which, slot = lax.div(row, 192), lax.div(lax.rem(row, 192), S1)
    half, first = jnp.zeros_like(row), jnp.zeros_like(row)
    for p, (d, h) in enumerate(SLOTS):
        first = jnp.where(slot == p, d, first)
        half = jnp.where(slot == p, h, half)
    second = half * 2 + lax.div(lax.rem(row, S1), S2)
    third = lax.div(lax.rem(row, S2), S3)
    at = {}
    for axis, mine in (("x", x), ("y", y), ("z", z)):
        far = jnp.zeros_like(row)
        for s in range(3):
            far = jnp.where(which == s, (first, second, third)[ORDER[s].index(axis)], far)
        at[axis] = lax.rem(far + mine, 4)
    owner = (lax.div(at["x"], 2) * 2 + core) * 32 + at["z"] * 8 + at["y"] * 2 + lax.rem(at["x"], 2)
    wanted = owner * 9 + which * S3 + lax.rem(row, S3)
    for k in range(D // 128):
        sel[:, 128 * k : 128 * k + 128] = jnp.where(wanted == lane + 128 * k, 1.0, 0.0).astype(BF16)

    def take(dy):
        x_first[dy].wait_recv()
        xa[dy] = add16(xa[dy], part[dy, 0, :, 0:XL])

    take(2)
    far_up2 = send(xa.at[2, :, l1], xfu, up)
    far_up.wait_recv()
    yfu[...] = add16(yfu[...], part[1, 0, :, XL:D])
    near_up[0] = send(yfu, ynu.at[0], up)
    far_down.wait_recv()
    yfd[...] = add16(yfd[...], part[3, 1, :, XL:D])
    near_down[1] = send(yfd, ynd.at[1], down)
    far_down2 = send(xa.at[2, :, l2], xfd, down)
    take(1)
    near_up2 = [send(xa.at[1, :, l2], xnu.at[:, l2], up)]
    take(3)
    near_down2 = [send(xa.at[3, :, l1], xnd.at[:, l1], down)]

    for j in range(4):
        cot_in[j].wait()

        @pl.loop(0, 10)
        def _(i):
            cv[j, pl.ds(pl.multiple_of(i * 16, 16), 16), :] = cn[j, pl.ds(i * 8, 8)].reshape(16, CHUNK)

        tail = jnp.concatenate([cn[j, 80].astype(F32), jnp.zeros((14, CHUNK), F32)], axis=0)
        cv[j, 160:176, :] = tail.astype(BF16)

    far_up2.wait_recv()
    xfu[...] = add16(xfu[...], xa[1, :, 0 : XL // 2])
    near_up2.append(send(xfu, xnu.at[:, l1], up))
    near_up[1].wait_recv()
    near_down[1].wait_recv()
    sb[...] = (
        part[0, 1, :, XL:D].astype(F32) + ynu[1].astype(F32) + ynd[1].astype(F32)
    ).astype(BF16)
    last_x = send(sb, yx, side)
    far_down2.wait_recv()
    xfd[...] = add16(xfd[...], xa[3, :, XL // 2 : XL])
    near_down2.append(send(xfd, xnd.at[:, l2], down))

    def keep(value, lanes):
        value = value.astype(BF16)
        pb[0:160, lanes] = value[0:160]
        tail = jnp.concatenate(
            [value[160:162].astype(F32), jnp.zeros((14, value.shape[1]), F32)], axis=0
        )
        pb[160:176, lanes] = tail.astype(BF16)

    take(0)
    for copy in near_up2 + near_down2:
        copy.wait_recv()
    keep(xa[0].astype(F32) + xnu[...].astype(F32) + xnd[...].astype(F32), slice(0, XL))
    near_up[0].wait_recv()
    near_down[0].wait_recv()
    last_x.wait_recv()
    keep(
        part[0, 0, :, XL:D].astype(F32) + ynu[0].astype(F32) + ynd[0].astype(F32) + yx[...].astype(F32),
        slice(XL, D),
    )
    pooled_twin = send(pb.at[pl.ds(0, PADDED)], pb.at[pl.ds(PADDED, PADDED)], twin)

    grad_twin = []

    def gelu_rows(values, cotangent):
        square = values * values
        t = jnp.tanh(values * (C0 + (C0 * C1) * square))
        plus = 0.5 * (1.0 + t)
        slope = plus + (0.5 * values) * (1.0 - t * t) * (C0 + (3.0 * C0 * C1) * square)
        return (values * plus).astype(BF16), (cotangent * slope).astype(BF16)

    def product(j):
        pre[j % 2] = jnp.dot(pb[0:PADDED, :], wv[j], preferred_element_type=F32)

    def forward(j):
        for i in range(11):
            rows = slice(16 * i, 16 * i + 16)
            act, grad = gelu_rows(pre[j % 2, rows, :], cv[j, rows, :].astype(F32))
            pa[j, rows, :] = act
            gr[j, rows, :] = grad

    def share(j):
        grad_twin.append(send(gr.at[j, pl.ds(0, PADDED)], gr.at[j, pl.ds(PADDED, PADDED)], twin))

    def give(j):
        for i in range(10):
            out_proj[8 * i : 8 * i + 8, :, CHUNK * j : CHUNK * j + CHUNK] = (
                pa[j, 16 * i : 16 * i + 16, :].reshape(8, 2, CHUNK)
            )
        out_proj[80, :, CHUNK * j : CHUNK * j + CHUNK] = pa[j, 160:162, :]

    msg = {}

    def wait(*names):
        for name in names:
            msg[name].wait_recv()

    def add3(a, b, c):
        return a.astype(F32) + b.astype(F32) + c.astype(F32)

    def backward(j):
        grad_twin[j].wait_recv()
        got = jnp.dot(pt[...], gr[j], preferred_element_type=F32)
        for s in range(3):
            for p in range(8):
                base = s * 192 + p * S1
                g[s, j, p] = got[base : base + S1].astype(BF16)
        for s in range(3):
            to = hop[ORDER[s][0]]
            msg["ru", s, j] = send(g.at[s, j, pl.ds(0, 2)], ru.at[s, j], to[1])
            msg["rd", s, j] = send(g.at[s, j, pl.ds(2, 2)], rd.at[s, j], to[3])

    def relay(j):
        for s in range(3):
            to = hop[ORDER[s][0]]
            wait(("ru", s, j))
            ru[s, j, 0] = add16(ru[s, j, 0], g[s, j, 4])
            msg["nu", s, j] = send(ru.at[s, j, 0], nu.at[s, j], to[1])
            wait(("rd", s, j))
            rd[s, j, 0] = add16(rd[s, j, 0], g[s, j, 5])
            msg["nd", s, j] = send(rd.at[s, j, 0], nd.at[s, j], to[3])

    def finish(j):
        for s in range(3):
            wait(("nu", s, j), ("nd", s, j))
            for h, value in enumerate(
                (add3(g[s, j, 6], nu[s, j], rd[s, j, 1]), add3(g[s, j, 7], ru[s, j, 1], nd[s, j]))
            ):
                for b in range(2):
                    r1[s, 2 * h + b, j] = value[S2 * b : S2 * b + S2].astype(BF16)

    def second_stage(q):
        steps = pl.ds(2 * q, 2)
        for d in (2, 1, 3):
            for s in range(3):
                msg["second", s, q, d] = send(r1.at[s, d, steps], in2.at[s, d, steps], hop[ORDER[s][1]][d])

    def second_finish(q):
        for s in range(3):
            wait(*(("second", s, q, d) for d in (1, 2, 3)))
            for j in (2 * q, 2 * q + 1):
                value = add3(r1[s, 0, j], in2[s, 1, j], in2[s, 3, j]) + in2[s, 2, j].astype(F32)
                for c in range(4):
                    r2[s, c, j] = value[S3 * c : S3 * c + S3].astype(BF16)

    def third_stage(q):
        steps = pl.ds(2 * q, 2)
        for s in range(3):
            to = hop[ORDER[s][2]]
            for d in (2, 1, 3):
                msg["last", s, q, d] = send(r2.at[s, d, steps], r3.at[s, d, steps], to[d])

    def owned(q):
        for s in range(3):
            wait(*(("last", s, q, d) for d in (1, 2, 3)))
            for j in (2 * q, 2 * q + 1):
                total = r2[s, 0, j].astype(F32)
                for d in (1, 2, 3):
                    total = total + r3[s, d, j].astype(F32)
                out_grad[S3 * s : S3 * s + S3, j * CHUNK : j * CHUNK + CHUNK] = total

    settle()
    for copy in wgt_in:
        copy.wait()

    def step(j):
        product(j)
        forward(j)
        share(j)

    step(0)
    pooled_twin.wait_recv()
    pt[...] = lax.dot_general(
        sel[...], pb[...], (((1,), (1,)), ((), ())), preferred_element_type=F32
    ).astype(BF16)
    backward(0)
    step(1)
    step(2)
    backward(1)
    relay(0)
    step(3)
    backward(2)
    relay(1)
    backward(3)
    relay(2)
    finish(0)
    finish(1)
    second_stage(0)
    relay(3)
    finish(2)
    give(0)
    finish(3)
    second_stage(1)
    second_finish(0)
    third_stage(0)
    give(1)
    settle()
    second_finish(1)
    third_stage(1)
    give(2)
    owned(0)
    give(3)
    owned(1)
    settle()


def hand_over(projected, weight_grad, out_projected, out_grad, sem):
    copies = [pltpu.make_async_copy(weight_grad, out_grad, sem.at[9])]
    for i in range(9):
        rows = pl.ds(9 * i, 9)
        copies.append(pltpu.make_async_copy(projected.at[rows], out_projected.at[rows], sem.at[i]))
    for copy in copies:
        copy.start()
    for copy in copies:
        copy.wait()


def per_device(features, shot_ids, band_width, proj_weight, cotangent):
    frames = jnp.swapaxes(features, 1, 2).reshape(2, TOKS * POOL, D)
    cot = cotangent.transpose(1, 2, 0, 3).reshape(TOKS, 2, H)
    vm = lambda *shape: pltpu.VMEM(shape, BF16)
    sems = lambda n: pltpu.SemaphoreType.DMA((n,))
    any_spec = pl.BlockSpec(memory_space=pl.ANY)
    vmem_spec = pl.BlockSpec(memory_space=pltpu.VMEM)
    pin = lambda space, *arrays: [pltpu.with_memory_space_constraint(a, space) for a in arrays]
    projected, weight_grad = pl.pallas_call(
        kernel,
        out_shape=(pltpu.VMEM(cot.shape, BF16), pltpu.VMEM((9, H), F32)),
        in_specs=[any_spec] * 5,
        out_specs=(vmem_spec, vmem_spec),
        scratch_shapes=[
            vm(4, D, CHUNK), vm(4, PADDED, CHUNK), vm(576, D),
            vm(2, TOKS * POOL, D), vm(4, TOKS, 2, CHUNK), vm(256, 256), vm(4, 2, ROWS, D),
            vm(4, ROWS, XL), vm(ROWS, XL // 2), vm(ROWS, XL // 2), vm(ROWS, XL), vm(ROWS, XL),
            vm(ROWS, YL), vm(ROWS, YL), vm(2, ROWS, YL), vm(2, ROWS, YL), vm(ROWS, YL), vm(ROWS, YL),
            pltpu.VMEM(shot_ids.shape, jnp.int32), pltpu.SMEM(band_width.shape, jnp.int32),
            vm(4, PADDED, CHUNK), pltpu.VMEM((2, PADDED, CHUNK), F32),
            vm(2 * PADDED, D), vm(576, 2 * PADDED), vm(4, 2 * PADDED, CHUNK),
            vm(3, 4, 8, S1, CHUNK),
            vm(3, 4, 2, S1, CHUNK), vm(3, 4, 2, S1, CHUNK), vm(3, 4, S1, CHUNK), vm(3, 4, S1, CHUNK),
            vm(3, 4, 4, S2, CHUNK), vm(3, 4, 4, S2, CHUNK),
            vm(3, 4, 4, S3, CHUNK), vm(3, 4, 4, S3, CHUNK),
            sems(12), sems(128), sems(128),
        ],
        compiler_params=pltpu.CompilerParams(
            collective_id=0, has_side_effects=True, vmem_limit_bytes=50 * 1024 * 1024
        ),
        cost_estimate=pl.CostEstimate(
            flops=4 * 10**9, bytes_accessed=14 * 10**6, transcendentals=600000
        ),
    )(*pin(pltpu.HBM, frames, proj_weight, cot, shot_ids, band_width))
    projected, weight_grad = pl.pallas_call(
        hand_over,
        out_shape=(
            jax.ShapeDtypeStruct(projected.shape, BF16),
            jax.ShapeDtypeStruct(weight_grad.shape, F32),
        ),
        in_specs=[vmem_spec, vmem_spec],
        out_specs=(any_spec, any_spec),
        scratch_shapes=[pltpu.SemaphoreType.DMA((10,))],
    )(*pin(pltpu.VMEM, projected, weight_grad))
    return projected.reshape(1, TOKS, 2, H).transpose(2, 0, 1, 3), weight_grad


def solution(mesh):
    return jax.shard_map(
        per_device,
        mesh=mesh,
        in_specs=(
            P("dp", "tm", None, None),
            P("dp", None),
            P("dp", None),
            P(),
            P("dp", "tm", None, None),
        ),
        out_specs=(P("dp", "tm", None, None), P(("dp", "tm"), None)),
        check_vma=False,
    )
```

```python
import jax
import jax.numpy as jnp
from jax import lax
from jax.experimental import pallas as pl
from jax.experimental.pallas import tpu as pltpu
from jax.sharding import PartitionSpec as P

BLOCK = 64
POOL = 8
DECAY = 16.0
F32, BF16 = jnp.float32, jnp.bfloat16
MESH = pl.DeviceIdType.MESH

D, H, TOKS = 1152, 3584, 81
ROWS = 2 * TOKS
PADDED = 176
XL = 512
YL = D - XL
CHUNK = H // 4
ORDER = (("z", "y", "x"), ("y", "x", "z"), ("x", "z", "y"))
SLOTS = ((2, 0), (1, 1), (2, 1), (3, 0), (1, 0), (3, 1), (0, 0), (0, 1))
S1, S2, S3 = 24, 12, 3
C0 = 0.7978845608028654
C1 = 0.044715


def add16(a, b):
    return a + b


class Place:
    def __init__(self, local_sem, send_sem, recv_sem):
        dp, tm = lax.axis_index("dp"), lax.axis_index("tm")
        self.core = lax.rem(dp, 2)
        self.lo = lax.rem(tm, 2)
        self.z, self.y = lax.div(tm, 8), lax.rem(lax.div(tm, 2), 4)
        self.x = lax.div(dp, 2) * 2 + self.lo
        here = {"x": self.x, "y": self.y, "z": self.z}
        self.index = {a: [lax.rem(here[a] + d, 4) for d in range(4)] for a in "xyz"}
        self.hop = {a: [self.dev(**{a: self.index[a][d]}) for d in range(4)] for a in "xyz"}
        self.mate = self.dev(x=self.x + 1 - 2 * self.lo)
        self.twin = self.dev(core=1 - self.core)
        self.sems = local_sem, send_sem, recv_sem
        self.count = [0, 0]
        self.sends = []

    def dev(self, x=None, y=None, z=None, core=None):
        x, y, z, core = (
            mine if other is None else other
            for other, mine in ((x, self.x), (y, self.y), (z, self.z), (core, self.core))
        )
        return (lax.div(x, 2) * 2 + core, z * 8 + y * 2 + lax.rem(x, 2))

    def greet(self, friends):
        barrier = pltpu.get_barrier_semaphore()
        for friend in friends:
            pl.semaphore_signal(barrier, inc=1, device_id=friend, device_id_type=MESH)
        return lambda: pl.semaphore_wait(barrier, len(friends))

    def local(self, src, dst):
        i = self.count[0]
        self.count[0] += 1
        copy = pltpu.make_async_copy(src, dst, self.sems[0].at[i])
        copy.start()
        return copy

    def send(self, src, dst, to):
        i = self.count[1]
        self.count[1] += 1
        copy = pltpu.make_async_remote_copy(
            src_ref=src, dst_ref=dst, send_sem=self.sems[1].at[i], recv_sem=self.sems[2].at[i],
            device_id=to, device_id_type=MESH,
        )
        copy.start()
        self.sends.append(copy)
        return copy

    def settle(self):
        for copy in self.sends:
            copy.wait_send()
        self.sends.clear()


def iota(shape, axis):
    return lax.broadcasted_iota(jnp.int32, shape, axis)


def kernel(
    feat, wgt, cot, shots_in, band_in,
    out_proj, out_grad,
    wv, cv, sel, fv, cn, kron, part,
    xa, xfu, xfd, xnu, xnd, yfu, yfd, ynu, ynd, sb, yx,
    ids_v, band_s,
    pa, pre, pb, pt, gr, g,
    ru, rd, nu, nd, r1, in2, r2, r3,
    local_sem, send_sem, recv_sem,
):
    here = Place(local_sem, send_sem, recv_sem)
    core, x, y, z, lo = here.core, here.x, here.y, here.z, here.lo
    hop, local, send, settle, twin = here.hop, here.local, here.send, here.settle, here.twin
    la, lb = pl.ds(0, XL), pl.ds(XL, YL)
    ids_in = local(shots_in, ids_v)
    width_in = local(band_in, band_s)
    feat_b = local(feat.at[:, :, lb], fv.at[:, :, lb])
    feat_a = local(feat.at[:, :, la], fv.at[:, :, la])

    everybody = here.greet([hop[a][d] for a in "xyz" for d in (1, 2, 3)] + [twin])

    frame, other = iota((BLOCK, 128), 0), iota((BLOCK, 128), 1)
    distance = jnp.abs(frame - other)
    decay = jnp.exp(-distance.astype(F32) / DECAY)
    ids_in.wait()
    width_in.wait()
    ids = ids_v[...].astype(F32)
    ids = jnp.where(z < 2, ids[:, 0:128], ids[:, 128:256])
    ids = jnp.where(lax.rem(z, 2) == 0, ids, pltpu.roll(ids, 64, 1))
    target_of = iota((256, 128), 0)
    rel = lax.div(target_of, 32)
    target_of = lax.rem(y + lax.div(rel, 2), 4) * 2 + jnp.where(lax.rem(rel, 2) == 0, lo, 1 - lo)
    own_frame = jnp.where(iota((128, 256), 0) == (y * 2 + lo) * POOL + lax.rem(iota((128, 256), 1), 8), 1.0, 0.0)
    own_frame = own_frame.astype(BF16)
    out_row, in_row = iota((256, 256), 0), iota((256, 256), 1)
    same_token = lax.div(lax.rem(out_row, 32), 2) == lax.div(lax.rem(in_row, 128), 8)
    spread = jnp.zeros((256, 256), F32)
    for v in range(2):
        along = jnp.broadcast_to(ids[v : v + 1], (BLOCK, 128))
        down_ids = jnp.sum(jnp.where(frame == other, along, 0.0), axis=1, keepdims=True)
        allowed = (along == down_ids) & (distance <= band_s[v, z]) & (other < BLOCK)
        raw = jnp.where(allowed, decay, 0.0)
        mix = (raw / jnp.sum(raw, axis=1, keepdims=True)).astype(BF16).astype(F32)
        combined = (mix.reshape(8, POOL, 128).sum(axis=1) * 0.125).astype(BF16).astype(F32)
        rows = jnp.zeros((256, 128), F32)
        for p in range(8):
            rows = jnp.where(target_of == p, combined[p : p + 1], rows)
        full = jnp.dot(rows.astype(BF16), own_frame, preferred_element_type=F32)
        mine_too = same_token & (lax.rem(out_row, 2) == v) & (lax.div(in_row, 128) == v)
        spread = jnp.where(mine_too, full, spread)
    kron[...] = spread.astype(BF16)

    def partial_sums(lanes):
        for c in range(6):
            if c < 5:
                blocks = [fv[v, 128 * c : 128 * c + 128, lanes] for v in range(2)]
            else:
                empty = jnp.zeros((120, lanes.stop - lanes.start), BF16)
                blocks = [b for v in range(2) for b in (fv[v, 640:648, lanes], empty)]
            got = jnp.dot(kron[...], jnp.concatenate(blocks, axis=0), preferred_element_type=F32)
            size = 32 if c < 5 else 2
            for r in range(8):
                part[r // 2, r % 2, 32 * c : 32 * c + size, lanes] = got[32 * r : 32 * r + size].astype(BF16)

    l1, l2 = pl.ds(0, XL // 2), pl.ds(XL // 2, XL // 2)
    up, down, side = hop["y"][1], hop["y"][3], here.mate

    feat_b.wait()
    partial_sums(slice(XL, D))
    everybody()
    far_up = send(part.at[2, 0, :, lb], yfu, up)
    far_down = send(part.at[2, 1, :, lb], yfd, down)
    near_up = {1: send(part.at[1, 1, :, lb], ynu.at[1], up)}
    near_down = {0: send(part.at[3, 0, :, lb], ynd.at[0], down)}
    feat_a.wait()
    partial_sums(slice(0, XL))
    x_first = {dy: send(part.at[dy, 1, :, la], xa.at[dy], side) for dy in (2, 1, 3, 0)}

    columns = [pl.ds(j * CHUNK, CHUNK) for j in range(4)]
    cot_in = [local(cot.at[:, :, columns[j]], cn.at[j]) for j in range(4)]
    wgt_in = [local(wgt.at[:, columns[j]], wv.at[j]) for j in range(4)]

    row, lane = iota((576, 128), 0), iota((576, 128), 1)
    which, slot = lax.div(row, 192), lax.div(lax.rem(row, 192), S1)
    half, first = jnp.zeros_like(row), jnp.zeros_like(row)
    for p, (d, h) in enumerate(SLOTS):
        first = jnp.where(slot == p, d, first)
        half = jnp.where(slot == p, h, half)
    second = half * 2 + lax.div(lax.rem(row, S1), S2)
    third = lax.div(lax.rem(row, S2), S3)
    at = {}
    for axis, mine in (("x", x), ("y", y), ("z", z)):
        far = jnp.zeros_like(row)
        for s in range(3):
            far = jnp.where(which == s, (first, second, third)[ORDER[s].index(axis)], far)
        at[axis] = lax.rem(far + mine, 4)
    owner = (lax.div(at["x"], 2) * 2 + core) * 32 + at["z"] * 8 + at["y"] * 2 + lax.rem(at["x"], 2)
    wanted = owner * 9 + which * S3 + lax.rem(row, S3)
    for k in range(D // 128):
        sel[:, 128 * k : 128 * k + 128] = jnp.where(wanted == lane + 128 * k, 1.0, 0.0).astype(BF16)

    def take(dy):
        x_first[dy].wait_recv()
        xa[dy] = add16(xa[dy], part[dy, 0, :, 0:XL])

    far_up.wait_recv()
    yfu[...] = add16(yfu[...], part[1, 0, :, XL:D])
    near_up[0] = send(yfu, ynu.at[0], up)
    far_down.wait_recv()
    yfd[...] = add16(yfd[...], part[3, 1, :, XL:D])
    near_down[1] = send(yfd, ynd.at[1], down)
    take(2)
    far_up2 = send(xa.at[2, :, l1], xfu, up)
    far_down2 = send(xa.at[2, :, l2], xfd, down)
    take(1)
    near_up2 = [send(xa.at[1, :, l2], xnu.at[:, l2], up)]
    take(3)
    near_down2 = [send(xa.at[3, :, l1], xnd.at[:, l1], down)]

    for j in range(4):
        cot_in[j].wait()

        @pl.loop(0, 10)
        def _(i):
            cv[j, pl.ds(pl.multiple_of(i * 16, 16), 16), :] = cn[j, pl.ds(i * 8, 8)].reshape(16, CHUNK)

        tail = jnp.concatenate([cn[j, 80].astype(F32), jnp.zeros((14, CHUNK), F32)], axis=0)
        cv[j, 160:176, :] = tail.astype(BF16)

    far_up2.wait_recv()
    xfu[...] = add16(xfu[...], xa[1, :, 0 : XL // 2])
    near_up2.append(send(xfu, xnu.at[:, l1], up))
    near_up[1].wait_recv()
    near_down[1].wait_recv()
    sb[...] = (
        part[0, 1, :, XL:D].astype(F32) + ynu[1].astype(F32) + ynd[1].astype(F32)
    ).astype(BF16)
    last_x = send(sb, yx, side)
    far_down2.wait_recv()
    xfd[...] = add16(xfd[...], xa[3, :, XL // 2 : XL])
    near_down2.append(send(xfd, xnd.at[:, l2], down))

    def keep(value, lanes):
        value = value.astype(BF16)
        pb[0:160, lanes] = value[0:160]
        tail = jnp.concatenate(
            [value[160:162].astype(F32), jnp.zeros((14, value.shape[1]), F32)], axis=0
        )
        pb[160:176, lanes] = tail.astype(BF16)

    take(0)
    for copy in near_up2 + near_down2:
        copy.wait_recv()
    keep(xa[0].astype(F32) + xnu[...].astype(F32) + xnd[...].astype(F32), slice(0, XL))
    near_up[0].wait_recv()
    near_down[0].wait_recv()
    last_x.wait_recv()
    keep(
        part[0, 0, :, XL:D].astype(F32) + ynu[0].astype(F32) + ynd[0].astype(F32) + yx[...].astype(F32),
        slice(XL, D),
    )
    pooled_twin = send(pb.at[pl.ds(0, PADDED)], pb.at[pl.ds(PADDED, PADDED)], twin)

    grad_twin = []

    def gelu_rows(values, cotangent):
        square = values * values
        t = jnp.tanh(values * (C0 + (C0 * C1) * square))
        plus = 0.5 * (1.0 + t)
        slope = plus + (0.5 * values) * (1.0 - t * t) * (C0 + (3.0 * C0 * C1) * square)
        return (values * plus).astype(BF16), (cotangent * slope).astype(BF16)

    def product(j):
        pre[j % 2] = jnp.dot(pb[0:PADDED, :], wv[j], preferred_element_type=F32)

    def forward(j):
        for i in range(11):
            rows = slice(16 * i, 16 * i + 16)
            act, grad = gelu_rows(pre[j % 2, rows, :], cv[j, rows, :].astype(F32))
            pa[j, rows, :] = act
            gr[j, rows, :] = grad

    def share(j):
        grad_twin.append(send(gr.at[j, pl.ds(0, PADDED)], gr.at[j, pl.ds(PADDED, PADDED)], twin))

    def give(j):
        for i in range(10):
            out_proj[8 * i : 8 * i + 8, :, CHUNK * j : CHUNK * j + CHUNK] = (
                pa[j, 16 * i : 16 * i + 16, :].reshape(8, 2, CHUNK)
            )
        out_proj[80, :, CHUNK * j : CHUNK * j + CHUNK] = pa[j, 160:162, :]

    msg = {}

    def wait(*names):
        for name in names:
            msg[name].wait_recv()

    def add3(a, b, c):
        return a.astype(F32) + b.astype(F32) + c.astype(F32)

    def backward(j):
        grad_twin[j].wait_recv()
        got = jnp.dot(pt[...], gr[j], preferred_element_type=F32)
        for s in range(3):
            for p in range(8):
                base = s * 192 + p * S1
                g[s, j, p] = got[base : base + S1].astype(BF16)
        for s in range(3):
            to = hop[ORDER[s][0]]
            msg["ru", s, j] = send(g.at[s, j, pl.ds(0, 2)], ru.at[s, j], to[1])
            msg["rd", s, j] = send(g.at[s, j, pl.ds(2, 2)], rd.at[s, j], to[3])

    def relay(j):
        for s in range(3):
            to = hop[ORDER[s][0]]
            wait(("ru", s, j))
            ru[s, j, 0] = add16(ru[s, j, 0], g[s, j, 4])
            msg["nu", s, j] = send(ru.at[s, j, 0], nu.at[s, j], to[1])
            wait(("rd", s, j))
            rd[s, j, 0] = add16(rd[s, j, 0], g[s, j, 5])
            msg["nd", s, j] = send(rd.at[s, j, 0], nd.at[s, j], to[3])

    def finish(j):
        for s in range(3):
            wait(("nu", s, j), ("nd", s, j))
            for h, value in enumerate(
                (add3(g[s, j, 6], nu[s, j], rd[s, j, 1]), add3(g[s, j, 7], ru[s, j, 1], nd[s, j]))
            ):
                for b in range(2):
                    r1[s, 2 * h + b, j] = value[S2 * b : S2 * b + S2].astype(BF16)

    def second_stage(q):
        steps = pl.ds(2 * q, 2)
        for d in (2, 1, 3):
            for s in range(3):
                msg["second", s, q, d] = send(r1.at[s, d, steps], in2.at[s, d, steps], hop[ORDER[s][1]][d])

    def second_finish(q):
        for s in range(3):
            wait(*(("second", s, q, d) for d in (1, 2, 3)))
            for j in (2 * q, 2 * q + 1):
                value = add3(r1[s, 0, j], in2[s, 1, j], in2[s, 3, j]) + in2[s, 2, j].astype(F32)
                for c in range(4):
                    r2[s, c, j] = value[S3 * c : S3 * c + S3].astype(BF16)

    def third_stage(q):
        steps = pl.ds(2 * q, 2)
        for s in range(3):
            to = hop[ORDER[s][2]]
            for d in (2, 1, 3):
                msg["last", s, q, d] = send(r2.at[s, d, steps], r3.at[s, d, steps], to[d])

    def owned(q):
        for s in range(3):
            wait(*(("last", s, q, d) for d in (1, 2, 3)))
            for j in (2 * q, 2 * q + 1):
                total = r2[s, 0, j].astype(F32)
                for d in (1, 2, 3):
                    total = total + r3[s, d, j].astype(F32)
                out_grad[S3 * s : S3 * s + S3, j * CHUNK : j * CHUNK + CHUNK] = total

    settle()
    for copy in wgt_in:
        copy.wait()

    def step(j):
        product(j)
        forward(j)
        share(j)

    step(0)
    step(1)
    pooled_twin.wait_recv()
    pt[...] = lax.dot_general(
        sel[...], pb[...], (((1,), (1,)), ((), ())), preferred_element_type=F32
    ).astype(BF16)
    backward(0)
    step(2)
    backward(1)
    step(3)
    relay(0)
    backward(2)
    relay(1)
    backward(3)
    relay(2)
    finish(0)
    finish(1)
    second_stage(0)
    relay(3)
    finish(2)
    give(0)
    finish(3)
    second_stage(1)
    second_finish(0)
    third_stage(0)
    give(1)
    settle()
    second_finish(1)
    third_stage(1)
    give(2)
    owned(0)
    give(3)
    owned(1)
    settle()


def hand_over(projected, weight_grad, out_projected, out_grad, sem):
    copies = [pltpu.make_async_copy(weight_grad, out_grad, sem.at[9])]
    for i in range(9):
        rows = pl.ds(9 * i, 9)
        copies.append(pltpu.make_async_copy(projected.at[rows], out_projected.at[rows], sem.at[i]))
    for copy in copies:
        copy.start()
    for copy in copies:
        copy.wait()


def per_device(features, shot_ids, band_width, proj_weight, cotangent):
    frames = jnp.swapaxes(features, 1, 2).reshape(2, TOKS * POOL, D)
    cot = cotangent.transpose(1, 2, 0, 3).reshape(TOKS, 2, H)
    vm = lambda *shape: pltpu.VMEM(shape, BF16)
    sems = lambda n: pltpu.SemaphoreType.DMA((n,))
    any_spec = pl.BlockSpec(memory_space=pl.ANY)
    vmem_spec = pl.BlockSpec(memory_space=pltpu.VMEM)
    pin = lambda space, *arrays: [pltpu.with_memory_space_constraint(a, space) for a in arrays]
    projected, weight_grad = pl.pallas_call(
        kernel,
        out_shape=(pltpu.VMEM(cot.shape, BF16), pltpu.VMEM((9, H), F32)),
        in_specs=[any_spec] * 5,
        out_specs=(vmem_spec, vmem_spec),
        scratch_shapes=[
            vm(4, D, CHUNK), vm(4, PADDED, CHUNK), vm(576, D),
            vm(2, TOKS * POOL, D), vm(4, TOKS, 2, CHUNK), vm(256, 256), vm(4, 2, ROWS, D),
            vm(4, ROWS, XL), vm(ROWS, XL // 2), vm(ROWS, XL // 2), vm(ROWS, XL), vm(ROWS, XL),
            vm(ROWS, YL), vm(ROWS, YL), vm(2, ROWS, YL), vm(2, ROWS, YL), vm(ROWS, YL), vm(ROWS, YL),
            pltpu.VMEM(shot_ids.shape, jnp.int32), pltpu.SMEM(band_width.shape, jnp.int32),
            vm(4, PADDED, CHUNK), pltpu.VMEM((2, PADDED, CHUNK), F32),
            vm(2 * PADDED, D), vm(576, 2 * PADDED), vm(4, 2 * PADDED, CHUNK),
            vm(3, 4, 8, S1, CHUNK),
            vm(3, 4, 2, S1, CHUNK), vm(3, 4, 2, S1, CHUNK), vm(3, 4, S1, CHUNK), vm(3, 4, S1, CHUNK),
            vm(3, 4, 4, S2, CHUNK), vm(3, 4, 4, S2, CHUNK),
            vm(3, 4, 4, S3, CHUNK), vm(3, 4, 4, S3, CHUNK),
            sems(12), sems(128), sems(128),
        ],
        compiler_params=pltpu.CompilerParams(
            collective_id=0, has_side_effects=True, vmem_limit_bytes=50 * 1024 * 1024
        ),
        cost_estimate=pl.CostEstimate(
            flops=4 * 10**9, bytes_accessed=14 * 10**6, transcendentals=600000
        ),
    )(*pin(pltpu.HBM, frames, proj_weight, cot, shot_ids, band_width))
    projected, weight_grad = pl.pallas_call(
        hand_over,
        out_shape=(
            jax.ShapeDtypeStruct(projected.shape, BF16),
            jax.ShapeDtypeStruct(weight_grad.shape, F32),
        ),
        in_specs=[vmem_spec, vmem_spec],
        out_specs=(any_spec, any_spec),
        scratch_shapes=[pltpu.SemaphoreType.DMA((10,))],
    )(*pin(pltpu.VMEM, projected, weight_grad))
    return projected.reshape(1, TOKS, 2, H).transpose(2, 0, 1, 3), weight_grad


def solution(mesh):
    return jax.shard_map(
        per_device,
        mesh=mesh,
        in_specs=(
            P("dp", "tm", None, None),
            P("dp", None),
            P("dp", None),
            P(),
            P("dp", "tm", None, None),
        ),
        out_specs=(P("dp", "tm", None, None), P(("dp", "tm"), None)),
        check_vma=False,
    )
```
